256 devices in a mesh: frame: 16 (over z, x_lo), row: 16 (over y, x_hi, core).
Axes of the slice: x: 4 (x_hi: 2, x_lo: 2; x = x_hi * 2 + x_lo), y: 4, z: 8, core: 2. Of those that a mesh axis runs over, the one named last changes fastest.
Arguments:
- latents: bfloat16 [16, 64, 128, 320], P('frame', 'row'), may hold values from -6 to 6
- conv_weight: bfloat16 [3, 3, 320, 320], replicated, may hold values from -0.109375 to 0.109375
- query_weight: bfloat16 [320, 320], replicated, may hold values from -0.3125 to 0.3125
- key_weight: bfloat16 [320, 320], replicated, may hold values from -0.3125 to 0.3125
- value_weight: bfloat16 [320, 320], replicated, may hold values from -0.3125 to 0.3125
- out_weight: bfloat16 [320, 320], replicated, may hold values from -0.3125 to 0.3125
- norm_gain: float32 [320], replicated, may hold values from 0.1 to 1.9
- out_grad: bfloat16 [16, 64, 128, 320], P('frame', 'row'), may hold values from -6 to 6
Outputs:
- block_out: bfloat16 [16, 64, 128, 320], P('frame', 'row')
- latents_grad: bfloat16 [16, 64, 128, 320], P('frame', 'row')
- conv_grad: float32 [3, 3, 320, 320], replicated
- query_grad: float32 [320, 320], replicated
- key_grad: float32 [320, 320], replicated
- value_grad: float32 [320, 320], replicated
- out_weight_grad: float32 [320, 320], replicated
- gain_grad: float32 [320], replicated
The draws below stay inside these ranges and needn't reach their ends.
All inputs are finite; a program needn't handle non-finite values.
Results may differ from the reference program's by a relative error of at most 0.02.
Values may be sent and summed in bfloat16 or wider, within the bound.
A program may use at most 64 MiB of HBM per device.

```python
import jax
import jax.numpy as jnp
from jax import lax

C = 320
HEADS = 5
W = 128
F = 16
H = 64


def levels(key, shape, shards, low, largest):
    def one(axis_at, parts):
        heights = jax.random.uniform(jax.random.fold_in(jax.random.fold_in(key, 6), axis_at), (parts,), jnp.float32, low / len(shards), largest / len(shards))
        return jnp.repeat(jnp.exp(heights), shape[axis_at] // parts).reshape((-1,) + (1,) * (len(shape) - axis_at - 1))

    factor_of = one(*shards[0])
    for cut in shards[1:]:
        factor_of = factor_of * one(*cut)
    return factor_of


def normal_values(rng, dims, scale, most, pieces=(), held_as=jnp.bfloat16):
    array = jax.random.normal(rng, dims, jnp.float32) * scale
    if len(pieces) > 0:
        array = levels(rng, dims, pieces, -0.22, 0.18) * array
    return jnp.clip(array, min=-most, max=most).astype(held_as)


def setup_inputs(seed: int = 0) -> dict:
    key_of = jax.random.split(jax.random.key(seed), 9)
    return {
        "latents": normal_values(key_of[0], (F, H, W, C), 1.0, 6.0, ((0, 16), (1, 16))),
        "conv_weight": normal_values(key_of[1], (3, 3, C, C), (9 * C) ** -0.5, 0.109375),
        "query_weight": normal_values(key_of[2], (C, C), C ** -0.5, 0.3125),
        "key_weight": normal_values(key_of[3], (C, C), C ** -0.5, 0.3125),
        "value_weight": normal_values(key_of[4], (C, C), C ** -0.5, 0.3125),
        "out_weight": normal_values(key_of[5], (C, C), C ** -0.5, 0.3125),
        "norm_gain": jnp.clip(1.0 + 0.18 * jax.random.normal(key_of[6], (C,), jnp.float32), 0.1, 1.9),
        "out_grad": normal_values(key_of[7], (F, H, W, C), 1.0, 6.0, ((0, 16), (1, 16))),
    }


EPS = 1e-06

def conv_apply(padded, weight, rows, width):
    total = None
    for row_off in range(3):
        for col_off in range(3):
            piece = padded[:, row_off:row_off + rows, col_off:col_off + width, :]
            term = jnp.dot(piece, weight[row_off, col_off], preferred_element_type=jnp.float32)
            total = term if total is None else total + term
    return total

def outer_sum(left, right):
    left_flat = left.reshape(-1, left.shape[-1])
    right_flat = right.reshape(-1, right.shape[-1])
    return lax.dot_general(left_flat, right_flat, (((0,), (0,)), ((), ())), preferred_element_type=jnp.float32)

def back_dot(field, weight):
    return lax.dot_general(field, weight, (((field.ndim - 1,), (1,)), ((), ())), preferred_element_type=jnp.float32)

def conv_weight_grad(padded, grad, rows, width):
    taps = []
    for row_off in range(3):
        for col_off in range(3):
            piece = padded[:, row_off:row_off + rows, col_off:col_off + width, :]
            taps.append(outer_sum(piece, grad))
    chan = grad.shape[-1]
    return jnp.stack(taps).reshape(3, 3, chan, chan)

def conv_input_grad(grad_pad, weight, rows, width):
    total = None
    for row_off in range(3):
        for col_off in range(3):
            piece = grad_pad[:, 2 - row_off:2 - row_off + rows, 2 - col_off:2 - col_off + width, :]
            term = back_dot(piece, weight[row_off, col_off])
            total = term if total is None else total + term
    return total

def split_heads(field):
    frames, rows, width, chan = field.shape
    return field.reshape(frames, rows, width, HEADS, chan // HEADS).astype(jnp.float32)

def attend(queries, key_rows, value_rows):
    frames, rows, width, chan = queries.shape
    factor = (chan // HEADS) ** (-0.5)
    scores = jnp.einsum('frwhd,grwhd->rwhfg', split_heads(queries), split_heads(key_rows)) * factor
    expo = jnp.exp(scores)
    probs = expo / lax.optimization_barrier(jnp.sum(expo, axis=-1, keepdims=True))
    probs_b = probs.astype(jnp.bfloat16)
    mixed = jnp.einsum('rwhfg,grwhd->frwhd', probs_b.astype(jnp.float32), split_heads(value_rows))
    return (probs, probs_b, mixed.reshape(frames, rows, width, chan).astype(jnp.bfloat16))

def attend_back(probs, probs_b, queries, key_rows, value_rows, mixed_grad):
    frames, rows, width, chan = queries.shape
    factor = (chan // HEADS) ** (-0.5)
    grad_heads = split_heads(mixed_grad)
    prob_grad = jnp.einsum('frwhd,grwhd->rwhfg', grad_heads, split_heads(value_rows))
    score_grad = probs * (prob_grad - lax.optimization_barrier(jnp.sum(probs * prob_grad, axis=-1, keepdims=True))) * factor
    score_b = score_grad.astype(jnp.bfloat16).astype(jnp.float32)
    query_part = jnp.einsum('rwhfg,grwhd->frwhd', score_b, split_heads(key_rows))
    key_part = jnp.einsum('rwhfg,frwhd->grwhd', score_b, split_heads(queries))
    value_part = jnp.einsum('rwhfg,frwhd->grwhd', probs_b.astype(jnp.float32), grad_heads)
    shape = (frames, rows, width, chan)
    return (query_part.reshape(shape).astype(jnp.bfloat16), key_part.reshape(shape).astype(jnp.bfloat16), value_part.reshape(shape).astype(jnp.bfloat16))

def reference(latents, conv_weight, query_weight, key_weight, value_weight, out_weight, norm_gain, out_grad):
    frames, rows, width, chan = latents.shape
    latent_f = latents.astype(jnp.float32)
    sigma = jax.nn.sigmoid(latent_f)
    act = (latent_f * sigma).astype(jnp.bfloat16)
    padded = jnp.pad(act, ((0, 0), (1, 1), (1, 1), (0, 0)))
    resid = (latent_f + conv_apply(padded, conv_weight, rows, width)).astype(jnp.bfloat16)
    resid_f = resid.astype(jnp.float32)
    inv_rms = lax.rsqrt(lax.optimization_barrier(jnp.mean(resid_f * resid_f, axis=-1, keepdims=True)) + EPS)
    normed = (resid_f * inv_rms * norm_gain).astype(jnp.bfloat16)
    queries = jnp.dot(normed, query_weight, preferred_element_type=jnp.float32).astype(jnp.bfloat16)
    key_rows = jnp.dot(normed, key_weight, preferred_element_type=jnp.float32).astype(jnp.bfloat16)
    value_rows = jnp.dot(normed, value_weight, preferred_element_type=jnp.float32).astype(jnp.bfloat16)
    probs, probs_b, mixed = attend(queries, key_rows, value_rows)
    block_out = (resid_f + jnp.dot(mixed, out_weight, preferred_element_type=jnp.float32)).astype(jnp.bfloat16)
    factor = (frames * rows * width) ** (-0.5)
    grad_out_w = outer_sum(mixed, out_grad)
    mixed_grad = back_dot(out_grad, out_weight).astype(jnp.bfloat16)
    query_part, key_part, value_part = attend_back(probs, probs_b, queries, key_rows, value_rows, mixed_grad)
    grad_query = outer_sum(normed, query_part)
    grad_key = outer_sum(normed, key_part)
    grad_value = outer_sum(normed, value_part)
    normed_grad = (back_dot(query_part, query_weight) + back_dot(key_part, key_weight) + back_dot(value_part, value_weight)).astype(jnp.bfloat16)
    normed_gf = normed_grad.astype(jnp.float32)
    grad_gain = lax.optimization_barrier(jnp.sum((normed_gf * resid_f * inv_rms).reshape(-1, chan), axis=0))
    tangent = normed_gf * norm_gain
    resid_part = inv_rms * tangent - resid_f * inv_rms ** 3 * lax.optimization_barrier(jnp.mean(tangent * resid_f, axis=-1, keepdims=True))
    resid_grad = (out_grad.astype(jnp.float32) + resid_part).astype(jnp.bfloat16)
    grad_conv = conv_weight_grad(padded, resid_grad, rows, width)
    grad_pad = jnp.pad(resid_grad, ((0, 0), (1, 1), (1, 1), (0, 0)))
    act_grad = conv_input_grad(grad_pad, conv_weight, rows, width)
    latents_grad = (resid_grad.astype(jnp.float32) + act_grad * sigma * (1.0 + latent_f * (1.0 - sigma))).astype(jnp.bfloat16)
    return (block_out, latents_grad, grad_conv * factor, grad_query * factor, grad_key * factor, grad_value * factor, grad_out_w * factor, grad_gain * factor)
```

```python
import functools

import jax
import jax.numpy as jnp
from jax import lax
from jax.experimental import pallas as pl
from jax.experimental.pallas import tpu as pltpu
from jax.sharding import PartitionSpec as P

HEADS = 5
MESH = pl.DeviceIdType.MESH
ORDERS = ("xyz", "yxz", "zxy")
TILE = (16, 128)


EPS = 1e-06


def padded_2(cells, sides, width):
    for axis, dim in sides:
        count = lax.axis_size(axis)
        ends = count - 1
        head = lax.slice_in_dim(cells, 0, width, axis=dim)
        tail = lax.slice_in_dim(cells, cells.shape[dim] - width, cells.shape[dim], axis=dim)
        cells = jnp.concatenate(
            [
                lax.ppermute(tail, axis, [(i, (i + 1) % count) for i in range(ends)]),
                cells,
                lax.ppermute(head, axis, [((i + 1) % count, i) for i in range(ends)]),
            ],
            axis=dim,
        )
    return cells


def pad_rows(field):
    rimmed = padded_2(field, (("row", 1),), 1)
    return jnp.pad(rimmed, ((0, 0), (0, 0), (1, 1), (0, 0)))


def conv_apply(padded, weight, rows, width):
    total = None
    for row_off in range(3):
        for col_off in range(3):
            piece = padded[:, row_off : row_off + rows, col_off : col_off + width, :]
            term = jnp.dot(piece, weight[row_off, col_off], preferred_element_type=jnp.float32)
            total = term if total is None else total + term
    return total


def outer_sum(left, right):
    left_flat = left.reshape(-1, left.shape[-1])
    right_flat = right.reshape(-1, right.shape[-1])
    return lax.dot_general(
        left_flat, right_flat, (((0,), (0,)), ((), ())), preferred_element_type=jnp.float32
    )


def back_dot(field, weight):
    return lax.dot_general(
        field, weight, (((field.ndim - 1,), (1,)), ((), ())), preferred_element_type=jnp.float32
    )


def conv_weight_grad(padded, grad, rows, width):
    taps = []
    for row_off in range(3):
        for col_off in range(3):
            piece = padded[:, row_off : row_off + rows, col_off : col_off + width, :]
            taps.append(outer_sum(piece, grad))
    chan = grad.shape[-1]
    return jnp.stack(taps).reshape(3, 3, chan, chan)


def conv_input_grad(grad_pad, weight, rows, width):
    total = None
    for row_off in range(3):
        for col_off in range(3):
            piece = grad_pad[
                :, 2 - row_off : 2 - row_off + rows, 2 - col_off : 2 - col_off + width, :
            ]
            term = back_dot(piece, weight[row_off, col_off])
            total = term if total is None else total + term
    return total


def split_heads(field):
    frames, rows, width, chan = field.shape
    return field.reshape(frames, rows, width, HEADS, chan // HEADS)


def attend(queries, key_rows, value_rows):
    frames, rows, width, chan = queries.shape
    factor = (chan // HEADS) ** (-0.5)
    scores = (
        jnp.einsum(
            "frwhd,grwhd->rwhfg",
            split_heads(queries),
            split_heads(key_rows),
            preferred_element_type=jnp.float32,
        )
        * factor
    )
    expo = jnp.exp(scores)
    probs = expo / jnp.sum(expo, axis=-1, keepdims=True)
    probs_b = probs.astype(jnp.bfloat16)
    mixed = jnp.einsum(
        "rwhfg,grwhd->frwhd", probs_b, split_heads(value_rows), preferred_element_type=jnp.float32
    )
    return (probs, probs_b, mixed.reshape(frames, rows, width, chan).astype(jnp.bfloat16))


def attend_back(probs, probs_b, queries, key_rows, value_rows, mixed_grad):
    frames, rows, width, chan = queries.shape
    factor = (chan // HEADS) ** (-0.5)
    grad_heads = split_heads(mixed_grad)
    prob_grad = jnp.einsum(
        "frwhd,grwhd->rwhfg",
        grad_heads,
        split_heads(value_rows),
        preferred_element_type=jnp.float32,
    )
    score_grad = probs * (prob_grad - jnp.sum(probs * prob_grad, axis=-1, keepdims=True)) * factor
    score_b = score_grad.astype(jnp.bfloat16)
    query_part = jnp.einsum(
        "rwhfg,grwhd->frwhd", score_b, split_heads(key_rows), preferred_element_type=jnp.float32
    )
    key_part = jnp.einsum(
        "rwhfg,frwhd->grwhd", score_b, split_heads(queries), preferred_element_type=jnp.float32
    )
    value_part = jnp.einsum(
        "rwhfg,frwhd->grwhd", probs_b, grad_heads, preferred_element_type=jnp.float32
    )
    shape = (frames, rows, width, chan)
    return (
        query_part.reshape(shape).astype(jnp.bfloat16),
        key_part.reshape(shape).astype(jnp.bfloat16),
        value_part.reshape(shape).astype(jnp.bfloat16),
    )


def chip_sizes():
    return {"c": 2, "x": 4, "y": lax.axis_size("row") // 4, "z": lax.axis_size("frame") // 2}


def my_place():
    frame, row = lax.axis_index("frame"), lax.axis_index("row")
    return {
        "z": frame // 2,
        "x": lax.rem(row // 2, 2) * 2 + lax.rem(frame, 2),
        "y": row // 4,
        "c": lax.rem(row, 2),
    }


def device_of(place):
    return (
        place["z"] * 2 + lax.rem(place["x"], 2),
        (place["y"] * 2 + place["x"] // 2) * 2 + place["c"],
    )


def along(place, axis, step, sizes):
    moved = dict(place)
    moved[axis] = lax.rem(place[axis] + step, sizes[axis])
    return device_of(moved)


def axis_partners(place, sizes):
    return [
        along(place, axis, step, sizes) for axis in "cxyz" for step in range(1, sizes[axis])
    ]


def greet(partners):
    barrier = pltpu.get_barrier_semaphore()
    for partner in partners:
        pl.semaphore_signal(barrier, inc=1, device_id=partner, device_id_type=MESH)
    pl.semaphore_wait(barrier, len(partners))


def send(source, target, sems, slot, device):
    copy = pltpu.make_async_remote_copy(
        src_ref=source,
        dst_ref=target,
        send_sem=sems[0].at[slot],
        recv_sem=sems[1].at[slot],
        device_id=device,
        device_id_type=MESH,
    )
    copy.start()
    return copy


def add_up(target, own, received):
    def body(at, carry):
        total = own[at].astype(jnp.float32)
        for part in received:
            total = total + part[at].astype(jnp.float32)
        target[at] = total.astype(target.dtype)
        return carry

    lax.fori_loop(0, target.shape[0], body, 0)


class Summer:
    def __init__(self, order, place, sizes, term, total, scratch, sems):
        self.order, self.place, self.sizes = order, place, sizes
        self.term, self.total, self.sems = term, total, sems
        self.core_in, self.held, self.inbox = scratch[0], scratch[1:4], scratch[4:7]
        self.slot = 0
        self.sent = []
        self.wait = []

    def push(self, source, target, axis, step):
        device = along(self.place, axis, step, self.sizes)
        copy = send(source, target, self.sems, self.slot, device)
        self.slot += 1
        self.sent.append(copy)
        self.wait.append(copy)

    def arrive(self):
        for copy in self.wait:
            copy.wait_recv()
        self.wait = []

    def core_start(self):
        self.push(self.term.at[1 - self.place["c"]], self.core_in, "c", 1)

    def core_end(self):
        self.arrive()
        add_up(self.held[0], self.term.at[self.place["c"]], [self.core_in])

    def scatter_start(self, level):
        axis = self.order[level]
        for step in range(1, self.sizes[axis]):
            peer = lax.rem(self.place[axis] + step, self.sizes[axis])
            self.push(self.held[level].at[peer], self.inbox[level].at[step - 1], axis, step)

    def scatter_end(self, level):
        self.arrive()
        axis = self.order[level]
        received = [self.inbox[level].at[step] for step in range(self.sizes[axis] - 1)]
        own = self.held[level].at[self.place[axis]]
        if level < 2:
            add_up(self.held[level + 1], own, received)
        else:
            total = own[...].astype(jnp.float32)
            for part in received:
                total = total + part[...].astype(jnp.float32)
            self.mine(3)[...] = total.astype(self.total.dtype)

    def mine(self, levels):
        view = self.total.at[self.place["c"]]
        for level in range(levels):
            view = view.at[self.place[self.order[level]]]
        return view

    def gather_start(self, level):
        axis = self.order[level]
        for step in range(1, self.sizes[axis]):
            self.push(self.mine(level + 1), self.mine(level + 1), axis, step)

    def core_back(self):
        self.push(self.mine(0), self.mine(0), "c", 1)

    def finish(self):
        for copy in self.sent:
            copy.wait_send()


def summer_scratch(order, sizes, rows):
    n1, n2, n3 = (sizes[axis] for axis in order)
    shapes = [
        (n1, n2, n3, rows, 128),
        (n1, n2, n3, rows, 128),
        (n2, n3, rows, 128),
        (n3, rows, 128),
        (n1 - 1, n2, n3, rows, 128),
        (n2 - 1, n3, rows, 128),
        (n3 - 1, rows, 128),
    ]
    copies = 2 * (1 + n1 + n2 + n3 - 3)
    return [pltpu.VMEM(shape, jnp.bfloat16) for shape in shapes] + [
        pltpu.SemaphoreType.DMA((copies,)),
        pltpu.SemaphoreType.DMA((copies,)),
    ]


def sum_kernel(sizes, *refs):
    count = len(ORDERS)
    terms, totals, rest = refs[:count], refs[count : 2 * count], refs[2 * count :]
    place = my_place()
    greet(axis_partners(place, sizes))
    parts = []
    for at, order in enumerate(ORDERS):
        scratch = rest[9 * at : 9 * at + 9]
        parts.append(
            Summer(order, place, sizes, terms[at], totals[at], scratch[:7], scratch[7:])
        )
    for part in parts:
        part.core_start()
    for part in parts:
        part.core_end()
        part.scatter_start(0)
    for level in range(3):
        for part in parts:
            part.scatter_end(level)
            if level < 2:
                part.scatter_start(level + 1)
            else:
                part.gather_start(2)
    for level in (1, 0):
        for part in parts:
            part.arrive()
            part.gather_start(level)
    for part in parts:
        part.arrive()
        part.core_back()
    for part in parts:
        part.arrive()
        part.finish()


def sum_everywhere(terms):
    sizes = chip_sizes()
    shapes = [(2,) + tuple(sizes[axis] for axis in order) + TILE for order in ORDERS]
    each = 2 * sizes["x"] * sizes["y"] * sizes["z"] * TILE[0] * TILE[1]
    flat = jnp.concatenate([term.astype(jnp.bfloat16).reshape(-1) for term in terms])
    flat = jnp.pad(flat, (0, each * len(ORDERS) - flat.size))
    cut = [flat[at * each : (at + 1) * each].reshape(shape) for at, shape in enumerate(shapes)]
    scratch = []
    for order in ORDERS:
        scratch += summer_scratch(order, sizes, TILE[0])
    totals = pl.pallas_call(
        functools.partial(sum_kernel, sizes),
        out_shape=[jax.ShapeDtypeStruct(shape, jnp.bfloat16) for shape in shapes],
        in_specs=[pl.BlockSpec(memory_space=pltpu.VMEM)] * len(ORDERS),
        out_specs=[pl.BlockSpec(memory_space=pltpu.VMEM)] * len(ORDERS),
        scratch_shapes=scratch,
        compiler_params=pltpu.CompilerParams(
            collective_id=0, has_side_effects=True, vmem_limit_bytes=48 << 20
        ),
    )(*cut)
    back = jnp.concatenate([total.reshape(-1) for total in totals])
    out, start = [], 0
    for term in terms:
        out.append(back[start : start + term.size].reshape(term.shape).astype(jnp.float32))
        start += term.size
    return out


def project(normed, weight):
    return jnp.dot(normed, weight, preferred_element_type=jnp.float32).astype(jnp.bfloat16)


def on_device(
    latents, conv_weight, query_weight, key_weight, value_weight, out_weight, norm_gain, out_grad
):
    frames, rows, width, chan = latents.shape
    cells_all = frames * rows * width * lax.axis_size("frame") * lax.axis_size("row")
    latent_f = latents.astype(jnp.float32)
    sigma = jax.nn.sigmoid(latent_f)
    act = (latent_f * sigma).astype(jnp.bfloat16)
    padded = pad_rows(act)
    resid = (latent_f + conv_apply(padded, conv_weight, rows, width)).astype(jnp.bfloat16)
    resid_f = resid.astype(jnp.float32)
    inv_rms = lax.rsqrt(jnp.mean(resid_f * resid_f, axis=-1, keepdims=True) + EPS)
    normed = (resid_f * inv_rms * norm_gain).astype(jnp.bfloat16)
    side = lax.axis_size("frame")

    def exchange(field):
        cut = field.reshape(side, -1, chan)
        return lax.all_to_all(cut, "frame", split_axis=0, concat_axis=0, tiled=True)

    out_grad_pix = exchange(out_grad)
    normed_pix = exchange(normed)[:, :, None]
    queries = project(normed_pix, query_weight)
    key_rows = project(normed_pix, key_weight)
    value_rows = project(normed_pix, value_weight)
    probs, probs_b, mixed_pix = attend(queries, key_rows, value_rows)
    mixed = exchange(mixed_pix).reshape(frames, rows, width, chan)
    block_out = (resid_f + jnp.dot(mixed, out_weight, preferred_element_type=jnp.float32)).astype(
        jnp.bfloat16
    )
    grad_out_w = outer_sum(mixed, out_grad)
    mixed_grad_pix = back_dot(out_grad_pix, out_weight).astype(jnp.bfloat16)[:, :, None]
    query_part, key_part, value_part = attend_back(
        probs, probs_b, queries, key_rows, value_rows, mixed_grad_pix
    )
    grad_query = outer_sum(normed_pix, query_part)
    grad_key = outer_sum(normed_pix, key_part)
    grad_value = outer_sum(normed_pix, value_part)
    normed_grad_pix = (
        back_dot(query_part, query_weight)
        + back_dot(key_part, key_weight)
        + back_dot(value_part, value_weight)
    ).astype(jnp.bfloat16)
    normed_grad = exchange(normed_grad_pix).reshape(frames, rows, width, chan)
    normed_gf = normed_grad.astype(jnp.float32)
    grad_gain = jnp.sum((normed_gf * resid_f * inv_rms).reshape(-1, chan), axis=0)
    tangent = normed_gf * norm_gain
    resid_part = inv_rms * tangent - resid_f * inv_rms**3 * jnp.mean(
        tangent * resid_f, axis=-1, keepdims=True
    )
    resid_grad = (out_grad.astype(jnp.float32) + resid_part).astype(jnp.bfloat16)
    grad_conv = conv_weight_grad(padded, resid_grad, rows, width)
    grad_pad = pad_rows(resid_grad)
    act_grad = conv_input_grad(grad_pad, conv_weight, rows, width)
    latents_grad = (
        resid_grad.astype(jnp.float32) + act_grad * sigma * (1.0 + latent_f * (1.0 - sigma))
    ).astype(jnp.bfloat16)
    summed = sum_everywhere(
        [grad_conv, grad_query, grad_key, grad_value, grad_out_w, grad_gain]
    )
    factor = cells_all ** (-0.5)
    return (
        block_out,
        latents_grad,
        summed[0] * factor,
        summed[1] * factor,
        summed[2] * factor,
        summed[3] * factor,
        summed[4] * factor,
        summed[5] * factor,
    )


def solution(mesh):
    return jax.shard_map(
        on_device,
        mesh=mesh,
        in_specs=(
            P("frame", "row", None, None),
            P(),
            P(),
            P(),
            P(),
            P(),
            P(),
            P("frame", "row", None, None),
        ),
        out_specs=(
            P("frame", "row", None, None),
            P("frame", "row", None, None),
            P(),
            P(),
            P(),
            P(),
            P(),
            P(),
        ),
        check_vma=False,
    )
```

```python
import functools

import jax
import jax.numpy as jnp
from jax import lax
from jax.experimental import pallas as pl
from jax.experimental.pallas import tpu as pltpu
from jax.sharding import PartitionSpec as P

EPS = 1e-06
MESH = pl.DeviceIdType.MESH
CHAN = 320
WIDE = 384
COLS = 128
ROWS = 4
HALF = 256
CONV_TILES = 512
SMALL_TILES = 256
PART = 256
MATRIX_TILES = 50
GAIN_TILE = 450
BLOCK = 16
F32 = jnp.float32
BF16 = jnp.bfloat16


def chip_sizes():
    return {"c": 2, "x": 4, "y": lax.axis_size("row") // 4, "z": lax.axis_size("frame") // 2}


def my_place():
    frame, row = lax.axis_index("frame"), lax.axis_index("row")
    return {
        "z": frame // 2,
        "x": lax.rem(row // 2, 2) * 2 + lax.rem(frame, 2),
        "y": row // 4,
        "c": lax.rem(row, 2),
    }


def device_of(place):
    return (
        place["z"] * 2 + lax.rem(place["x"], 2),
        (place["y"] * 2 + place["x"] // 2) * 2 + place["c"],
    )


def along(place, axis, step, sizes):
    moved = dict(place)
    moved[axis] = lax.rem(place[axis] + step, sizes[axis])
    return device_of(moved)


def remote(source, target, send_sem, recv_sem, device):
    copy = pltpu.make_async_remote_copy(
        src_ref=source,
        dst_ref=target,
        send_sem=send_sem,
        recv_sem=recv_sem,
        device_id=device,
        device_id_type=MESH,
    )
    copy.start()
    return copy


def dot(left, right):
    return jnp.dot(left, right, preferred_element_type=F32)


def dot_nt(left, right):
    return lax.dot_general(left, right, (((1,), (1,)), ((), ())), preferred_element_type=F32)


def dot_tn(left, right):
    return lax.dot_general(left, right, (((0,), (0,)), ((), ())), preferred_element_type=F32)


def add_up(target, start, own, own_start, received):
    count = own.shape[0] if own_start is None else received[0].shape[0]
    step = min(count, BLOCK)
    own_start = 0 if own_start is None else own_start

    def body(at, carry):
        at = at * step
        total = own[pl.ds(own_start + at, step)].astype(F32)
        for part in received:
            total = total + part[pl.ds(at, step)].astype(F32)
        target[pl.ds(start + at, step)] = total.astype(BF16)
        return carry

    lax.fori_loop(0, count // step, body, 0)


class Summer:
    def __init__(self, order, place, sizes, term, total, base, scratch):
        self.order, self.place, self.sizes = order, place, sizes
        self.term, self.total, self.base = term, total, base
        self.core_in, self.held, self.inbox = scratch[0], scratch[1:4], scratch[4:7]
        self.send_sems, self.recv_sems = scratch[7], scratch[8]
        self.spans = [PART // 2]
        for axis in order:
            self.spans.append(self.spans[-1] // sizes[axis])
        self.slot = 0
        self.sent = []
        self.wait = []

    def push(self, source, target, axis, step):
        device = along(self.place, axis, step, self.sizes)
        copy = remote(
            source, target, self.send_sems.at[self.slot], self.recv_sems.at[self.slot], device
        )
        self.slot += 1
        self.sent.append(copy)
        self.wait.append(copy)

    def arrive(self):
        for copy in self.wait:
            copy.wait_recv()
        self.wait = []

    def core_start(self):
        other = self.base + (1 - self.place["c"]) * self.spans[0]
        self.push(self.term.at[pl.ds(other, self.spans[0])], self.core_in, "c", 1)

    def core_end(self):
        self.arrive()
        mine = self.base + self.place["c"] * self.spans[0]
        add_up(self.held[0], 0, self.term, mine, [self.core_in])

    def scatter_start(self, level):
        axis, span = self.order[level], self.spans[level + 1]
        for step in range(1, self.sizes[axis]):
            peer = lax.rem(self.place[axis] + step, self.sizes[axis])
            self.push(
                self.held[level].at[pl.ds(peer * span, span)],
                self.inbox[level].at[step - 1],
                axis,
                step,
            )

    def scatter_end(self, level):
        self.arrive()
        axis, span = self.order[level], self.spans[level + 1]
        received = [self.inbox[level].at[step] for step in range(self.sizes[axis] - 1)]
        mine = self.place[axis] * span
        if level < 2:
            add_up(self.held[level + 1], 0, self.held[level], mine, received)
        else:
            add_up(self.total, self.start_of(3), self.held[level], mine, received)

    def start_of(self, levels):
        start = self.base + self.place["c"] * self.spans[0]
        for level in range(levels):
            start = start + self.place[self.order[level]] * self.spans[level + 1]
        return start

    def gather_start(self, level):
        axis = self.order[level]
        mine = self.total.at[pl.ds(self.start_of(level + 1), self.spans[level + 1])]
        for step in range(1, self.sizes[axis]):
            self.push(mine, mine, axis, step)

    def core_back(self):
        mine = self.total.at[pl.ds(self.start_of(0), self.spans[0])]
        self.push(mine, mine, "c", 1)

    def finish(self):
        for copy in self.sent:
            copy.wait_send()


def summer_scratch(order, sizes):
    spans = [PART // 2]
    for axis in order:
        spans.append(spans[-1] // sizes[axis])
    shapes = [(spans[0], 16, 128)]
    shapes += [(span, 16, 128) for span in spans[:3]]
    shapes += [(sizes[axis] - 1, span, 16, 128) for axis, span in zip(order, spans[1:])]
    copies = 2 * (1 + sum(sizes[axis] - 1 for axis in order))
    return [pltpu.VMEM(shape, BF16) for shape in shapes] + [
        pltpu.SemaphoreType.DMA((copies,)),
        pltpu.SemaphoreType.DMA((copies,)),
    ]


def pack(matrix, tiles, base):
    held = matrix.astype(BF16)
    for block in range(2):
        cut = held[:, block * 128 : block * 128 + 128]
        tiles[pl.ds(base + 20 * block, 20)] = cut.reshape(20, 16, 128)
    low, high = held[:160, 256:], held[160:, 256:]
    tail = jnp.concatenate([low, high], axis=1)
    tiles[pl.ds(base + 40, 10)] = tail.reshape(10, 16, 128)


def unpack(tiles, base, target, row):
    for block in range(2):
        cut = tiles[pl.ds(base + 20 * block, 20)].reshape(320, 128)
        target[pl.ds(row, 320), block * 128 : block * 128 + 128] = cut
    tail = tiles[pl.ds(base + 40, 10)].reshape(160, 128)
    target[pl.ds(row, 160), 256:] = tail[:, :64]
    target[pl.ds(row + 160, 160), 256:] = tail[:, 64:]


def shifts(cells):
    column = lax.broadcasted_iota(jnp.int32, cells.shape, 0)
    left = jnp.where(column == 0, 0.0, pltpu.roll(cells, 1, 0))
    right = jnp.where(column == COLS - 1, 0.0, pltpu.roll(cells, COLS - 1, 0))
    return [left, cells, right]


class Swap:
    def __init__(self, source, target, send_sems, recv_sems, peers, me):
        self.source, self.target, self.peers, self.me = source, target, peers, me
        self.send_sems, self.recv_sems = send_sems, recv_sems

    def start(self, half):
        for frame, device in self.peers:
            remote(
                self.source.at[half, frame],
                self.target.at[half, self.me],
                self.send_sems.at[half],
                self.recv_sems.at[half],
                device,
            )
        self.target[half, self.me] = self.source[half, self.me]

    def wait(self, half):
        span = self.target.at[half, pl.ds(0, len(self.peers))]
        pltpu.make_async_copy(span, span, self.recv_sems.at[half]).wait()

    def finish(self):
        for half in range(2):
            span = self.source.at[half, pl.ds(0, len(self.peers))]
            pltpu.make_async_copy(span, span, self.send_sems.at[half]).wait()


def norm_of(resid):
    return lax.rsqrt(jnp.mean(resid * resid, axis=-1, keepdims=True) + EPS)


def cell_start(half, at):
    if half == 0:
        return COLS + at * 64
    return jnp.where(at < 2, at * 64, HALF + at * 64)


def attention(q_s, k_s, v_s, d_s, bias, mixed_s, qp_s, kp_s, vp_s):
    lane = lax.broadcasted_iota(jnp.int32, (1, 128), 1)
    low = lane < 64
    masks = [jnp.where(low, 1.0, 0.0).astype(BF16), jnp.where(low, 0.0, 1.0).astype(BF16)]

    def tile(at, carry):
        span = pl.ds(pl.multiple_of(at * 128, 128), 128)
        queries, keys, values, grads = q_s[:, span], k_s[:, span], v_s[:, span], d_s[:, span]
        found = []
        for mask in masks:
            scores = dot_nt(queries * mask, keys) * 0.125 + bias[...]
            expo = jnp.exp(scores)
            probs = expo * (1.0 / jnp.sum(expo, axis=-1, keepdims=True))
            probs_b = probs.astype(BF16)
            mixed = dot(probs_b, values)
            prob_grad = dot_nt(grads * mask, values)
            inner = jnp.sum(probs * prob_grad, axis=-1, keepdims=True)
            score_b = (probs * (prob_grad - inner) * 0.125).astype(BF16)
            found.append(
                (mixed, dot(score_b, keys), dot_tn(score_b, queries), dot_tn(probs_b, grads))
            )
        for target, first, second in zip((mixed_s, qp_s, kp_s, vp_s), *found):
            target[:, span] = jnp.where(low, first, second).astype(BF16)
        return carry

    lax.fori_loop(0, 3, tile, 0)


def block_kernel(sizes, latents, conv_w, query_w, key_w, value_w, out_w, gain, out_grad, *refs):
    (block_out, latents_grad, conv_sum, small_sum, gain_sum), refs = refs[:5], refs[5:]
    (
        lat, grad, weights, wq, wk, wv, wo, gain_v, in_sems,
        padded, halo, halo_send, halo_recv, acc, resid, act_t,
        normed_out, normed_in, og_out, og_in, ng_out, ng_in, mix_out, mix_in,
        swap_send, swap_recv,
        q_s, k_s, v_s, d_s, bias, mixed_s, qp_s, kp_s, vp_s, parts, flip,
        resid_grad, grad_pad, gain_acc, conv_terms, conv_total, small_terms, small_total,
    ), refs = refs[:44], refs[44:]
    frames = lax.axis_size("frame")
    rows_n = lax.axis_size("row")
    chunk = HALF // frames
    me, row = lax.axis_index("frame"), lax.axis_index("row")
    place = my_place()
    peers = []
    for step in range(1, frames):
        frame = lax.rem(me + step, frames)
        peers.append((frame, (frame, row)))
    above = (me, lax.rem(row + rows_n - 1, rows_n))
    below = (me, lax.rem(row + 1, rows_n))

    barrier = pltpu.get_barrier_semaphore()
    partners = [device for _, device in peers] + [above, below]
    for axis in "cxy":
        partners += [along(place, axis, step, sizes) for step in range(1, sizes[axis])]
    for device in partners:
        pl.semaphore_signal(barrier, inc=1, device_id=device, device_id_type=MESH)

    loads = []
    pairs = (
        (latents, lat), (out_grad, grad), (conv_w, weights), (gain, gain_v),
        (out_w, wo), (query_w, wq), (key_w, wk), (value_w, wv),
    )
    for at, (source, target) in enumerate(pairs):
        loads.append(pltpu.make_async_copy(source, target, in_sems.at[at]))
        loads[-1].start()

    loads[0].wait()

    def activate(at, carry):
        cells = lat[pl.ds(at * COLS, COLS)].astype(F32)
        act = (cells * jax.nn.sigmoid(cells)).astype(BF16).astype(F32)
        for shift, copy in enumerate(shifts(act)):
            padded[shift, pl.ds((at + 1) * COLS, COLS)] = copy.astype(BF16)
        return carry

    lax.fori_loop(0, ROWS, activate, 0)
    pl.semaphore_wait(barrier, len(partners))

    def halo_start(source, kind):
        return [
            remote(source.at[pl.ds(COLS, COLS)], halo.at[kind, 1],
                   halo_send.at[kind, 0], halo_recv.at[kind, 0], above),
            remote(source.at[pl.ds(ROWS * COLS, COLS)], halo.at[kind, 0],
                   halo_send.at[kind, 1], halo_recv.at[kind, 1], below),
        ]

    def halo_end(copies, kind, target):
        for copy in copies:
            copy.wait_recv()
        ends = (row > 0, row < rows_n - 1)
        for side, inside in enumerate(ends):
            keep = jnp.where(inside, 1.0, 0.0).astype(F32)
            cells = halo[kind, side].astype(F32) * keep
            for shift, copy in enumerate(shifts(cells)):
                target[shift, pl.ds(side * (ROWS + 1) * COLS, COLS)] = copy.astype(BF16)

    act_halo = halo_start(padded.at[1], 0)

    swaps = []
    buffers = ((og_out, og_in), (normed_out, normed_in), (ng_out, ng_in), (mix_out, mix_in))
    for at, (source, target) in enumerate(buffers):
        swaps.append(Swap(source, target, swap_send.at[at], swap_recv.at[at], peers, me))
    og_swap, normed_swap, ng_swap, mix_swap = swaps

    loads[1].wait()
    og_out[0] = grad[COLS : COLS + HALF].reshape(frames, chunk, CHAN)
    og_out[1, : frames // 2] = grad[:COLS].reshape(frames // 2, chunk, CHAN)
    og_out[1, frames // 2 :] = grad[COLS + HALF :].reshape(frames // 2, chunk, CHAN)
    loads[2].wait()
    loads[3].wait()

    def conv_half(half):
        acc[pl.ds(0, HALF)] = jnp.zeros((HALF, CHAN), F32)

        def tap(at, carry):
            a, b = at // 3, lax.rem(at, 3)
            if half == 0:
                cells = padded[b, pl.ds((a + 1) * COLS, HALF)]
            else:
                cells = jnp.concatenate(
                    [padded[b, pl.ds(a * COLS, COLS)], padded[b, pl.ds((a + 3) * COLS, COLS)]]
                )
            acc[pl.ds(0, HALF)] += dot(cells, weights[at])
            return carry

        lax.fori_loop(0, 9, tap, 0)
        count = 64 // chunk

        def finish(at, carry):
            cells = lat[pl.ds(pl.multiple_of(cell_start(half, at), 64), 64)].astype(F32)
            held = (cells + acc[pl.ds(at * 64, 64)]).astype(BF16)
            resid[half, pl.ds(at * 64, 64)] = held
            held = held.astype(F32)
            normed = (held * norm_of(held) * gain_v[...]).astype(BF16)
            normed_out[half, pl.ds(at * count, count)] = normed.reshape(count, chunk, CHAN)
            return carry

        lax.fori_loop(0, 4, finish, 0)

    conv_half(0)
    normed_swap.start(0)
    og_swap.start(0)
    halo_end(act_halo, 0, padded)
    conv_half(1)
    normed_swap.start(1)
    og_swap.start(1)

    position = lax.broadcasted_iota(jnp.int32, (HALF, HALF), 0)
    other = lax.broadcasted_iota(jnp.int32, (HALF, HALF), 1)
    same = lax.rem(position, chunk) == lax.rem(other, chunk)
    bias[...] = jnp.where(same, 0.0, -1e30)
    for field in (q_s, k_s, v_s, d_s):
        field[:, 256:] = jnp.zeros((HALF, 128), BF16)
    for shift in range(3):
        act_t[shift] = padded[shift].astype(F32).T.astype(BF16)
    for load in loads[4:]:
        load.wait()

    for half in range(2):
        og_swap.wait(half)
        d_s[:, :CHAN] = dot_nt(og_in[half].reshape(HALF, CHAN), wo[...]).astype(BF16)
        normed_swap.wait(half)
        normed = normed_in[half].reshape(HALF, CHAN)
        q_s[:, :CHAN] = dot(normed, wq[...]).astype(BF16)
        k_s[:, :CHAN] = dot(normed, wk[...]).astype(BF16)
        v_s[:, :CHAN] = dot(normed, wv[...]).astype(BF16)
        attention(q_s, k_s, v_s, d_s, bias, mixed_s, qp_s, kp_s, vp_s)
        back = dot_nt(qp_s[:, :CHAN], wq[...])
        back = back + dot_nt(kp_s[:, :CHAN], wk[...])
        back = back + dot_nt(vp_s[:, :CHAN], wv[...])
        ng_out[half] = back.astype(BF16).reshape(frames, chunk, CHAN)
        ng_swap.start(half)
        mix_out[half] = mixed_s[:, :CHAN].reshape(frames, chunk, CHAN)
        mix_swap.start(half)
        for at, field in enumerate((qp_s, kp_s, vp_s)):
            parts[at, pl.ds(half * HALF, HALF)] = field[:, :CHAN]

    flip[0] = normed_in[...].reshape(2 * HALF, CHAN).astype(F32).T.astype(BF16)
    flip[1] = mix_out[...].reshape(2 * HALF, CHAN).astype(F32).T.astype(BF16)
    for at in range(3):
        pack(dot(flip[0], parts[at]), small_terms, at * MATRIX_TILES)
    pack(dot(flip[1], og_in[...].reshape(2 * HALF, CHAN)), small_terms, 3 * MATRIX_TILES)
    spare = SMALL_TILES - 4 * MATRIX_TILES
    small_terms[pl.ds(4 * MATRIX_TILES, spare)] = jnp.zeros((spare, 16, 128), BF16)

    summers = []
    for at, order in enumerate(("xyz", "yxz", "zxy")):
        scratch = refs[9 * at : 9 * at + 9]
        if at < 2:
            summers.append(
                Summer(order, place, sizes, conv_terms, conv_total, at * PART, scratch)
            )
        else:
            summers.append(Summer(order, place, sizes, small_terms, small_total, 0, scratch))
    first, second, small = summers
    small.core_start()

    gain_acc[...] = jnp.zeros((8, CHAN), F32)
    for half in range(2):
        ng_swap.wait(half)

        def undo_norm(at, carry, half=half):
            count = 64 // chunk
            begin = pl.multiple_of(cell_start(half, at), 64)
            held = resid[half, pl.ds(at * 64, 64)].astype(F32)
            back = ng_in[half, pl.ds(at * count, count)].reshape(64, CHAN).astype(F32)
            inv = norm_of(held)
            product = back * held
            total = jnp.sum((product * inv).reshape(8, 8, CHAN), axis=0)
            gain_acc[...] += total
            tangent = back * gain_v[...]
            mean = jnp.mean(product * gain_v[...], axis=-1, keepdims=True)
            value = grad[pl.ds(begin, 64)].astype(F32) + (
                inv * tangent - held * (inv * inv * inv) * mean
            )
            resid_grad[pl.ds(begin, 64)] = value.astype(BF16)
            return carry

        lax.fori_loop(0, 4, undo_norm, 0)
    small.core_end()
    small.scatter_start(0)

    def pad_grad(at, carry):
        cells = resid_grad[pl.ds(at * COLS, COLS)].astype(F32)
        for shift, copy in enumerate(shifts(cells)):
            grad_pad[shift, pl.ds((at + 1) * COLS, COLS)] = copy.astype(BF16)
        return carry

    lax.fori_loop(0, ROWS, pad_grad, 0)
    grad_halo = halo_start(grad_pad.at[1], 1)

    def conv_tap(at, carry):
        a, b = at // 3, lax.rem(at, 3)
        cells = act_t[b, :, pl.ds(pl.multiple_of(a * COLS, COLS), ROWS * COLS)]
        pack(dot(cells, resid_grad[...]), conv_terms, at * MATRIX_TILES)
        return carry

    lax.fori_loop(0, 6, conv_tap, 0)
    first.core_start()
    spare = CONV_TILES - GAIN_TILE
    conv_terms[pl.ds(GAIN_TILE, spare)] = jnp.zeros((spare, 16, 128), BF16)
    gains = jnp.sum(gain_acc[...], axis=0, keepdims=True)
    line = lax.broadcasted_iota(jnp.int32, (16, 128), 0)
    gain_tile = jnp.where(line == 0, gains[:, :128], jnp.where(line == 1, gains[:, 128:256], 0.0))
    conv_terms[GAIN_TILE] = gain_tile.astype(BF16)
    tail = jnp.where(line[:, :64] == 0, gains[:, 256:], 0.0)
    conv_terms[GAIN_TILE + 1, :, :64] = tail.astype(BF16)
    lax.fori_loop(6, 9, conv_tap, 0)
    second.core_start()
    small.scatter_end(0)
    small.scatter_start(1)
    first.core_end()
    first.scatter_start(0)
    second.core_end()
    second.scatter_start(0)
    small.scatter_end(1)
    small.scatter_start(2)

    for half in range(2):
        mix_swap.wait(half)
        acc[pl.ds(0, HALF)] = dot(mix_in[half].reshape(HALF, CHAN), wo[...])

        def write_out(at, carry, half=half):
            begin = pl.multiple_of(cell_start(half, at), 64)
            held = resid[half, pl.ds(at * 64, 64)].astype(F32)
            block_out[pl.ds(begin, 64)] = (held + acc[pl.ds(at * 64, 64)]).astype(BF16)
            return carry

        lax.fori_loop(0, 4, write_out, 0)
    for part in (first, second):
        part.scatter_end(0)
        part.scatter_start(1)
    small.scatter_end(2)
    small.gather_start(2)
    halo_end(grad_halo, 1, grad_pad)
    acc[...] = jnp.zeros((2 * HALF, CHAN), F32)

    def back_tap(at, carry):
        a, b = at // 3, lax.rem(at, 3)
        cells = grad_pad[2 - b, pl.ds((2 - a) * COLS, ROWS * COLS)]
        acc[...] += dot_nt(cells, weights[at])
        return carry

    lax.fori_loop(0, 4, back_tap, 0)
    for part in (first, second):
        part.scatter_end(1)
        part.scatter_start(2)
    small.arrive()
    small.gather_start(1)
    lax.fori_loop(4, 9, back_tap, 0)
    for part in (first, second):
        part.scatter_end(2)
        part.gather_start(2)
    small.arrive()
    small.gather_start(0)

    def write_back(at, carry):
        cells = lat[pl.ds(at * COLS, COLS)].astype(F32)
        sigma = jax.nn.sigmoid(cells)
        slope = sigma * (1.0 + cells * (1.0 - sigma))
        value = resid_grad[pl.ds(at * COLS, COLS)].astype(F32) + acc[pl.ds(at * COLS, COLS)] * slope
        latents_grad[pl.ds(at * COLS, COLS)] = value.astype(BF16)
        return carry

    lax.fori_loop(0, ROWS, write_back, 0)
    for part in (first, second):
        part.arrive()
        part.gather_start(1)
    small.arrive()
    small.core_back()
    for part in (first, second):
        part.arrive()
        part.gather_start(0)
    small.arrive()

    def small_out(at, carry):
        unpack(small_total, at * MATRIX_TILES, small_sum, at * CHAN)
        return carry

    lax.fori_loop(0, 4, small_out, 0)
    for part in (first, second):
        part.arrive()
        part.core_back()
    for part in (first, second):
        part.arrive()

    def conv_out(at, carry):
        unpack(conv_total, at * MATRIX_TILES, conv_sum, at * CHAN)
        return carry

    lax.fori_loop(0, 9, conv_out, 0)
    gain_sum[...] = conv_total[GAIN_TILE : GAIN_TILE + 2]
    for part in summers:
        part.finish()
    for swap in swaps:
        swap.finish()
    for copy in act_halo + grad_halo:
        copy.wait_send()


def block_scratch(sizes, frames):
    chunk = HALF // frames
    field = (2, frames, chunk, CHAN)
    vmem = pltpu.VMEM
    dma = pltpu.SemaphoreType.DMA
    weight = vmem((CHAN, CHAN), BF16)
    shapes = [
        vmem((ROWS * COLS, CHAN), BF16), vmem((ROWS * COLS, CHAN), BF16),
        vmem((9, CHAN, CHAN), BF16), weight, weight, weight, weight, vmem((1, CHAN), F32), dma((8,)),
        vmem((3, (ROWS + 2) * COLS, CHAN), BF16), vmem((2, 2, COLS, CHAN), BF16),
        dma((2, 2)), dma((2, 2)), vmem((2 * HALF, CHAN), F32), vmem((2, HALF, CHAN), BF16),
        vmem((3, CHAN, (ROWS + 2) * COLS), BF16),
    ]
    shapes += [vmem(field, BF16)] * 8 + [dma((4, 2)), dma((4, 2))]
    shapes += [vmem((HALF, WIDE), BF16)] * 4 + [vmem((HALF, HALF), F32)]
    shapes += [vmem((HALF, WIDE), BF16)] * 4
    shapes += [vmem((3, 2 * HALF, CHAN), BF16), vmem((2, CHAN, 2 * HALF), BF16)]
    shapes += [vmem((ROWS * COLS, CHAN), BF16), vmem((3, (ROWS + 2) * COLS, CHAN), BF16)]
    shapes += [vmem((8, CHAN), F32)]
    shapes += [vmem((CONV_TILES, 16, 128), BF16)] * 2 + [vmem((SMALL_TILES, 16, 128), BF16)] * 2
    for order in ("xyz", "yxz", "zxy"):
        shapes += summer_scratch(order, sizes)
    return shapes


def on_device(
    latents, conv_weight, query_weight, key_weight, value_weight, out_weight, norm_gain, out_grad
):
    shape = latents.shape
    cells = ROWS * COLS
    sizes = chip_sizes()
    frames = lax.axis_size("frame")
    anywhere = pl.BlockSpec(memory_space=pl.ANY)
    inside = pl.BlockSpec(memory_space=pltpu.VMEM)
    block_out, latents_grad, conv_sum, small_sum, gain_sum = pl.pallas_call(
        functools.partial(block_kernel, sizes),
        out_shape=[
            jax.ShapeDtypeStruct((cells, CHAN), BF16),
            jax.ShapeDtypeStruct((cells, CHAN), BF16),
            jax.ShapeDtypeStruct((9 * CHAN, CHAN), BF16),
            jax.ShapeDtypeStruct((4 * CHAN, CHAN), BF16),
            jax.ShapeDtypeStruct((2, 16, 128), BF16),
        ],
        in_specs=[anywhere] * 8,
        out_specs=[inside] * 5,
        scratch_shapes=block_scratch(sizes, frames),
        compiler_params=pltpu.CompilerParams(
            collective_id=0, has_side_effects=True, vmem_limit_bytes=56 << 20
        ),
    )(
        latents.reshape(cells, CHAN),
        conv_weight.reshape(9, CHAN, CHAN),
        query_weight,
        key_weight,
        value_weight,
        out_weight,
        norm_gain.reshape(1, CHAN),
        out_grad.reshape(cells, CHAN),
    )
    factor = (cells * frames * lax.axis_size("row")) ** (-0.5)
    small = [
        small_sum[at * CHAN : (at + 1) * CHAN].astype(F32) * factor for at in range(4)
    ]
    gains = jnp.concatenate([gain_sum[0, 0], gain_sum[0, 1], gain_sum[1, 0, :64]])
    return (
        block_out.reshape(shape),
        latents_grad.reshape(shape),
        conv_sum.astype(F32).reshape(3, 3, CHAN, CHAN) * factor,
        *small,
        gains.astype(F32) * factor,
    )


def solution(mesh):
    split = P("frame", "row", None, None)
    return jax.shard_map(
        on_device,
        mesh=mesh,
        in_specs=(split, P(), P(), P(), P(), P(), P(), split),
        out_specs=(split, split, P(), P(), P(), P(), P(), P()),
        check_vma=False,
    )
```

```python
import functools

import jax
import jax.numpy as jnp
from jax import lax
from jax.experimental import pallas as pl
from jax.experimental.pallas import tpu as pltpu
from jax.sharding import PartitionSpec as P

EPS = 1e-06
MESH = pl.DeviceIdType.MESH
CHAN = 320
WIDE = 384
COLS = 128
ROWS = 4
HALF = 256
CONV_TILES = 512
SMALL_TILES = 256
PART = 256
MATRIX_TILES = 50
GAIN_TILE = 450
BLOCK = 16
F32 = jnp.float32
BF16 = jnp.bfloat16


def chip_sizes():
    return {"c": 2, "x": 4, "y": lax.axis_size("row") // 4, "z": lax.axis_size("frame") // 2}


def my_place():
    frame, row = lax.axis_index("frame"), lax.axis_index("row")
    return {
        "z": frame // 2,
        "x": lax.rem(row // 2, 2) * 2 + lax.rem(frame, 2),
        "y": row // 4,
        "c": lax.rem(row, 2),
    }


def device_of(place):
    return (
        place["z"] * 2 + lax.rem(place["x"], 2),
        (place["y"] * 2 + place["x"] // 2) * 2 + place["c"],
    )


def along(place, axis, step, sizes):
    moved = dict(place)
    moved[axis] = lax.rem(place[axis] + step, sizes[axis])
    return device_of(moved)


def remote(source, target, send_sem, recv_sem, device):
    copy = pltpu.make_async_remote_copy(
        src_ref=source,
        dst_ref=target,
        send_sem=send_sem,
        recv_sem=recv_sem,
        device_id=device,
        device_id_type=MESH,
    )
    copy.start()
    return copy


def dot(left, right):
    return jnp.dot(left, right, preferred_element_type=F32)


def dot_nt(left, right):
    return lax.dot_general(left, right, (((1,), (1,)), ((), ())), preferred_element_type=F32)


def dot_tn(left, right):
    return lax.dot_general(left, right, (((0,), (0,)), ((), ())), preferred_element_type=F32)


def add_up(target, start, own, own_start, received):
    count = received[0].shape[0]
    step = min(count, BLOCK)

    def body(at, carry):
        at = at * step
        total = own[pl.ds(own_start + at, step)].astype(F32)
        for part in received:
            total = total + part[pl.ds(at, step)].astype(F32)
        target[pl.ds(start + at, step)] = total.astype(BF16)
        return carry

    lax.fori_loop(0, count // step, body, 0)


def wait_bytes(span, sem):
    pltpu.make_async_copy(span, span, sem).wait()


class ConvSummer:
    ORDERS = ("xy", "yx")

    def __init__(self, place, sizes, terms, total, scratch):
        self.place, self.sizes, self.terms, self.total = place, sizes, terms, total
        (
            self.core_in, self.held0, self.inbox0, self.held1, self.inbox1, self.held2, self.inbox2,
            self.core_sems, self.scatter0, self.scatter1, self.scatter2,
            self.gather2, self.gather1, self.gather0, self.back, self.sends,
        ) = scratch
        self.unit = PART // (2 * sizes["x"] * sizes["y"] * sizes["z"])
        self.group = self.unit * sizes["z"]
        self.n1 = [sizes[order[0]] for order in self.ORDERS]
        self.n2 = [sizes[order[1]] for order in self.ORDERS]

    def at(self, part, axis):
        return self.place[self.ORDERS[part][axis]]

    def peer(self, part, axis, step):
        return lax.rem(self.at(part, axis) + step, self.sizes[self.ORDERS[part][axis]])

    def device(self, axis, step):
        return along(self.place, axis, step, self.sizes)

    def tile(self, part, chunk, core, group, unit=0):
        span = self.n2[part] * self.group
        return part * PART + (chunk * 2 + core) * span + group * self.group + unit * self.unit

    def core_start(self, piece):
        n1, span = self.n1[0], self.n2[0] * self.group
        start = piece * 2 * span + (1 - self.place["c"]) * span
        remote(
            self.terms.at[pl.ds(start, span)],
            self.core_in.at[pl.ds(piece * span, span)],
            self.sends.at[0],
            self.core_sems.at[piece],
            self.device("c", 1),
        )

    def core_wait(self, part, chunk):
        span = self.n2[part] * self.group
        wait_bytes(self.core_in.at[pl.ds(0, span)], self.core_sems.at[part * self.n1[part] + chunk])

    def core_sum(self, part, chunk, group):
        own = self.tile(part, chunk, self.place["c"], group)
        there = (part * self.n1[part] + chunk) * self.n2[part] * self.group + group * self.group
        total = self.terms[pl.ds(own, self.group)].astype(F32)
        return total + self.core_in[pl.ds(there, self.group)].astype(F32)

    def scatter_first(self):
        for step2 in range(self.n2[0]):
            step2 = (step2 + 1) % self.n2[0]
            for step in range(1, self.n1[0]):
                for part in range(2):
                    chunk, group = self.peer(part, 0, step), self.peer(part, 1, step2)
                    if step2 == 1:
                        self.core_wait(part, chunk)
                    slot = part * self.n1[part] * self.n2[part] + chunk * self.n2[part] + group
                    held = self.held0.at[pl.ds(slot * self.group, self.group)]
                    held[...] = self.core_sum(part, chunk, group).astype(BF16)
                    remote(
                        held,
                        self.inbox0.at[part, group, pl.ds((step - 1) * self.group, self.group)],
                        self.sends.at[1],
                        self.scatter0.at[part, step2],
                        self.device(self.ORDERS[part][0], step),
                    )

    def scatter_second(self):
        for step2 in range(self.n2[0]):
            step2 = (step2 + 1) % self.n2[0]
            for part in range(2):
                chunk, group = self.at(part, 0), self.peer(part, 1, step2)
                if step2 == 1:
                    self.core_wait(part, chunk)
                wait_bytes(self.inbox0.at[part, group], self.scatter0.at[part, step2])
                total = self.core_sum(part, chunk, group)
                for step in range(self.n1[part] - 1):
                    span = pl.ds(step * self.group, self.group)
                    total = total + self.inbox0[part, group, span].astype(F32)
                held = self.held1.at[part, group]
                held[...] = total.astype(BF16)
                if step2 > 0:
                    remote(
                        held,
                        self.inbox1.at[part, pl.ds((step2 - 1) * self.group, self.group)],
                        self.sends.at[2],
                        self.scatter1.at[part],
                        self.device(self.ORDERS[part][1], step2),
                    )

    def scatter_third(self):
        for part in range(2):
            wait_bytes(self.inbox1.at[part], self.scatter1.at[part])
            total = self.held1[part, self.at(part, 1)].astype(F32)
            for step in range(self.n2[part] - 1):
                total = total + self.inbox1[part, pl.ds(step * self.group, self.group)].astype(F32)
            self.held2[part] = total.astype(BF16)
            for step in range(1, self.sizes["z"]):
                peer = lax.rem(self.place["z"] + step, self.sizes["z"])
                remote(
                    self.held2.at[part, pl.ds(peer * self.unit, self.unit)],
                    self.inbox2.at[part, pl.ds((step - 1) * self.unit, self.unit)],
                    self.sends.at[3],
                    self.scatter2.at[part],
                    self.device("z", step),
                )

    def gather_third(self):
        for part in range(2):
            wait_bytes(self.inbox2.at[part], self.scatter2.at[part])
            z = self.place["z"]
            total = self.held2[part, pl.ds(z * self.unit, self.unit)].astype(F32)
            for step in range(self.sizes["z"] - 1):
                total = total + self.inbox2[part, pl.ds(step * self.unit, self.unit)].astype(F32)
            mine = self.tile(part, self.at(part, 0), self.place["c"], self.at(part, 1), z)
            self.total[pl.ds(mine, self.unit)] = total.astype(BF16)
            span = self.total.at[pl.ds(mine, self.unit)]
            for step in range(1, self.sizes["z"]):
                remote(
                    span, span, self.sends.at[4], self.gather2.at[part], self.device("z", step)
                )

    def spread(self, part, chunk, group, axis, steps, send, sem):
        span = self.total.at[pl.ds(self.tile(part, chunk, self.place["c"], group), self.group)]
        for step in steps:
            remote(span, span, self.sends.at[send], sem, self.device(axis, step))

    def gather_rest(self):
        n1, n2 = self.n1[0], self.n2[0]
        for part in range(2):
            wait_bytes(
                self.total.at[pl.ds(0, (self.sizes["z"] - 1) * self.unit)], self.gather2.at[part]
            )
            first, second = self.ORDERS[part]
            chunk, group = self.at(part, 0), self.at(part, 1)
            for step in range(1, n2):
                sem = self.gather1.at[part, step]
                self.spread(part, chunk, group, second, [step], 5, sem)
            self.spread(part, chunk, group, first, range(1, n1), 6, self.gather0.at[part, 0])
            self.spread(part, chunk, group, "c", [1], 7, self.back.at[0])
        for step2 in range(1, n2):
            for part in range(2):
                first = self.ORDERS[part][0]
                chunk = self.at(part, 0)
                group = self.peer(part, 1, n2 - step2)
                wait_bytes(self.total.at[pl.ds(0, self.group)], self.gather1.at[part, step2])
                self.spread(
                    part, chunk, group, first, range(1, n1), 6, self.gather0.at[part, step2]
                )
                self.spread(part, chunk, group, "c", [1], 7, self.back.at[0])
        for step2 in range(n2):
            for part in range(2):
                wait_bytes(
                    self.total.at[pl.ds(0, (n1 - 1) * self.group)], self.gather0.at[part, step2]
                )
                group = self.peer(part, 1, n2 - step2)
                for step in range(1, n1):
                    chunk = self.peer(part, 0, n1 - step)
                    self.spread(part, chunk, group, "c", [1], 7, self.back.at[0])

    def finish(self):
        wait_bytes(self.total.at[pl.ds(0, PART)], self.back.at[0])
        n1, n2, nz = self.n1[0], self.n2[0], self.sizes["z"]
        counts = (
            PART, 2 * n2 * (n1 - 1) * self.group, 2 * (n2 - 1) * self.group,
            2 * (nz - 1) * self.unit, 2 * (nz - 1) * self.unit, 2 * (n2 - 1) * self.group,
            2 * n2 * (n1 - 1) * self.group, PART,
        )
        for at, count in enumerate(counts):
            wait_bytes(self.total.at[pl.ds(0, count)], self.sends.at[at])


def conv_summer_scratch(sizes):
    unit = PART // (2 * sizes["x"] * sizes["y"] * sizes["z"])
    group = unit * sizes["z"]
    n1, n2 = sizes["x"], sizes["y"]
    tiles = [
        (PART,), (PART,), (2, n2, (n1 - 1) * group), (2, n2, group), (2, (n2 - 1) * group),
        (2, group), (2, (sizes["z"] - 1) * unit),
    ]
    sems = [(2 * n1,), (2, n2), (2,), (2,), (2,), (2, n2), (2, n2), (1,), (8,)]
    return [pltpu.VMEM(shape + (16, 128), BF16) for shape in tiles] + [
        pltpu.SemaphoreType.DMA(shape) for shape in sems
    ]


class Summer:
    def __init__(self, order, place, sizes, term, total, base, scratch):
        self.order, self.place, self.sizes = order, place, sizes
        self.term, self.total, self.base = term, total, base
        self.core_in, self.held, self.inbox = scratch[0], scratch[1:4], scratch[4:7]
        self.send_sems, self.recv_sems = scratch[7], scratch[8]
        self.spans = [PART // 2]
        for axis in order:
            self.spans.append(self.spans[-1] // sizes[axis])
        self.slot = 0
        self.sent = []
        self.wait = []

    def push(self, source, target, axis, step):
        device = along(self.place, axis, step, self.sizes)
        copy = remote(
            source, target, self.send_sems.at[self.slot], self.recv_sems.at[self.slot], device
        )
        self.slot += 1
        self.sent.append(copy)
        self.wait.append(copy)

    def arrive(self):
        for copy in self.wait:
            copy.wait_recv()
        self.wait = []

    def core_start(self):
        other = self.base + (1 - self.place["c"]) * self.spans[0]
        self.push(self.term.at[pl.ds(other, self.spans[0])], self.core_in, "c", 1)

    def core_end(self):
        self.arrive()
        mine = self.base + self.place["c"] * self.spans[0]
        add_up(self.held[0], 0, self.term, mine, [self.core_in])

    def scatter_start(self, level):
        axis, span = self.order[level], self.spans[level + 1]
        for step in range(1, self.sizes[axis]):
            peer = lax.rem(self.place[axis] + step, self.sizes[axis])
            self.push(
                self.held[level].at[pl.ds(peer * span, span)],
                self.inbox[level].at[step - 1],
                axis,
                step,
            )

    def scatter_end(self, level):
        self.arrive()
        axis, span = self.order[level], self.spans[level + 1]
        received = [self.inbox[level].at[step] for step in range(self.sizes[axis] - 1)]
        mine = self.place[axis] * span
        if level < 2:
            add_up(self.held[level + 1], 0, self.held[level], mine, received)
        else:
            add_up(self.total, self.start_of(3), self.held[level], mine, received)

    def start_of(self, levels):
        start = self.base + self.place["c"] * self.spans[0]
        for level in range(levels):
            start = start + self.place[self.order[level]] * self.spans[level + 1]
        return start

    def gather_start(self, level):
        axis = self.order[level]
        mine = self.total.at[pl.ds(self.start_of(level + 1), self.spans[level + 1])]
        for step in range(1, self.sizes[axis]):
            self.push(mine, mine, axis, step)

    def core_back(self):
        mine = self.total.at[pl.ds(self.start_of(0), self.spans[0])]
        self.push(mine, mine, "c", 1)

    def finish(self):
        for copy in self.sent:
            copy.wait_send()


def summer_scratch(order, sizes):
    spans = [PART // 2]
    for axis in order:
        spans.append(spans[-1] // sizes[axis])
    shapes = [(spans[0], 16, 128)]
    shapes += [(span, 16, 128) for span in spans[:3]]
    shapes += [(sizes[axis] - 1, span, 16, 128) for axis, span in zip(order, spans[1:])]
    copies = 2 * (1 + sum(sizes[axis] - 1 for axis in order))
    return [pltpu.VMEM(shape, BF16) for shape in shapes] + [
        pltpu.SemaphoreType.DMA((copies,)),
        pltpu.SemaphoreType.DMA((copies,)),
    ]


def pack(matrix, tiles, base):
    held = matrix.astype(BF16)
    for block in range(2):
        cut = held[:, block * 128 : block * 128 + 128]
        tiles[pl.ds(base + 20 * block, 20)] = cut.reshape(20, 16, 128)
    low, high = held[:160, 256:], held[160:, 256:]
    tail = jnp.concatenate([low, high], axis=1)
    tiles[pl.ds(base + 40, 10)] = tail.reshape(10, 16, 128)


def unpack(tiles, base, target, at, factor):
    for block in range(2):
        cut = tiles[pl.ds(base + 20 * block, 20)].reshape(CHAN, 128)
        target[at, :, block * 128 : block * 128 + 128] = cut.astype(F32) * factor
    tail = tiles[pl.ds(base + 40, 10)].reshape(160, 128).astype(F32) * factor
    target[at, :160, 256:] = tail[:, :64]
    target[at, 160:, 256:] = tail[:, 64:]


def finish_kernel(factor, block_in, back_in, conv_in, small_in, *refs):
    (block_out, back_out, conv_out), small_outs, gain_out = refs[:3], refs[3:7], refs[7]
    conv, small, wide, fields, through, load_sems, store_sems = refs[8:]
    moves = []
    for at, (source, target) in enumerate(((block_in, block_out), (back_in, back_out))):
        moves.append(
            (
                pltpu.make_async_copy(source, fields.at[at], through.at[at]),
                pltpu.make_async_copy(fields.at[at], target, through.at[at + 2]),
            )
        )
        moves[-1][0].start()

    def load(at, source, target):
        span = pl.ds(at * MATRIX_TILES, MATRIX_TILES)
        return source.at[span], target.at[span]

    for at in range(4):
        pltpu.make_async_copy(*load(at, small_in, small), load_sems.at[9 + at]).start()
    for at in range(9):
        pltpu.make_async_copy(*load(at, conv_in, conv), load_sems.at[at]).start()
    last = pl.ds(GAIN_TILE, 2)
    gain_load = pltpu.make_async_copy(conv_in.at[last], conv.at[last], load_sems.at[13])
    gain_load.start()
    for at in range(4):
        pltpu.make_async_copy(*load(at, small_in, small), load_sems.at[9 + at]).wait()
        unpack(small, at * MATRIX_TILES, wide, 9 + at, factor)
        pltpu.make_async_copy(wide.at[9 + at], small_outs[at], store_sems.at[9 + at]).start()

    def conv_tap(at, carry):
        pltpu.make_async_copy(*load(at, conv_in, conv), load_sems.at[at]).wait()
        unpack(conv, at * MATRIX_TILES, wide, at, factor)
        pltpu.make_async_copy(wide.at[at], conv_out.at[at], store_sems.at[at]).start()
        return carry

    for move in moves:
        move[0].wait()
        move[1].start()
    lax.fori_loop(0, 9, conv_tap, 0)
    gain_load.wait()
    gain_out[0:128] = (conv[GAIN_TILE].astype(F32) * factor)[0]
    gain_out[128:256] = (conv[GAIN_TILE].astype(F32) * factor)[1]
    gain_out[256:] = (conv[GAIN_TILE + 1].astype(F32) * factor)[0, :64]
    for move in moves:
        move[1].wait()
    for at in range(9):
        pltpu.make_async_copy(wide.at[at], conv_out.at[at], store_sems.at[at]).wait()
    for at in range(4):
        pltpu.make_async_copy(wide.at[9 + at], small_outs[at], store_sems.at[9 + at]).wait()


def shifts(cells):
    column = lax.broadcasted_iota(jnp.int32, cells.shape, 0)
    left = jnp.where(column == 0, 0.0, pltpu.roll(cells, 1, 0))
    right = jnp.where(column == COLS - 1, 0.0, pltpu.roll(cells, COLS - 1, 0))
    return [left, cells, right]


class Swap:
    def __init__(self, source, target, send_sems, recv_sems, peers, me):
        self.source, self.target, self.peers, self.me = source, target, peers, me
        self.send_sems, self.recv_sems = send_sems, recv_sems

    def start(self, half):
        for frame, device in self.peers:
            remote(
                self.source.at[half, frame],
                self.target.at[half, self.me],
                self.send_sems.at[half],
                self.recv_sems.at[half],
                device,
            )
        self.target[half, self.me] = self.source[half, self.me]

    def wait(self, half):
        span = self.target.at[half, pl.ds(0, len(self.peers))]
        pltpu.make_async_copy(span, span, self.recv_sems.at[half]).wait()

    def finish(self):
        for half in range(2):
            span = self.source.at[half, pl.ds(0, len(self.peers))]
            pltpu.make_async_copy(span, span, self.send_sems.at[half]).wait()


def norm_of(resid):
    return lax.rsqrt(jnp.mean(resid * resid, axis=-1, keepdims=True) + EPS)


def cell_start(half, at):
    if half == 0:
        return COLS + at * 64
    return jnp.where(at < 2, at * 64, HALF + at * 64)


def attention(q_s, k_s, v_s, d_s, bias, mixed_s, qp_s, kp_s, vp_s):
    lane = lax.broadcasted_iota(jnp.int32, (1, 128), 1)
    low = lane < 64
    masks = [jnp.where(low, 1.0, 0.0).astype(BF16), jnp.where(low, 0.0, 1.0).astype(BF16)]

    def tile(at, carry):
        span = pl.ds(pl.multiple_of(at * 128, 128), 128)
        queries, keys, values, grads = q_s[:, span], k_s[:, span], v_s[:, span], d_s[:, span]
        found = []
        for mask in masks:
            scores = dot_nt(queries * mask, keys) * 0.125 + bias[...]
            expo = jnp.exp(scores)
            probs = expo * (1.0 / jnp.sum(expo, axis=-1, keepdims=True))
            probs_b = probs.astype(BF16)
            mixed = dot(probs_b, values)
            prob_grad = dot_nt(grads * mask, values)
            inner = jnp.sum(probs * prob_grad, axis=-1, keepdims=True)
            score_b = (probs * (prob_grad - inner) * 0.125).astype(BF16)
            found.append(
                (mixed, dot(score_b, keys), dot_tn(score_b, queries), dot_tn(probs_b, grads))
            )
        for target, first, second in zip((mixed_s, qp_s, kp_s, vp_s), *found):
            target[:, span] = jnp.where(low, first, second).astype(BF16)
        return carry

    lax.fori_loop(0, 3, tile, 0)


def block_kernel(sizes, latents, conv_w, query_w, key_w, value_w, out_w, gain, out_grad, *refs):
    (block_out, latents_grad, conv_total, small_total), refs = refs[:4], refs[4:]
    (
        lat_in, grad_in, lat, grad, weights, wq, wk, wv, wo, gain_v, in_sems,
        padded, halo, halo_send, halo_recv, acc, resid, act_t,
        normed_out, normed_in, og_out, og_in, ng_out, ng_in, mix_out, mix_in,
        swap_send, swap_recv,
        q_s, k_s, v_s, d_s, bias, mixed_s, qp_s, kp_s, vp_s, parts, flip,
        resid_grad, grad_pad, gain_acc, conv_terms, small_terms,
    ), refs = refs[:44], refs[44:]
    frames = lax.axis_size("frame")
    rows_n = lax.axis_size("row")
    chunk = HALF // frames
    me, row = lax.axis_index("frame"), lax.axis_index("row")
    place = my_place()
    peers = []
    for step in range(1, frames):
        frame = lax.rem(me + step, frames)
        peers.append((frame, (frame, row)))
    above = (me, lax.rem(row + rows_n - 1, rows_n))
    below = (me, lax.rem(row + 1, rows_n))

    barrier = pltpu.get_barrier_semaphore()
    partners = [device for _, device in peers] + [above, below]
    for axis in "cxy":
        partners += [along(place, axis, step, sizes) for step in range(1, sizes[axis])]
    for device in partners:
        pl.semaphore_signal(barrier, inc=1, device_id=device, device_id_type=MESH)

    loads = []
    pairs = (
        (latents, lat_in), (out_grad, grad_in), (conv_w, weights), (gain, gain_v),
        (out_w, wo), (query_w, wq), (key_w, wk), (value_w, wv),
    )
    for at, (source, target) in enumerate(pairs):
        loads.append(pltpu.make_async_copy(source, target, in_sems.at[at]))
        loads[-1].start()

    loads[0].wait()

    def activate(at, carry):
        span = pl.ds(at * COLS, COLS)
        cells = lat_in[at].astype(F32).T
        lat[span] = cells.astype(BF16)
        act = (cells * jax.nn.sigmoid(cells)).astype(BF16).astype(F32)
        for shift, copy in enumerate(shifts(act)):
            padded[shift, pl.ds((at + 1) * COLS, COLS)] = copy.astype(BF16)
        return carry

    lax.fori_loop(0, ROWS, activate, 0)
    pl.semaphore_wait(barrier, len(partners))

    def halo_start(source, kind):
        return [
            remote(source.at[pl.ds(COLS, COLS)], halo.at[kind, 1],
                   halo_send.at[kind, 0], halo_recv.at[kind, 0], above),
            remote(source.at[pl.ds(ROWS * COLS, COLS)], halo.at[kind, 0],
                   halo_send.at[kind, 1], halo_recv.at[kind, 1], below),
        ]

    def halo_end(copies, kind, target):
        for copy in copies:
            copy.wait_recv()
        ends = (row > 0, row < rows_n - 1)
        for side, inside in enumerate(ends):
            keep = jnp.where(inside, 1.0, 0.0).astype(F32)
            cells = halo[kind, side].astype(F32) * keep
            for shift, copy in enumerate(shifts(cells)):
                target[shift, pl.ds(side * (ROWS + 1) * COLS, COLS)] = copy.astype(BF16)

    act_halo = halo_start(padded.at[1], 0)

    swaps = []
    buffers = ((og_out, og_in), (normed_out, normed_in), (ng_out, ng_in), (mix_out, mix_in))
    for at, (source, target) in enumerate(buffers):
        swaps.append(Swap(source, target, swap_send.at[at], swap_recv.at[at], peers, me))
    og_swap, normed_swap, ng_swap, mix_swap = swaps

    loads[1].wait()

    def flip_grad(at, carry):
        grad[pl.ds(at * COLS, COLS)] = grad_in[at].astype(F32).T.astype(BF16)
        return carry

    lax.fori_loop(0, ROWS, flip_grad, 0)
    og_out[0] = grad[COLS : COLS + HALF].reshape(frames, chunk, CHAN)
    og_out[1, : frames // 2] = grad[:COLS].reshape(frames // 2, chunk, CHAN)
    og_out[1, frames // 2 :] = grad[COLS + HALF :].reshape(frames // 2, chunk, CHAN)
    og_swap.start(0)
    og_swap.start(1)
    loads[2].wait()
    loads[3].wait()

    def conv_half(half):
        acc[pl.ds(0, HALF)] = jnp.zeros((HALF, CHAN), F32)

        def tap(at, carry):
            a, b = at // 3, lax.rem(at, 3)
            if half == 0:
                cells = padded[b, pl.ds((a + 1) * COLS, HALF)]
            else:
                cells = jnp.concatenate(
                    [padded[b, pl.ds(a * COLS, COLS)], padded[b, pl.ds((a + 3) * COLS, COLS)]]
                )
            acc[pl.ds(0, HALF)] += dot(cells, weights[at])
            return carry

        lax.fori_loop(0, 9, tap, 0)
        count = 64 // chunk

        def finish(at, carry):
            cells = lat[pl.ds(pl.multiple_of(cell_start(half, at), 64), 64)].astype(F32)
            held = (cells + acc[pl.ds(at * 64, 64)]).astype(BF16)
            resid[half, pl.ds(at * 64, 64)] = held
            held = held.astype(F32)
            normed = (held * norm_of(held) * gain_v[...].reshape(1, CHAN)).astype(BF16)
            normed_out[half, pl.ds(at * count, count)] = normed.reshape(count, chunk, CHAN)
            return carry

        lax.fori_loop(0, 4, finish, 0)

    conv_half(0)
    normed_swap.start(0)
    halo_end(act_halo, 0, padded)
    conv_half(1)
    normed_swap.start(1)

    position = lax.broadcasted_iota(jnp.int32, (HALF, HALF), 0)
    other = lax.broadcasted_iota(jnp.int32, (HALF, HALF), 1)
    same = lax.rem(position, chunk) == lax.rem(other, chunk)
    bias[...] = jnp.where(same, 0.0, -1e30)
    for field in (q_s, k_s, v_s, d_s):
        field[:, 256:] = jnp.zeros((HALF, 128), BF16)
    for shift in range(3):
        act_t[shift] = padded[shift].astype(F32).T.astype(BF16)
    for load in loads[4:]:
        load.wait()

    for half in range(2):
        og_swap.wait(half)
        d_s[:, :CHAN] = dot_nt(og_in[half].reshape(HALF, CHAN), wo[...]).astype(BF16)
        normed_swap.wait(half)
        normed = normed_in[half].reshape(HALF, CHAN)
        q_s[:, :CHAN] = dot(normed, wq[...]).astype(BF16)
        k_s[:, :CHAN] = dot(normed, wk[...]).astype(BF16)
        v_s[:, :CHAN] = dot(normed, wv[...]).astype(BF16)
        attention(q_s, k_s, v_s, d_s, bias, mixed_s, qp_s, kp_s, vp_s)
        back = dot_nt(qp_s[:, :CHAN], wq[...])
        back = back + dot_nt(kp_s[:, :CHAN], wk[...])
        back = back + dot_nt(vp_s[:, :CHAN], wv[...])
        ng_out[half] = back.astype(BF16).reshape(frames, chunk, CHAN)
        ng_swap.start(half)
        mix_out[half] = mixed_s[:, :CHAN].reshape(frames, chunk, CHAN)
        mix_swap.start(half)
        for at, field in enumerate((qp_s, kp_s, vp_s)):
            parts[at, pl.ds(half * HALF, HALF)] = field[:, :CHAN]

    flip[0] = normed_in[...].reshape(2 * HALF, CHAN).astype(F32).T.astype(BF16)
    flip[1] = mix_out[...].reshape(2 * HALF, CHAN).astype(F32).T.astype(BF16)
    for at in range(3):
        pack(dot(flip[0], parts[at]), small_terms, at * MATRIX_TILES)
    pack(dot(flip[1], og_in[...].reshape(2 * HALF, CHAN)), small_terms, 3 * MATRIX_TILES)
    spare = SMALL_TILES - 4 * MATRIX_TILES
    small_terms[pl.ds(4 * MATRIX_TILES, spare)] = jnp.zeros((spare, 16, 128), BF16)

    conv = ConvSummer(place, sizes, conv_terms, conv_total, refs[9:])
    small = Summer("yxz", place, sizes, small_terms, small_total, 0, refs[:9])
    small.core_start()

    gain_acc[...] = jnp.zeros((8, CHAN), F32)
    for half in range(2):
        ng_swap.wait(half)

        def undo_norm(at, carry, half=half):
            count = 64 // chunk
            begin = pl.multiple_of(cell_start(half, at), 64)
            held = resid[half, pl.ds(at * 64, 64)].astype(F32)
            back = ng_in[half, pl.ds(at * count, count)].reshape(64, CHAN).astype(F32)
            inv = norm_of(held)
            product = back * held
            total = jnp.sum((product * inv).reshape(8, 8, CHAN), axis=0)
            gain_acc[...] += total
            tangent = back * gain_v[...].reshape(1, CHAN)
            mean = jnp.mean(product * gain_v[...].reshape(1, CHAN), axis=-1, keepdims=True)
            value = grad[pl.ds(begin, 64)].astype(F32) + (
                inv * tangent - held * (inv * inv * inv) * mean
            )
            resid_grad[pl.ds(begin, 64)] = value.astype(BF16)
            return carry

        lax.fori_loop(0, 4, undo_norm, 0)
    small.core_end()
    small.scatter_start(0)

    def pad_grad(at, carry):
        cells = resid_grad[pl.ds(at * COLS, COLS)].astype(F32)
        for shift, copy in enumerate(shifts(cells)):
            grad_pad[shift, pl.ds((at + 1) * COLS, COLS)] = copy.astype(BF16)
        return carry

    lax.fori_loop(0, ROWS, pad_grad, 0)
    grad_halo = halo_start(grad_pad.at[1], 1)

    span = 2 * (PART // 8)
    spare = CONV_TILES - GAIN_TILE
    conv_terms[pl.ds(GAIN_TILE, spare)] = jnp.zeros((spare, 16, 128), BF16)
    gains = jnp.sum(gain_acc[...], axis=0, keepdims=True)
    line = lax.broadcasted_iota(jnp.int32, (16, 128), 0)
    gain_tile = jnp.where(line == 0, gains[:, :128], jnp.where(line == 1, gains[:, 128:256], 0.0))
    conv_terms[GAIN_TILE] = gain_tile.astype(BF16)
    tail = jnp.where(line[:, :64] == 0, gains[:, 256:], 0.0)
    conv_terms[GAIN_TILE + 1, :, :64] = tail.astype(BF16)

    def conv_tap(at, carry):
        a, b = at // 3, lax.rem(at, 3)
        cells = act_t[b, :, pl.ds(pl.multiple_of(a * COLS, COLS), ROWS * COLS)]
        pack(dot(cells, resid_grad[...]), conv_terms, at * MATRIX_TILES)
        done = ((at + 1) * MATRIX_TILES) // span

        @pl.when(done > (at * MATRIX_TILES) // span)
        def _():
            conv.core_start(done - 1)

        return carry

    lax.fori_loop(0, 9, conv_tap, 0)
    conv.core_start(7)
    conv.scatter_first()
    small.scatter_end(0)
    small.scatter_start(1)
    for half in range(2):
        mix_swap.wait(half)
        acc[pl.ds(0, HALF)] = dot(mix_in[half].reshape(HALF, CHAN), wo[...])

        def write_out(at, carry, half=half):
            held = resid[half, pl.ds(at * COLS, COLS)].astype(F32)
            total = held + acc[pl.ds(at * COLS, COLS)]
            row_at = at + 1 if half == 0 else at * 3
            block_out[row_at] = total.T.astype(BF16)
            return carry

        lax.fori_loop(0, 2, write_out, 0)
    halo_end(grad_halo, 1, grad_pad)
    acc[...] = jnp.zeros((2 * HALF, CHAN), F32)

    def back_tap(at, carry):
        a, b = at // 3, lax.rem(at, 3)
        cells = grad_pad[2 - b, pl.ds((2 - a) * COLS, ROWS * COLS)]
        acc[...] += dot_nt(cells, weights[at])
        return carry

    conv.scatter_second()
    small.scatter_end(1)
    small.scatter_start(2)
    lax.fori_loop(0, 3, back_tap, 0)
    conv.scatter_third()
    lax.fori_loop(3, 7, back_tap, 0)
    conv.gather_third()
    small.scatter_end(2)
    small.gather_start(2)
    lax.fori_loop(7, 9, back_tap, 0)
    def write_back(at, carry):
        cells = lat[pl.ds(at * COLS, COLS)].astype(F32)
        sigma = jax.nn.sigmoid(cells)
        slope = sigma * (1.0 + cells * (1.0 - sigma))
        value = resid_grad[pl.ds(at * COLS, COLS)].astype(F32) + acc[pl.ds(at * COLS, COLS)] * slope
        latents_grad[at] = value.T.astype(BF16)
        return carry

    lax.fori_loop(0, ROWS, write_back, 0)
    small.arrive()
    small.gather_start(1)
    conv.gather_rest()
    small.arrive()
    small.gather_start(0)
    small.arrive()
    small.core_back()
    small.arrive()
    small.finish()
    conv.finish()
    for swap in swaps:
        swap.finish()
    for copy in act_halo + grad_halo:
        copy.wait_send()


def block_scratch(sizes, frames):
    chunk = HALF // frames
    field = (2, frames, chunk, CHAN)
    vmem = pltpu.VMEM
    dma = pltpu.SemaphoreType.DMA
    weight = vmem((CHAN, CHAN), BF16)
    shapes = [
        vmem((ROWS, CHAN, COLS), BF16), vmem((ROWS, CHAN, COLS), BF16),
        vmem((ROWS * COLS, CHAN), BF16), vmem((ROWS * COLS, CHAN), BF16),
        vmem((9, CHAN, CHAN), BF16), weight, weight, weight, weight, vmem((CHAN,), F32), dma((8,)),
        vmem((3, (ROWS + 2) * COLS, CHAN), BF16), vmem((2, 2, COLS, CHAN), BF16),
        dma((2, 2)), dma((2, 2)), vmem((2 * HALF, CHAN), F32), vmem((2, HALF, CHAN), BF16),
        vmem((3, CHAN, (ROWS + 2) * COLS), BF16),
    ]
    shapes += [vmem(field, BF16)] * 8 + [dma((4, 2)), dma((4, 2))]
    shapes += [vmem((HALF, WIDE), BF16)] * 4 + [vmem((HALF, HALF), F32)]
    shapes += [vmem((HALF, WIDE), BF16)] * 4
    shapes += [vmem((3, 2 * HALF, CHAN), BF16), vmem((2, CHAN, 2 * HALF), BF16)]
    shapes += [vmem((ROWS * COLS, CHAN), BF16), vmem((3, (ROWS + 2) * COLS, CHAN), BF16)]
    shapes += [vmem((8, CHAN), F32)]
    shapes += [vmem((CONV_TILES, 16, 128), BF16), vmem((SMALL_TILES, 16, 128), BF16)]
    return shapes + summer_scratch("yxz", sizes) + conv_summer_scratch(sizes)


def on_device(
    latents, conv_weight, query_weight, key_weight, value_weight, out_weight, norm_gain, out_grad
):
    sizes = chip_sizes()
    frames = lax.axis_size("frame")
    anywhere = pl.BlockSpec(memory_space=pl.ANY)
    inside = pl.BlockSpec(memory_space=pltpu.VMEM)
    field = jax.ShapeDtypeStruct((ROWS, CHAN, COLS), BF16)
    block_out, latents_grad, conv_sum, small_sum = pl.pallas_call(
        functools.partial(block_kernel, sizes),
        out_shape=[
            field,
            field,
            jax.ShapeDtypeStruct((CONV_TILES, 16, 128), BF16),
            jax.ShapeDtypeStruct((SMALL_TILES, 16, 128), BF16),
        ],
        in_specs=[anywhere] * 8,
        out_specs=[inside] * 4,
        scratch_shapes=block_scratch(sizes, frames),
        compiler_params=pltpu.CompilerParams(
            collective_id=0, has_side_effects=True, vmem_limit_bytes=56 << 20
        ),
    )(
        jnp.swapaxes(latents[0], 1, 2),
        conv_weight.reshape(9, CHAN, CHAN),
        query_weight,
        key_weight,
        value_weight,
        out_weight,
        norm_gain,
        jnp.swapaxes(out_grad[0], 1, 2),
    )
    factor = (ROWS * COLS * frames * lax.axis_size("row")) ** (-0.5)
    weight = jax.ShapeDtypeStruct((CHAN, CHAN), F32)
    outs = pl.pallas_call(
        functools.partial(finish_kernel, factor),
        out_shape=[
            field,
            field,
            jax.ShapeDtypeStruct((9, CHAN, CHAN), F32),
            weight,
            weight,
            weight,
            weight,
            jax.ShapeDtypeStruct((CHAN,), F32),
        ],
        in_specs=[anywhere] * 4,
        out_specs=[anywhere] * 7 + [inside],
        scratch_shapes=[
            pltpu.VMEM((CONV_TILES, 16, 128), BF16),
            pltpu.VMEM((SMALL_TILES, 16, 128), BF16),
            pltpu.VMEM((13, CHAN, CHAN), F32),
            pltpu.VMEM((2, ROWS, CHAN, COLS), BF16),
            pltpu.SemaphoreType.DMA((4,)),
            pltpu.SemaphoreType.DMA((14,)),
            pltpu.SemaphoreType.DMA((13,)),
        ],
        compiler_params=pltpu.CompilerParams(vmem_limit_bytes=56 << 20),
    )(block_out, latents_grad, conv_sum, small_sum)
    return (
        jnp.swapaxes(outs[0], 1, 2)[None],
        jnp.swapaxes(outs[1], 1, 2)[None],
        outs[2].reshape(3, 3, CHAN, CHAN),
        *outs[3:7],
        outs[7],
    )


def solution(mesh):
    split = P("frame", "row", None, None)
    return jax.shard_map(
        on_device,
        mesh=mesh,
        in_specs=(split, P(), P(), P(), P(), P(), P(), split),
        out_specs=(split, split, P(), P(), P(), P(), P(), P()),
        check_vma=False,
    )
```

```python
import functools

import jax
import jax.numpy as jnp
from jax import lax
from jax.experimental import pallas as pl
from jax.experimental.pallas import tpu as pltpu
from jax.sharding import PartitionSpec as P

EPS = 1e-06
MESH = pl.DeviceIdType.MESH
CHAN = 320
WIDE = 384
COLS = 128
ROWS = 4
HALF = 256
CONV_TILES = 512
SMALL_TILES = 256
PART = 256
MATRIX_TILES = 50
GAIN_TILE = 230
HALF_CHAN = 160
HALF_TILES = 25
BLOCK = 16
F32 = jnp.float32
BF16 = jnp.bfloat16


def chip_sizes():
    return {"c": 2, "x": 4, "y": lax.axis_size("row") // 4, "z": lax.axis_size("frame") // 2}


def my_place():
    frame, row = lax.axis_index("frame"), lax.axis_index("row")
    return {
        "z": frame // 2,
        "x": lax.rem(row // 2, 2) * 2 + lax.rem(frame, 2),
        "y": row // 4,
        "c": lax.rem(row, 2),
    }


def device_of(place):
    return (
        place["z"] * 2 + lax.rem(place["x"], 2),
        (place["y"] * 2 + place["x"] // 2) * 2 + place["c"],
    )


def along(place, axis, step, sizes):
    moved = dict(place)
    moved[axis] = lax.rem(place[axis] + step, sizes[axis])
    return device_of(moved)


def remote(source, target, send_sem, recv_sem, device):
    copy = pltpu.make_async_remote_copy(
        src_ref=source,
        dst_ref=target,
        send_sem=send_sem,
        recv_sem=recv_sem,
        device_id=device,
        device_id_type=MESH,
    )
    copy.start()
    return copy


def dot(left, right):
    return jnp.dot(left, right, preferred_element_type=F32)


def dot_nt(left, right):
    return lax.dot_general(left, right, (((1,), (1,)), ((), ())), preferred_element_type=F32)


def dot_tn(left, right):
    return lax.dot_general(left, right, (((0,), (0,)), ((), ())), preferred_element_type=F32)


def add_up(target, start, own, own_start, received):
    count = received[0].shape[0]
    step = min(count, BLOCK)

    def body(at, carry):
        at = at * step
        total = own[pl.ds(own_start + at, step)].astype(F32)
        for part in received:
            total = total + part[pl.ds(at, step)].astype(F32)
        target[pl.ds(start + at, step)] = total.astype(BF16)
        return carry

    lax.fori_loop(0, count // step, body, 0)


def wait_bytes(span, sem):
    pltpu.make_async_copy(span, span, sem).wait()


class ConvSummer:
    ORDERS = ("xy", "yx")

    def __init__(self, place, sizes, terms, total, scratch):
        self.place, self.sizes, self.terms, self.total = place, sizes, terms, total
        (
            self.inbox0, self.held1, self.inbox1, self.held2, self.inbox2,
            self.scatter0, self.scatter1, self.scatter2,
            self.gather2, self.gather1, self.gather0, self.back, self.sends,
        ) = scratch
        self.unit = PART // (2 * sizes["x"] * sizes["y"] * sizes["z"])
        self.group = self.unit * sizes["z"]
        self.n1 = [sizes[order[0]] for order in self.ORDERS]
        self.n2 = [sizes[order[1]] for order in self.ORDERS]

    def at(self, part, axis):
        return self.place[self.ORDERS[part][axis]]

    def peer(self, part, axis, step):
        return lax.rem(self.at(part, axis) + step, self.sizes[self.ORDERS[part][axis]])

    def device(self, axis, step):
        return along(self.place, axis, step, self.sizes)

    def local(self, part, chunk, group, unit=0):
        span = self.n2[part] * self.group
        return part * (PART // 2) + chunk * span + group * self.group + unit * self.unit

    def tile(self, part, chunk, group, unit=0):
        return self.place["c"] * PART + self.local(part, chunk, group, unit)

    def scatter_first(self, part):
        for step2 in range(self.n2[0]):
            step2 = (step2 + 1) % self.n2[0]
            for step in range(1, self.n1[0]):
                chunk, group = self.peer(part, 0, step), self.peer(part, 1, step2)
                remote(
                    self.terms.at[pl.ds(self.local(part, chunk, group), self.group)],
                    self.inbox0.at[part, group, pl.ds((step - 1) * self.group, self.group)],
                    self.sends.at[part],
                    self.scatter0.at[part, step2],
                    self.device(self.ORDERS[part][0], step),
                )

    def scatter_second(self):
        for step2 in range(self.n2[0]):
            step2 = (step2 + 1) % self.n2[0]
            for part in range(2):
                chunk, group = self.at(part, 0), self.peer(part, 1, step2)
                wait_bytes(self.inbox0.at[part, group], self.scatter0.at[part, step2])
                total = self.terms[pl.ds(self.local(part, chunk, group), self.group)].astype(F32)
                for step in range(self.n1[part] - 1):
                    span = pl.ds(step * self.group, self.group)
                    total = total + self.inbox0[part, group, span].astype(F32)
                held = self.held1.at[part, group]
                held[...] = total.astype(BF16)
                if step2 > 0:
                    remote(
                        held,
                        self.inbox1.at[part, pl.ds((step2 - 1) * self.group, self.group)],
                        self.sends.at[2],
                        self.scatter1.at[part],
                        self.device(self.ORDERS[part][1], step2),
                    )

    def scatter_third(self):
        for part in range(2):
            wait_bytes(self.inbox1.at[part], self.scatter1.at[part])
            total = self.held1[part, self.at(part, 1)].astype(F32)
            for step in range(self.n2[part] - 1):
                total = total + self.inbox1[part, pl.ds(step * self.group, self.group)].astype(F32)
            self.held2[part] = total.astype(BF16)
            for step in range(1, self.sizes["z"]):
                peer = lax.rem(self.place["z"] + step, self.sizes["z"])
                remote(
                    self.held2.at[part, pl.ds(peer * self.unit, self.unit)],
                    self.inbox2.at[part, pl.ds((step - 1) * self.unit, self.unit)],
                    self.sends.at[3],
                    self.scatter2.at[part],
                    self.device("z", step),
                )

    def gather_third(self):
        for part in range(2):
            wait_bytes(self.inbox2.at[part], self.scatter2.at[part])
            z = self.place["z"]
            total = self.held2[part, pl.ds(z * self.unit, self.unit)].astype(F32)
            for step in range(self.sizes["z"] - 1):
                total = total + self.inbox2[part, pl.ds(step * self.unit, self.unit)].astype(F32)
            mine = self.tile(part, self.at(part, 0), self.at(part, 1), z)
            self.total[pl.ds(mine, self.unit)] = total.astype(BF16)
            span = self.total.at[pl.ds(mine, self.unit)]
            for step in range(1, self.sizes["z"]):
                remote(
                    span, span, self.sends.at[4], self.gather2.at[part], self.device("z", step)
                )

    def spread(self, part, chunk, group, axis, steps, send, sem):
        span = self.total.at[pl.ds(self.tile(part, chunk, group), self.group)]
        for step in steps:
            remote(span, span, self.sends.at[send], sem, self.device(axis, step))

    def gather_rest(self, between):
        n1, n2 = self.n1[0], self.n2[0]
        for part in range(2):
            wait_bytes(
                self.total.at[pl.ds(0, (self.sizes["z"] - 1) * self.unit)], self.gather2.at[part]
            )
            first, second = self.ORDERS[part]
            chunk, group = self.at(part, 0), self.at(part, 1)
            for step in range(1, n2):
                sem = self.gather1.at[part, step]
                self.spread(part, chunk, group, second, [step], 5, sem)
            self.spread(part, chunk, group, first, range(1, n1), 6, self.gather0.at[part, 0])
            self.spread(part, chunk, group, "c", [1], 7, self.back.at[0])
        for step2 in range(1, n2):
            for part in range(2):
                first = self.ORDERS[part][0]
                chunk = self.at(part, 0)
                group = self.peer(part, 1, n2 - step2)
                wait_bytes(self.total.at[pl.ds(0, self.group)], self.gather1.at[part, step2])
                self.spread(
                    part, chunk, group, first, range(1, n1), 6, self.gather0.at[part, step2]
                )
                self.spread(part, chunk, group, "c", [1], 7, self.back.at[0])
        between()
        for step2 in range(n2):
            for part in range(2):
                wait_bytes(
                    self.total.at[pl.ds(0, (n1 - 1) * self.group)], self.gather0.at[part, step2]
                )
                group = self.peer(part, 1, n2 - step2)
                for step in range(1, n1):
                    chunk = self.peer(part, 0, n1 - step)
                    self.spread(part, chunk, group, "c", [1], 7, self.back.at[0])

    def finish(self):
        wait_bytes(self.total.at[pl.ds(0, PART)], self.back.at[0])
        n1, n2, nz = self.n1[0], self.n2[0], self.sizes["z"]
        counts = (
            n2 * (n1 - 1) * self.group, n2 * (n1 - 1) * self.group, 2 * (n2 - 1) * self.group,
            2 * (nz - 1) * self.unit, 2 * (nz - 1) * self.unit, 2 * (n2 - 1) * self.group,
            2 * n2 * (n1 - 1) * self.group, PART,
        )
        for at, count in enumerate(counts):
            wait_bytes(self.total.at[pl.ds(0, count)], self.sends.at[at])


def conv_summer_scratch(sizes):
    unit = PART // (2 * sizes["x"] * sizes["y"] * sizes["z"])
    group = unit * sizes["z"]
    n1, n2 = sizes["x"], sizes["y"]
    tiles = [
        (2, n2, (n1 - 1) * group), (2, n2, group), (2, (n2 - 1) * group),
        (2, group), (2, (sizes["z"] - 1) * unit),
    ]
    sems = [(2, n2), (2,), (2,), (2,), (2, n2), (2, n2), (1,), (8,)]
    return [pltpu.VMEM(shape + (16, 128), BF16) for shape in tiles] + [
        pltpu.SemaphoreType.DMA(shape) for shape in sems
    ]


class Summer:
    def __init__(self, order, place, sizes, term, total, base, scratch):
        self.order, self.place, self.sizes = order, place, sizes
        self.term, self.total, self.base = term, total, base
        self.core_in, self.held, self.inbox = scratch[0], scratch[1:4], scratch[4:7]
        self.send_sems, self.recv_sems = scratch[7], scratch[8]
        self.spans = [PART // 2]
        for axis in order:
            self.spans.append(self.spans[-1] // sizes[axis])
        self.slot = 0
        self.sent = []
        self.wait = []

    def push(self, source, target, axis, step):
        device = along(self.place, axis, step, self.sizes)
        copy = remote(
            source, target, self.send_sems.at[self.slot], self.recv_sems.at[self.slot], device
        )
        self.slot += 1
        self.sent.append(copy)
        self.wait.append(copy)

    def arrive(self):
        for copy in self.wait:
            copy.wait_recv()
        self.wait = []

    def core_start(self):
        other = self.base + (1 - self.place["c"]) * self.spans[0]
        self.push(self.term.at[pl.ds(other, self.spans[0])], self.core_in, "c", 1)

    def core_end(self):
        self.arrive()
        mine = self.base + self.place["c"] * self.spans[0]
        add_up(self.held[0], 0, self.term, mine, [self.core_in])

    def scatter_start(self, level):
        axis, span = self.order[level], self.spans[level + 1]
        for step in range(1, self.sizes[axis]):
            peer = lax.rem(self.place[axis] + step, self.sizes[axis])
            self.push(
                self.held[level].at[pl.ds(peer * span, span)],
                self.inbox[level].at[step - 1],
                axis,
                step,
            )

    def scatter_end(self, level):
        self.arrive()
        axis, span = self.order[level], self.spans[level + 1]
        received = [self.inbox[level].at[step] for step in range(self.sizes[axis] - 1)]
        mine = self.place[axis] * span
        if level < 2:
            add_up(self.held[level + 1], 0, self.held[level], mine, received)
        else:
            add_up(self.total, self.start_of(3), self.held[level], mine, received)

    def start_of(self, levels):
        start = self.base + self.place["c"] * self.spans[0]
        for level in range(levels):
            start = start + self.place[self.order[level]] * self.spans[level + 1]
        return start

    def gather_start(self, level):
        axis = self.order[level]
        mine = self.total.at[pl.ds(self.start_of(level + 1), self.spans[level + 1])]
        for step in range(1, self.sizes[axis]):
            self.push(mine, mine, axis, step)

    def core_back(self):
        mine = self.total.at[pl.ds(self.start_of(0), self.spans[0])]
        self.push(mine, mine, "c", 1)

    def finish(self):
        for copy in self.sent:
            copy.wait_send()


def summer_scratch(order, sizes):
    spans = [PART // 2]
    for axis in order:
        spans.append(spans[-1] // sizes[axis])
    shapes = [(spans[0], 16, 128)]
    shapes += [(span, 16, 128) for span in spans[:3]]
    shapes += [(sizes[axis] - 1, span, 16, 128) for axis, span in zip(order, spans[1:])]
    copies = 2 * (1 + sum(sizes[axis] - 1 for axis in order))
    return [pltpu.VMEM(shape, BF16) for shape in shapes] + [
        pltpu.SemaphoreType.DMA((copies,)),
        pltpu.SemaphoreType.DMA((copies,)),
    ]


def pack(matrix, tiles, base):
    held = matrix.astype(BF16)
    for block in range(2):
        cut = held[:, block * 128 : block * 128 + 128]
        tiles[pl.ds(base + 20 * block, 20)] = cut.reshape(20, 16, 128)
    low, high = held[:160, 256:], held[160:, 256:]
    tail = jnp.concatenate([low, high], axis=1)
    tiles[pl.ds(base + 40, 10)] = tail.reshape(10, 16, 128)


def pack_half(matrix, tiles, base):
    held = matrix.astype(BF16)
    for block in range(2):
        cut = held[:, block * 128 : block * 128 + 128]
        tiles[pl.ds(base + 10 * block, 10)] = cut.reshape(10, 16, 128)
    tail = jnp.concatenate([held[:80, 256:], held[80:, 256:]], axis=1)
    tiles[pl.ds(base + 20, 5)] = tail.reshape(5, 16, 128)


def unpack_half(tiles, base, target, at, row, factor):
    span = pl.ds(row, HALF_CHAN)
    for block in range(2):
        cut = tiles[pl.ds(base + 10 * block, 10)].reshape(HALF_CHAN, 128)
        target[at, span, block * 128 : block * 128 + 128] = cut.astype(F32) * factor
    tail = tiles[pl.ds(base + 20, 5)].reshape(80, 128).astype(F32) * factor
    target[at, pl.ds(row, 80), 256:] = tail[:, :64]
    target[at, pl.ds(row + 80, 80), 256:] = tail[:, 64:]


def unpack(tiles, base, target, at, factor):
    for block in range(2):
        cut = tiles[pl.ds(base + 20 * block, 20)].reshape(CHAN, 128)
        target[at, :, block * 128 : block * 128 + 128] = cut.astype(F32) * factor
    tail = tiles[pl.ds(base + 40, 10)].reshape(160, 128).astype(F32) * factor
    target[at, :160, 256:] = tail[:, :64]
    target[at, 160:, 256:] = tail[:, 64:]


def finish_kernel(factor, block_in, back_in, conv_in, small_in, *refs):
    (block_out, back_out, conv_out), small_outs, gain_out = refs[:3], refs[3:7], refs[7]
    conv, small, wide, fields, through, load_sems, store_sems = refs[8:]
    moves = []
    for at, (source, target) in enumerate(((block_in, block_out), (back_in, back_out))):
        moves.append(
            (
                pltpu.make_async_copy(source, fields.at[at], through.at[at]),
                pltpu.make_async_copy(fields.at[at], target, through.at[at + 2]),
            )
        )
        moves[-1][0].start()

    def load(at, source, target):
        span = pl.ds(at * MATRIX_TILES, MATRIX_TILES)
        return source.at[span], target.at[span]

    for at in range(4):
        pltpu.make_async_copy(*load(at, small_in, small), load_sems.at[9 + at]).start()
    conv_load = pltpu.make_async_copy(conv_in, conv, load_sems.at[0])
    conv_load.start()
    for at in range(4):
        pltpu.make_async_copy(*load(at, small_in, small), load_sems.at[9 + at]).wait()
        unpack(small, at * MATRIX_TILES, wide, 9 + at, factor)
        pltpu.make_async_copy(wide.at[9 + at], small_outs[at], store_sems.at[9 + at]).start()

    def conv_tap(at, carry):
        for core in range(2):
            start = core * PART + at * HALF_TILES
            unpack_half(conv, start, wide, at, core * HALF_CHAN, factor)
        pltpu.make_async_copy(wide.at[at], conv_out.at[at], store_sems.at[at]).start()
        return carry

    for move in moves:
        move[0].wait()
        move[1].start()
    conv_load.wait()
    lax.fori_loop(0, 9, conv_tap, 0)
    pieces = []
    for at in range(2):
        tiles = [conv[core * PART + GAIN_TILE + at].astype(F32) for core in range(2)]
        pieces.append((tiles[0] + tiles[1]) * factor)
    gain_out[0:128] = pieces[0][0]
    gain_out[128:256] = pieces[0][1]
    gain_out[256:] = pieces[1][0, :64]
    for move in moves:
        move[1].wait()
    for at in range(9):
        pltpu.make_async_copy(wide.at[at], conv_out.at[at], store_sems.at[at]).wait()
    for at in range(4):
        pltpu.make_async_copy(wide.at[9 + at], small_outs[at], store_sems.at[9 + at]).wait()


def shifts(cells):
    column = lax.broadcasted_iota(jnp.int32, cells.shape, 0)
    left = jnp.where(column == 0, 0.0, pltpu.roll(cells, 1, 0))
    right = jnp.where(column == COLS - 1, 0.0, pltpu.roll(cells, COLS - 1, 0))
    return [left, cells, right]


def store_chunks(target, half, at, cells):
    count = cells.shape[0] // 16
    span = pl.ds(at, count)
    for block in range(2):
        cut = cells[:, block * 128 : block * 128 + 128].reshape(count, 16, 128)
        target[half, span, 16 * block : 16 * block + 16] = cut
    tail = cells[:, 256:].astype(F32).reshape(count, 2, 8, 64)
    low, high = tail[:, 0].reshape(count * 8, 64), tail[:, 1].reshape(count * 8, 64)
    tail = jnp.concatenate([low, high], axis=1).reshape(count, 8, 128)
    target[half, span, 32:40] = tail.astype(BF16)


def load_chunks(source, half, at, count, target):
    span = pl.ds(at, count)
    for block in range(2):
        cut = source[half, span, 16 * block : 16 * block + 16].reshape(16 * count, 128)
        target[:, block * 128 : block * 128 + 128] = cut
    tail = source[half, span, 32:40].astype(F32).reshape(count * 8, 128)
    low = tail[:, :64].reshape(count, 1, 8, 64)
    high = tail[:, 64:].reshape(count, 1, 8, 64)
    tail = jnp.concatenate([low, high], axis=1).reshape(16 * count, 64)
    target[:, 256:] = tail.astype(BF16)


class Swap:
    def __init__(self, source, target, send_sems, recv_sems, peers, me):
        self.source, self.target, self.peers, self.me = source, target, peers, me
        self.send_sems, self.recv_sems = send_sems, recv_sems

    def start(self, half):
        for frame, device in self.peers:
            remote(
                self.source.at[half, frame],
                self.target.at[half, self.me],
                self.send_sems.at[half],
                self.recv_sems.at[half],
                device,
            )
        self.target[half, self.me] = self.source[half, self.me]

    def wait(self, half):
        span = self.target.at[half, pl.ds(0, len(self.peers))]
        pltpu.make_async_copy(span, span, self.recv_sems.at[half]).wait()

    def finish(self):
        for half in range(2):
            span = self.source.at[half, pl.ds(0, len(self.peers))]
            pltpu.make_async_copy(span, span, self.send_sems.at[half]).wait()


def norm_of(resid):
    return lax.rsqrt(jnp.mean(resid * resid, axis=-1, keepdims=True) + EPS)


def cell_start(half, at):
    if half == 0:
        return COLS + at * 64
    return jnp.where(at < 2, at * 64, HALF + at * 64)


def head_masks():
    low = lax.broadcasted_iota(jnp.int32, (1, 128), 1) < 64
    return low, [jnp.where(low, 1.0, 0.0).astype(BF16), jnp.where(low, 0.0, 1.0).astype(BF16)]


def attend(q_s, k_s, v_s, bias, probs_s, mixed_s):
    low, masks = head_masks()

    def tile(at, carry):
        span = pl.ds(pl.multiple_of(at * 128, 128), 128)
        queries, keys, values = q_s[:, span], k_s[:, span], v_s[:, span]
        found = []
        for head, mask in enumerate(masks):
            scores = dot_nt(queries * mask, keys) * 0.125 + bias[...]
            expo = jnp.exp(scores)
            probs = expo * (1.0 / jnp.sum(expo, axis=-1, keepdims=True))
            probs_s[2 * at + head] = probs
            found.append(dot(probs.astype(BF16), values))
        mixed_s[:, span] = jnp.where(low, *found).astype(BF16)
        return carry

    lax.fori_loop(0, 3, tile, 0)


def attend_back(q_s, k_s, v_s, d_s, probs_s, qp_s, kp_s, vp_s):
    low, masks = head_masks()

    def tile(at, carry):
        span = pl.ds(pl.multiple_of(at * 128, 128), 128)
        queries, keys, values, grads = q_s[:, span], k_s[:, span], v_s[:, span], d_s[:, span]
        found = []
        for head, mask in enumerate(masks):
            probs = probs_s[2 * at + head]
            prob_grad = dot_nt(grads * mask, values)
            inner = jnp.sum(probs * prob_grad, axis=-1, keepdims=True)
            score_b = (probs * (prob_grad - inner) * 0.125).astype(BF16)
            found.append(
                (
                    dot(score_b, keys),
                    dot_tn(score_b, queries),
                    dot_tn(probs.astype(BF16), grads),
                )
            )
        for target, first, second in zip((qp_s, kp_s, vp_s), *found):
            target[:, span] = jnp.where(low, first, second).astype(BF16)
        return carry

    lax.fori_loop(0, 3, tile, 0)


def block_kernel(sizes, latents, conv_w, query_w, key_w, value_w, out_w, gain, out_grad, *refs):
    (block_out, latents_grad, conv_total, small_total), refs = refs[:4], refs[4:]
    (
        lat_in, grad_in, lat, grad, weights, wq, wk, wv, wo, gain_v, in_sems,
        padded, halo, halo_send, halo_recv, acc, resid, act_c, act_in, act_t,
        normed_out, normed_in, og_out, og_in, ng_out, ng_in, mix_out, mix_in,
        swap_send, swap_recv,
        og_n, normed_n, mixed_n, back_n,
        q_s, k_s, v_s, d_s, bias, probs_s, out_acc, mixed_s, qp_s, kp_s, vp_s, parts, flip,
        resid_grad, rg_in, conv_acc, pair_send, pair_recv, grad_pad, gain_acc, conv_terms, small_terms,
    ), refs = refs[:56], refs[56:]
    frames = lax.axis_size("frame")
    rows_n = lax.axis_size("row")
    chunk = HALF // frames
    me, row = lax.axis_index("frame"), lax.axis_index("row")
    place = my_place()
    peers = []
    for step in range(1, frames):
        frame = lax.rem(me + step, frames)
        peers.append((frame, (frame, row)))
    above = (me, lax.rem(row + rows_n - 1, rows_n))
    below = (me, lax.rem(row + 1, rows_n))

    barrier = pltpu.get_barrier_semaphore()
    partners = [device for _, device in peers] + [above, below]
    for axis in "cxy":
        partners += [along(place, axis, step, sizes) for step in range(1, sizes[axis])]
    for device in partners:
        pl.semaphore_signal(barrier, inc=1, device_id=device, device_id_type=MESH)

    loads = []
    pairs = (
        (latents, lat_in), (out_grad, grad_in), (conv_w, weights), (gain, gain_v),
        (out_w, wo), (query_w, wq), (key_w, wk), (value_w, wv),
    )
    for at, (source, target) in enumerate(pairs):
        loads.append(pltpu.make_async_copy(source, target, in_sems.at[at]))
        loads[-1].start()

    loads[0].wait()

    def activate(at, carry):
        span = pl.ds(at * COLS, COLS)
        cells = lat_in[at].astype(F32).T
        lat[span] = cells.astype(BF16)
        act = (cells * jax.nn.sigmoid(cells)).astype(BF16).astype(F32)
        for shift, copy in enumerate(shifts(act)):
            padded[shift, pl.ds((at + 1) * COLS, COLS)] = copy.astype(BF16)
        return carry

    lax.fori_loop(0, ROWS, activate, 0)
    loads[1].wait()

    def flip_grad(at, carry):
        cells = grad_in[at].astype(F32).T.astype(BF16)
        grad[pl.ds(at * COLS, COLS)] = cells
        half = jnp.where((at == 0) | (at == ROWS - 1), 1, 0)
        store_chunks(og_out, half, jnp.where(at >= 2, 8, 0), cells)
        return carry

    lax.fori_loop(0, ROWS, flip_grad, 0)
    pl.semaphore_wait(barrier, len(partners))

    def halo_start(source, kind):
        return [
            remote(source.at[pl.ds(COLS, COLS)], halo.at[kind, 1],
                   halo_send.at[kind, 0], halo_recv.at[kind, 0], above),
            remote(source.at[pl.ds(ROWS * COLS, COLS)], halo.at[kind, 0],
                   halo_send.at[kind, 1], halo_recv.at[kind, 1], below),
        ]

    def halo_end(copies, kind, target):
        for copy in copies:
            copy.wait_recv()
        ends = (row > 0, row < rows_n - 1)
        for side, inside in enumerate(ends):
            keep = jnp.where(inside, 1.0, 0.0).astype(F32)
            cells = halo[kind, side].astype(F32) * keep
            for shift, copy in enumerate(shifts(cells)):
                target[shift, pl.ds(side * (ROWS + 1) * COLS, COLS)] = copy.astype(BF16)

    act_halo = halo_start(padded.at[1], 0)

    swaps = []
    buffers = ((og_out, og_in), (normed_out, normed_in), (ng_out, ng_in), (mix_out, mix_in))
    for at, (source, target) in enumerate(buffers):
        swaps.append(Swap(source, target, swap_send.at[at], swap_recv.at[at], peers, me))
    og_swap, normed_swap, ng_swap, mix_swap = swaps

    loads[2].wait()
    loads[3].wait()

    def conv_half(half):
        acc[pl.ds(0, HALF)] = jnp.zeros((HALF, CHAN), F32)

        def tap(at, carry):
            a, b = at // 3, lax.rem(at, 3)
            if half == 0:
                cells = padded[b, pl.ds((a + 1) * COLS, HALF)]
            else:
                cells = jnp.concatenate(
                    [padded[b, pl.ds(a * COLS, COLS)], padded[b, pl.ds((a + 3) * COLS, COLS)]]
                )
            acc[pl.ds(0, HALF)] += dot(cells, weights[at])
            return carry

        lax.fori_loop(0, 9, tap, 0)
        count = 64 // chunk

        def finish(at, carry):
            cells = lat[pl.ds(pl.multiple_of(cell_start(half, at), 64), 64)].astype(F32)
            held = (cells + acc[pl.ds(at * 64, 64)]).astype(BF16)
            resid[half, pl.ds(at * 64, 64)] = held
            held = held.astype(F32)
            normed = (held * norm_of(held) * gain_v[...].reshape(1, CHAN)).astype(BF16)
            store_chunks(normed_out, half, at * count, normed)
            return carry

        lax.fori_loop(0, 4, finish, 0)

    og_swap.start(0)
    conv_half(0)
    normed_swap.start(0)
    halo_end(act_halo, 0, padded)
    conv_half(1)
    normed_swap.start(1)
    og_swap.start(1)

    position = lax.broadcasted_iota(jnp.int32, (HALF, HALF), 0)
    other = lax.broadcasted_iota(jnp.int32, (HALF, HALF), 1)
    same = lax.rem(position, chunk) == lax.rem(other, chunk)
    bias[...] = jnp.where(same, 0.0, -1e30)
    for field in (q_s, k_s, v_s, d_s):
        field[:, 256:] = jnp.zeros((HALF, 128), BF16)
    act_c[...] = padded[1].astype(F32).T.astype(BF16)
    core = place["c"]
    partner = along(place, "c", 1, sizes)
    mine = pl.ds(pl.multiple_of(core * HALF_CHAN, HALF_CHAN), HALF_CHAN)
    theirs = pl.ds(pl.multiple_of((1 - core) * HALF_CHAN, HALF_CHAN), HALF_CHAN)
    pair = [remote(act_c.at[theirs], act_in, pair_send.at[0], pair_recv.at[0], partner)]

    def shift_lanes(at, carry, source, side):
        span = pl.ds(pl.multiple_of(at * COLS, COLS), COLS)
        cells = source[:, span].astype(F32)
        column = lax.broadcasted_iota(jnp.int32, cells.shape, 1)
        left = jnp.where(column == 0, 0.0, pltpu.roll(cells, 1, 1))
        right = jnp.where(column == COLS - 1, 0.0, pltpu.roll(cells, COLS - 1, 1))
        for shift, copy in enumerate((left, cells, right)):
            act_t[side, shift, :, span] = copy.astype(BF16)
        return carry

    own_rows = functools.partial(shift_lanes, source=act_c.at[mine], side=0)
    lax.fori_loop(0, ROWS + 2, own_rows, 0)
    for load in loads[4:]:
        load.wait()

    for half in range(2):
        normed_swap.wait(half)
        load_chunks(normed_in, half, 0, frames, normed_n.at[half])
        q_s[:, :CHAN] = dot(normed_n[half], wq[...]).astype(BF16)
        k_s[:, :CHAN] = dot(normed_n[half], wk[...]).astype(BF16)
        v_s[:, :CHAN] = dot(normed_n[half], wv[...]).astype(BF16)
        attend(q_s, k_s, v_s, bias, probs_s, mixed_s)
        mixed_n[half] = mixed_s[:, :CHAN]
        store_chunks(mix_out, half, 0, mixed_s[:, :CHAN])
        og_swap.wait(half)
        load_chunks(og_in, half, 0, frames, og_n.at[half])
        d_s[:, :CHAN] = dot_nt(og_n[half], wo[...]).astype(BF16)
        attend_back(q_s, k_s, v_s, d_s, probs_s, qp_s, kp_s, vp_s)
        back = dot_nt(qp_s[:, :CHAN], wq[...])
        back = back + dot_nt(kp_s[:, :CHAN], wk[...])
        back = back + dot_nt(vp_s[:, :CHAN], wv[...])
        store_chunks(ng_out, half, 0, back.astype(BF16))
        ng_swap.start(half)
        for at, field in enumerate((qp_s, kp_s, vp_s)):
            parts[at, pl.ds(half * HALF, HALF)] = field[:, :CHAN]

    mix_swap.start(0)
    mix_swap.start(1)
    pair[0].wait_recv()
    other_rows = functools.partial(shift_lanes, source=act_in, side=1)
    lax.fori_loop(0, ROWS + 2, other_rows, 0)
    flip[0] = normed_n[...].reshape(2 * HALF, CHAN).astype(F32).T.astype(BF16)
    flip[1] = mixed_n[...].reshape(2 * HALF, CHAN).astype(F32).T.astype(BF16)
    for at in range(3):
        pack(dot(flip[0], parts[at]), small_terms, at * MATRIX_TILES)
    pack(dot(flip[1], og_n[...].reshape(2 * HALF, CHAN)), small_terms, 3 * MATRIX_TILES)
    spare = SMALL_TILES - 4 * MATRIX_TILES
    small_terms[pl.ds(4 * MATRIX_TILES, spare)] = jnp.zeros((spare, 16, 128), BF16)

    conv = ConvSummer(place, sizes, conv_terms, conv_total, refs[9:])
    small = Summer("yxz", place, sizes, small_terms, small_total, 0, refs[:9])
    small.core_start()

    gain_acc[...] = jnp.zeros((8, CHAN), F32)
    for half in range(2):
        ng_swap.wait(half)
        load_chunks(ng_in, half, 0, frames, back_n)

        def undo_norm(at, carry, half=half):
            begin = pl.multiple_of(cell_start(half, at), 64)
            held = resid[half, pl.ds(at * 64, 64)].astype(F32)
            back = back_n[pl.ds(at * 64, 64)].astype(F32)
            inv = norm_of(held)
            product = back * held
            total = jnp.sum((product * inv).reshape(8, 8, CHAN), axis=0)
            gain_acc[...] += total
            tangent = back * gain_v[...].reshape(1, CHAN)
            mean = jnp.mean(product * gain_v[...].reshape(1, CHAN), axis=-1, keepdims=True)
            value = grad[pl.ds(begin, 64)].astype(F32) + (
                inv * tangent - held * (inv * inv * inv) * mean
            )
            resid_grad[half, pl.ds(at * 64, 64)] = value.astype(BF16)
            return carry

        lax.fori_loop(0, 4, undo_norm, 0)
        pair.append(
            remote(
                resid_grad.at[half],
                rg_in.at[half],
                pair_send.at[1 + half],
                pair_recv.at[1 + half],
                partner,
            )
        )
        if half == 0:
            pair[1].wait_recv()

            def first_taps(at, carry):
                a, b = at // 3, lax.rem(at, 3)
                span = pl.ds(pl.multiple_of((a + 1) * COLS, COLS), HALF)
                conv_acc[at] = dot(act_t[0, b, :, span], resid_grad[0]) + dot(
                    act_t[1, b, :, span], rg_in[0]
                )
                return carry

            lax.fori_loop(0, 9, first_taps, 0)
            small.core_end()
            small.scatter_start(0)

    def pad_grad(at, carry):
        half = jnp.where((at == 0) | (at == ROWS - 1), 1, 0)
        side = jnp.where(at >= 2, 1, 0)
        cells = resid_grad[half, pl.ds(side * COLS, COLS)].astype(F32)
        for shift, copy in enumerate(shifts(cells)):
            grad_pad[shift, pl.ds((at + 1) * COLS, COLS)] = copy.astype(BF16)
        return carry

    def edge_cells(side, b, a):
        spans = [pl.ds(pl.multiple_of((a + gap) * COLS, COLS), COLS) for gap in (0, ROWS - 1)]
        return jnp.concatenate([act_t[side, b, :, span] for span in spans], axis=1)

    def second_taps(at, carry):
        a, b = at // 3, lax.rem(at, 3)
        conv_acc[at] += dot(edge_cells(0, b, a), resid_grad[1])
        return carry

    lax.fori_loop(0, 9, second_taps, 0)
    lax.fori_loop(0, ROWS, pad_grad, 0)
    grad_halo = halo_start(grad_pad.at[1], 1)

    spare = PART - 9 * HALF_TILES
    conv_terms[pl.ds(9 * HALF_TILES, spare)] = jnp.zeros((spare, 16, 128), BF16)
    gains = jnp.sum(gain_acc[...], axis=0, keepdims=True)
    line = lax.broadcasted_iota(jnp.int32, (16, 128), 0)
    gain_tile = jnp.where(line == 0, gains[:, :128], jnp.where(line == 1, gains[:, 128:256], 0.0))
    conv_terms[GAIN_TILE] = gain_tile.astype(BF16)
    tail = jnp.where(line[:, :64] == 0, gains[:, 256:], 0.0)
    conv_terms[GAIN_TILE + 1, :, :64] = tail.astype(BF16)
    pair[2].wait_recv()

    def last_taps(at, carry):
        a, b = at // 3, lax.rem(at, 3)
        total = conv_acc[at] + dot(edge_cells(1, b, a), rg_in[1])
        pack_half(total, conv_terms, at * HALF_TILES)
        return carry

    lax.fori_loop(0, 6, last_taps, 0)
    conv.scatter_first(0)
    lax.fori_loop(6, 9, last_taps, 0)
    conv.scatter_first(1)
    small.scatter_end(0)
    small.scatter_start(1)

    def project_out(half):
        mix_swap.wait(half)
        load_chunks(mix_in, half, 0, frames, back_n)
        out_acc[...] = dot(back_n[...], wo[...])

        def write_out(at, carry):
            held = resid[half, pl.ds(at * COLS, COLS)].astype(F32)
            total = held + out_acc[pl.ds(at * COLS, COLS)]
            block_out[at + 1 if half == 0 else at * 3] = total.T.astype(BF16)
            return carry

        lax.fori_loop(0, 2, write_out, 0)

    halo_end(grad_halo, 1, grad_pad)
    acc[...] = jnp.zeros((2 * HALF, CHAN), F32)

    def back_tap(at, carry):
        a, b = at // 3, lax.rem(at, 3)
        cells = grad_pad[2 - b, pl.ds((2 - a) * COLS, ROWS * COLS)]
        acc[...] += dot_nt(cells, weights[at])
        return carry

    lax.fori_loop(0, 5, back_tap, 0)
    small.scatter_end(1)
    small.scatter_start(2)
    conv.scatter_second()
    small.scatter_end(2)
    small.gather_start(2)
    project_out(0)
    project_out(1)
    conv.scatter_third()
    small.arrive()
    small.gather_start(1)
    lax.fori_loop(5, 9, back_tap, 0)
    conv.gather_third()
    small.arrive()
    small.gather_start(0)
    def write_back(at, carry):
        cells = lat[pl.ds(at * COLS, COLS)].astype(F32)
        sigma = jax.nn.sigmoid(cells)
        slope = sigma * (1.0 + cells * (1.0 - sigma))
        half = jnp.where((at == 0) | (at == ROWS - 1), 1, 0)
        side = jnp.where(at >= 2, 1, 0)
        value = resid_grad[half, pl.ds(side * COLS, COLS)].astype(F32) + acc[pl.ds(at * COLS, COLS)] * slope
        latents_grad[at] = value.T.astype(BF16)
        return carry

    lax.fori_loop(0, ROWS, write_back, 0)
    def return_small():
        small.arrive()
        small.core_back()

    conv.gather_rest(return_small)
    small.arrive()
    small.finish()
    conv.finish()
    for swap in swaps:
        swap.finish()
    for copy in act_halo + grad_halo + pair:
        copy.wait_send()


def block_scratch(sizes, frames):
    field = (2, frames, 40, 128)
    vmem = pltpu.VMEM
    dma = pltpu.SemaphoreType.DMA
    weight = vmem((CHAN, CHAN), BF16)
    shapes = [
        vmem((ROWS, CHAN, COLS), BF16), vmem((ROWS, CHAN, COLS), BF16),
        vmem((ROWS * COLS, CHAN), BF16), vmem((ROWS * COLS, CHAN), BF16),
        vmem((9, CHAN, CHAN), BF16), weight, weight, weight, weight, vmem((CHAN,), F32), dma((8,)),
        vmem((3, (ROWS + 2) * COLS, CHAN), BF16), vmem((2, 2, COLS, CHAN), BF16),
        dma((2, 2)), dma((2, 2)), vmem((2 * HALF, CHAN), F32), vmem((2, HALF, CHAN), BF16),
        vmem((CHAN, (ROWS + 2) * COLS), BF16), vmem((HALF_CHAN, (ROWS + 2) * COLS), BF16),
        vmem((2, 3, HALF_CHAN, (ROWS + 2) * COLS), BF16),
    ]
    shapes += [vmem(field, BF16)] * 8 + [dma((4, 2)), dma((4, 2))]
    shapes += [vmem((2, HALF, CHAN), BF16)] * 3 + [vmem((HALF, CHAN), BF16)]
    shapes += [vmem((HALF, WIDE), BF16)] * 4 + [vmem((HALF, HALF), F32)]
    shapes += [vmem((6, HALF, HALF), F32), vmem((HALF, CHAN), F32)]
    shapes += [vmem((HALF, WIDE), BF16)] * 4
    shapes += [vmem((3, 2 * HALF, CHAN), BF16), vmem((2, CHAN, 2 * HALF), BF16)]
    shapes += [vmem((2, HALF, CHAN), BF16), vmem((2, HALF, CHAN), BF16)]
    shapes += [vmem((9, HALF_CHAN, CHAN), F32), dma((3,)), dma((3,))]
    shapes += [vmem((3, (ROWS + 2) * COLS, CHAN), BF16)]
    shapes += [vmem((8, CHAN), F32)]
    shapes += [vmem((PART, 16, 128), BF16), vmem((SMALL_TILES, 16, 128), BF16)]
    return shapes + summer_scratch("yxz", sizes) + conv_summer_scratch(sizes)


def on_device(
    latents, conv_weight, query_weight, key_weight, value_weight, out_weight, norm_gain, out_grad
):
    sizes = chip_sizes()
    frames = lax.axis_size("frame")
    anywhere = pl.BlockSpec(memory_space=pl.ANY)
    inside = pl.BlockSpec(memory_space=pltpu.VMEM)
    field = jax.ShapeDtypeStruct((ROWS, CHAN, COLS), BF16)
    block_out, latents_grad, conv_sum, small_sum = pl.pallas_call(
        functools.partial(block_kernel, sizes),
        out_shape=[
            field,
            field,
            jax.ShapeDtypeStruct((CONV_TILES, 16, 128), BF16),
            jax.ShapeDtypeStruct((SMALL_TILES, 16, 128), BF16),
        ],
        in_specs=[anywhere] * 8,
        out_specs=[inside] * 4,
        scratch_shapes=block_scratch(sizes, frames),
        compiler_params=pltpu.CompilerParams(
            collective_id=0, has_side_effects=True, vmem_limit_bytes=56 << 20
        ),
    )(
        jnp.swapaxes(latents[0], 1, 2),
        conv_weight.reshape(9, CHAN, CHAN),
        query_weight,
        key_weight,
        value_weight,
        out_weight,
        norm_gain,
        jnp.swapaxes(out_grad[0], 1, 2),
    )
    factor = (ROWS * COLS * frames * lax.axis_size("row")) ** (-0.5)
    weight = jax.ShapeDtypeStruct((CHAN, CHAN), F32)
    outs = pl.pallas_call(
        functools.partial(finish_kernel, factor),
        out_shape=[
            field,
            field,
            jax.ShapeDtypeStruct((9, CHAN, CHAN), F32),
            weight,
            weight,
            weight,
            weight,
            jax.ShapeDtypeStruct((CHAN,), F32),
        ],
        in_specs=[anywhere] * 4,
        out_specs=[anywhere] * 7 + [inside],
        scratch_shapes=[
            pltpu.VMEM((CONV_TILES, 16, 128), BF16),
            pltpu.VMEM((SMALL_TILES, 16, 128), BF16),
            pltpu.VMEM((13, CHAN, CHAN), F32),
            pltpu.VMEM((2, ROWS, CHAN, COLS), BF16),
            pltpu.SemaphoreType.DMA((4,)),
            pltpu.SemaphoreType.DMA((14,)),
            pltpu.SemaphoreType.DMA((13,)),
        ],
        compiler_params=pltpu.CompilerParams(vmem_limit_bytes=56 << 20),
    )(block_out, latents_grad, conv_sum, small_sum)
    return (
        jnp.swapaxes(outs[0], 1, 2)[None],
        jnp.swapaxes(outs[1], 1, 2)[None],
        outs[2].reshape(3, 3, CHAN, CHAN),
        *outs[3:7],
        outs[7],
    )


def solution(mesh):
    split = P("frame", "row", None, None)
    return jax.shard_map(
        on_device,
        mesh=mesh,
        in_specs=(split, P(), P(), P(), P(), P(), P(), split),
        out_specs=(split, split, P(), P(), P(), P(), P(), P()),
        check_vma=False,
    )
```

```python
import functools

import jax
import jax.numpy as jnp
from jax import lax
from jax.experimental import pallas as pl
from jax.experimental.pallas import tpu as pltpu
from jax.sharding import PartitionSpec as P

EPS = 1e-06
MESH = pl.DeviceIdType.MESH
CHAN = 320
WIDE = 384
COLS = 128
ROWS = 4
HALF = 256
CONV_TILES = 512
SMALL_TILES = 256
PART = 256
MATRIX_TILES = 50
GAIN_TILE = 230
HALF_CHAN = 160
HALF_TILES = 25
BLOCK = 16
F32 = jnp.float32
BF16 = jnp.bfloat16


def chip_sizes():
    return {"c": 2, "x": 4, "y": lax.axis_size("row") // 4, "z": lax.axis_size("frame") // 2}


def my_place():
    frame, row = lax.axis_index("frame"), lax.axis_index("row")
    return {
        "z": frame // 2,
        "x": lax.rem(row // 2, 2) * 2 + lax.rem(frame, 2),
        "y": row // 4,
        "c": lax.rem(row, 2),
    }


def device_of(place):
    return (
        place["z"] * 2 + lax.rem(place["x"], 2),
        (place["y"] * 2 + place["x"] // 2) * 2 + place["c"],
    )


def along(place, axis, step, sizes):
    moved = dict(place)
    moved[axis] = lax.rem(place[axis] + step, sizes[axis])
    return device_of(moved)


def remote(source, target, send_sem, recv_sem, device):
    copy = pltpu.make_async_remote_copy(
        src_ref=source,
        dst_ref=target,
        send_sem=send_sem,
        recv_sem=recv_sem,
        device_id=device,
        device_id_type=MESH,
    )
    copy.start()
    return copy


def dot(left, right):
    return jnp.dot(left, right, preferred_element_type=F32)


def dot_nt(left, right):
    return lax.dot_general(left, right, (((1,), (1,)), ((), ())), preferred_element_type=F32)


def dot_tn(left, right):
    return lax.dot_general(left, right, (((0,), (0,)), ((), ())), preferred_element_type=F32)


def add_up(target, start, own, own_start, received):
    count = received[0].shape[0]
    step = min(count, BLOCK)

    def body(at, carry):
        at = at * step
        total = own[pl.ds(own_start + at, step)].astype(F32)
        for part in received:
            total = total + part[pl.ds(at, step)].astype(F32)
        target[pl.ds(start + at, step)] = total.astype(BF16)
        return carry

    lax.fori_loop(0, count // step, body, 0)


def wait_bytes(span, sem):
    pltpu.make_async_copy(span, span, sem).wait()


class ConvSummer:
    ORDERS = ("xy", "yx")

    def __init__(self, place, sizes, terms, total, scratch):
        self.place, self.sizes, self.terms, self.total = place, sizes, terms, total
        (
            self.inbox0, self.held1, self.inbox1, self.held2, self.inbox2,
            self.scatter0, self.scatter1, self.scatter2,
            self.gather2, self.gather1, self.gather0, self.back, self.sends,
        ) = scratch
        self.unit = PART // (2 * sizes["x"] * sizes["y"] * sizes["z"])
        self.group = self.unit * sizes["z"]
        self.n1 = [sizes[order[0]] for order in self.ORDERS]
        self.n2 = [sizes[order[1]] for order in self.ORDERS]

    def at(self, part, axis):
        return self.place[self.ORDERS[part][axis]]

    def peer(self, part, axis, step):
        return lax.rem(self.at(part, axis) + step, self.sizes[self.ORDERS[part][axis]])

    def device(self, axis, step):
        return along(self.place, axis, step, self.sizes)

    def local(self, part, chunk, group, unit=0):
        span = self.n2[part] * self.group
        return part * (PART // 2) + chunk * span + group * self.group + unit * self.unit

    def tile(self, part, chunk, group, unit=0):
        return self.place["c"] * PART + self.local(part, chunk, group, unit)

    def scatter_first(self, part):
        for step2 in range(self.n2[0]):
            step2 = (step2 + 1) % self.n2[0]
            for step in range(1, self.n1[0]):
                chunk, group = self.peer(part, 0, step), self.peer(part, 1, step2)
                remote(
                    self.terms.at[pl.ds(self.local(part, chunk, group), self.group)],
                    self.inbox0.at[part, group, pl.ds((step - 1) * self.group, self.group)],
                    self.sends.at[part],
                    self.scatter0.at[part, step2],
                    self.device(self.ORDERS[part][0], step),
                )

    def scatter_second(self):
        for step2 in range(self.n2[0]):
            step2 = (step2 + 1) % self.n2[0]
            for part in range(2):
                chunk, group = self.at(part, 0), self.peer(part, 1, step2)
                wait_bytes(self.inbox0.at[part, group], self.scatter0.at[part, step2])
                total = self.terms[pl.ds(self.local(part, chunk, group), self.group)].astype(F32)
                for step in range(self.n1[part] - 1):
                    span = pl.ds(step * self.group, self.group)
                    total = total + self.inbox0[part, group, span].astype(F32)
                held = self.held1.at[part, group]
                held[...] = total.astype(BF16)
                if step2 > 0:
                    remote(
                        held,
                        self.inbox1.at[part, pl.ds((step2 - 1) * self.group, self.group)],
                        self.sends.at[2],
                        self.scatter1.at[part],
                        self.device(self.ORDERS[part][1], step2),
                    )

    def scatter_third(self):
        for part in range(2):
            wait_bytes(self.inbox1.at[part], self.scatter1.at[part])
            total = self.held1[part, self.at(part, 1)].astype(F32)
            for step in range(self.n2[part] - 1):
                total = total + self.inbox1[part, pl.ds(step * self.group, self.group)].astype(F32)
            self.held2[part] = total.astype(BF16)
            for step in range(1, self.sizes["z"]):
                peer = lax.rem(self.place["z"] + step, self.sizes["z"])
                remote(
                    self.held2.at[part, pl.ds(peer * self.unit, self.unit)],
                    self.inbox2.at[part, pl.ds((step - 1) * self.unit, self.unit)],
                    self.sends.at[3],
                    self.scatter2.at[part],
                    self.device("z", step),
                )

    def gather_third(self):
        for part in range(2):
            wait_bytes(self.inbox2.at[part], self.scatter2.at[part])
            z = self.place["z"]
            total = self.held2[part, pl.ds(z * self.unit, self.unit)].astype(F32)
            for step in range(self.sizes["z"] - 1):
                total = total + self.inbox2[part, pl.ds(step * self.unit, self.unit)].astype(F32)
            mine = self.tile(part, self.at(part, 0), self.at(part, 1), z)
            self.total[pl.ds(mine, self.unit)] = total.astype(BF16)
            span = self.total.at[pl.ds(mine, self.unit)]
            for step in range(1, self.sizes["z"]):
                remote(
                    span, span, self.sends.at[4], self.gather2.at[part], self.device("z", step)
                )

    def spread(self, part, chunk, group, axis, steps, send, sem):
        span = self.total.at[pl.ds(self.tile(part, chunk, group), self.group)]
        for step in steps:
            remote(span, span, self.sends.at[send], sem, self.device(axis, step))

    def gather_rest(self, between):
        n1, n2 = self.n1[0], self.n2[0]
        for part in range(2):
            wait_bytes(
                self.total.at[pl.ds(0, (self.sizes["z"] - 1) * self.unit)], self.gather2.at[part]
            )
            first, second = self.ORDERS[part]
            chunk, group = self.at(part, 0), self.at(part, 1)
            for step in range(1, n2):
                sem = self.gather1.at[part, step]
                self.spread(part, chunk, group, second, [step], 5, sem)
            self.spread(part, chunk, group, first, range(1, n1), 6, self.gather0.at[part, 0])
            self.spread(part, chunk, group, "c", [1], 7, self.back.at[0])
        for step2 in range(1, n2):
            for part in range(2):
                first = self.ORDERS[part][0]
                chunk = self.at(part, 0)
                group = self.peer(part, 1, n2 - step2)
                wait_bytes(self.total.at[pl.ds(0, self.group)], self.gather1.at[part, step2])
                self.spread(
                    part, chunk, group, first, range(1, n1), 6, self.gather0.at[part, step2]
                )
                self.spread(part, chunk, group, "c", [1], 7, self.back.at[0])
        between()
        for step2 in range(n2):
            for part in range(2):
                wait_bytes(
                    self.total.at[pl.ds(0, (n1 - 1) * self.group)], self.gather0.at[part, step2]
                )
                group = self.peer(part, 1, n2 - step2)
                for step in range(1, n1):
                    chunk = self.peer(part, 0, n1 - step)
                    self.spread(part, chunk, group, "c", [1], 7, self.back.at[0])

    def back_wait(self):
        wait_bytes(self.total.at[pl.ds(0, PART)], self.back.at[0])

    def finish(self):
        n1, n2, nz = self.n1[0], self.n2[0], self.sizes["z"]
        counts = (
            n2 * (n1 - 1) * self.group, n2 * (n1 - 1) * self.group, 2 * (n2 - 1) * self.group,
            2 * (nz - 1) * self.unit, 2 * (nz - 1) * self.unit, 2 * (n2 - 1) * self.group,
            2 * n2 * (n1 - 1) * self.group, PART,
        )
        for at, count in enumerate(counts):
            wait_bytes(self.total.at[pl.ds(0, count)], self.sends.at[at])


def conv_summer_scratch(sizes):
    unit = PART // (2 * sizes["x"] * sizes["y"] * sizes["z"])
    group = unit * sizes["z"]
    n1, n2 = sizes["x"], sizes["y"]
    tiles = [
        (2, n2, (n1 - 1) * group), (2, n2, group), (2, (n2 - 1) * group),
        (2, group), (2, (sizes["z"] - 1) * unit),
    ]
    sems = [(2, n2), (2,), (2,), (2,), (2, n2), (2, n2), (1,), (8,)]
    return [pltpu.VMEM(shape + (16, 128), BF16) for shape in tiles] + [
        pltpu.SemaphoreType.DMA(shape) for shape in sems
    ]


class Summer:
    def __init__(self, order, place, sizes, term, total, base, scratch):
        self.order, self.place, self.sizes = order, place, sizes
        self.term, self.total, self.base = term, total, base
        self.core_in, self.held, self.inbox = scratch[0], scratch[1:4], scratch[4:7]
        self.send_sems, self.recv_sems = scratch[7], scratch[8]
        self.spans = [PART // 2]
        for axis in order:
            self.spans.append(self.spans[-1] // sizes[axis])
        self.slot = 0
        self.sent = []
        self.wait = []

    def push(self, source, target, axis, step):
        device = along(self.place, axis, step, self.sizes)
        copy = remote(
            source, target, self.send_sems.at[self.slot], self.recv_sems.at[self.slot], device
        )
        self.slot += 1
        self.sent.append(copy)
        self.wait.append(copy)

    def arrive(self):
        for copy in self.wait:
            copy.wait_recv()
        self.wait = []

    def core_start(self):
        other = self.base + (1 - self.place["c"]) * self.spans[0]
        self.push(self.term.at[pl.ds(other, self.spans[0])], self.core_in, "c", 1)

    def core_end(self):
        self.arrive()
        mine = self.base + self.place["c"] * self.spans[0]
        add_up(self.held[0], 0, self.term, mine, [self.core_in])

    def scatter_start(self, level):
        axis, span = self.order[level], self.spans[level + 1]
        for step in range(1, self.sizes[axis]):
            peer = lax.rem(self.place[axis] + step, self.sizes[axis])
            self.push(
                self.held[level].at[pl.ds(peer * span, span)],
                self.inbox[level].at[step - 1],
                axis,
                step,
            )

    def scatter_end(self, level):
        self.arrive()
        axis, span = self.order[level], self.spans[level + 1]
        received = [self.inbox[level].at[step] for step in range(self.sizes[axis] - 1)]
        mine = self.place[axis] * span
        if level < 2:
            add_up(self.held[level + 1], 0, self.held[level], mine, received)
        else:
            add_up(self.total, self.start_of(3), self.held[level], mine, received)

    def start_of(self, levels):
        start = self.base + self.place["c"] * self.spans[0]
        for level in range(levels):
            start = start + self.place[self.order[level]] * self.spans[level + 1]
        return start

    def gather_start(self, level):
        axis = self.order[level]
        mine = self.total.at[pl.ds(self.start_of(level + 1), self.spans[level + 1])]
        for step in range(1, self.sizes[axis]):
            self.push(mine, mine, axis, step)

    def core_back(self):
        mine = self.total.at[pl.ds(self.start_of(0), self.spans[0])]
        self.push(mine, mine, "c", 1)

    def finish(self):
        for copy in self.sent:
            copy.wait_send()


def summer_scratch(order, sizes):
    spans = [PART // 2]
    for axis in order:
        spans.append(spans[-1] // sizes[axis])
    shapes = [(spans[0], 16, 128)]
    shapes += [(span, 16, 128) for span in spans[:3]]
    shapes += [(sizes[axis] - 1, span, 16, 128) for axis, span in zip(order, spans[1:])]
    copies = 2 * (1 + sum(sizes[axis] - 1 for axis in order))
    return [pltpu.VMEM(shape, BF16) for shape in shapes] + [
        pltpu.SemaphoreType.DMA((copies,)),
        pltpu.SemaphoreType.DMA((copies,)),
    ]


def pack(matrix, tiles, base):
    held = matrix.astype(BF16)
    for block in range(2):
        cut = held[:, block * 128 : block * 128 + 128]
        tiles[pl.ds(base + 20 * block, 20)] = cut.reshape(20, 16, 128)
    low, high = held[:160, 256:], held[160:, 256:]
    tail = jnp.concatenate([low, high], axis=1)
    tiles[pl.ds(base + 40, 10)] = tail.reshape(10, 16, 128)


def pack_half(matrix, tiles, base):
    held = matrix.astype(BF16)
    for block in range(2):
        cut = held[:, block * 128 : block * 128 + 128]
        tiles[pl.ds(base + 10 * block, 10)] = cut.reshape(10, 16, 128)
    tail = jnp.concatenate([held[:80, 256:], held[80:, 256:]], axis=1)
    tiles[pl.ds(base + 20, 5)] = tail.reshape(5, 16, 128)


def unpack_half(tiles, base, target, at, row, factor):
    span = pl.ds(row, HALF_CHAN)
    for block in range(2):
        cut = tiles[pl.ds(base + 10 * block, 10)].reshape(HALF_CHAN, 128)
        target[at, span, block * 128 : block * 128 + 128] = cut.astype(F32) * factor
    tail = tiles[pl.ds(base + 20, 5)].reshape(80, 128).astype(F32) * factor
    target[at, pl.ds(row, 80), 256:] = tail[:, :64]
    target[at, pl.ds(row + 80, 80), 256:] = tail[:, 64:]


def unpack(tiles, base, target, at, factor):
    for block in range(2):
        cut = tiles[pl.ds(base + 20 * block, 20)].reshape(CHAN, 128)
        target[at, :, block * 128 : block * 128 + 128] = cut.astype(F32) * factor
    tail = tiles[pl.ds(base + 40, 10)].reshape(160, 128).astype(F32) * factor
    target[at, :160, 256:] = tail[:, :64]
    target[at, 160:, 256:] = tail[:, 64:]


def finish_kernel(factor, block_in, back_in, conv_in, small_in, *refs):
    (block_out, back_out, conv_out), small_outs, gain_out = refs[:3], refs[3:7], refs[7]
    conv, small, wide, fields, through, load_sems, half_sems, store_sems = refs[8:]
    moves = []
    for at, (source, target) in enumerate(((block_in, block_out), (back_in, back_out))):
        moves.append(
            (
                pltpu.make_async_copy(source, fields.at[at], through.at[at]),
                pltpu.make_async_copy(fields.at[at], target, through.at[at + 2]),
            )
        )
        moves[-1][0].start()

    def load(at, source, target):
        span = pl.ds(at * MATRIX_TILES, MATRIX_TILES)
        return source.at[span], target.at[span]

    for at in range(4):
        pltpu.make_async_copy(*load(at, small_in, small), load_sems.at[9 + at]).start()
    def load_half(at, core):
        span = pl.ds(core * PART + at * HALF_TILES, HALF_TILES)
        return pltpu.make_async_copy(conv_in.at[span], conv.at[span], half_sems.at[at, core])

    for at in range(9):
        for core in range(2):
            load_half(at, core).start()
    gain_loads = []
    for core in range(2):
        span = pl.ds(core * PART + GAIN_TILE, 2)
        gain_loads.append(
            pltpu.make_async_copy(conv_in.at[span], conv.at[span], half_sems.at[9, core])
        )
        gain_loads[-1].start()
    for at in range(4):
        pltpu.make_async_copy(*load(at, small_in, small), load_sems.at[9 + at]).wait()
        unpack(small, at * MATRIX_TILES, wide, 9 + at, factor)
        pltpu.make_async_copy(wide.at[9 + at], small_outs[at], store_sems.at[9 + at]).start()

    def conv_tap(at, carry):
        for core in range(2):
            load_half(at, core).wait()
            start = core * PART + at * HALF_TILES
            unpack_half(conv, start, wide, at, core * HALF_CHAN, factor)
        pltpu.make_async_copy(wide.at[at], conv_out.at[at], store_sems.at[at]).start()
        return carry

    for move in moves:
        move[0].wait()
        move[1].start()
    lax.fori_loop(0, 9, conv_tap, 0)
    for copy in gain_loads:
        copy.wait()
    pieces = []
    for at in range(2):
        tiles = [conv[core * PART + GAIN_TILE + at].astype(F32) for core in range(2)]
        pieces.append((tiles[0] + tiles[1]) * factor)
    gain_out[0:128] = pieces[0][0]
    gain_out[128:256] = pieces[0][1]
    gain_out[256:] = pieces[1][0, :64]
    for move in moves:
        move[1].wait()
    for at in range(9):
        pltpu.make_async_copy(wide.at[at], conv_out.at[at], store_sems.at[at]).wait()
    for at in range(4):
        pltpu.make_async_copy(wide.at[9 + at], small_outs[at], store_sems.at[9 + at]).wait()


def shifts(cells):
    column = lax.broadcasted_iota(jnp.int32, cells.shape, 0)
    left = jnp.where(column == 0, 0.0, pltpu.roll(cells, 1, 0))
    right = jnp.where(column == COLS - 1, 0.0, pltpu.roll(cells, COLS - 1, 0))
    return [left, cells, right]


class Swap:
    def __init__(self, source, target, send_sems, recv_sems, peers, me):
        self.source, self.target, self.peers, self.me = source, target, peers, me
        self.send_sems, self.recv_sems = send_sems, recv_sems

    def start(self, half):
        for frame, device in self.peers:
            remote(
                self.source.at[half, frame],
                self.target.at[half, self.me],
                self.send_sems.at[half],
                self.recv_sems.at[half],
                device,
            )
        self.target[half, self.me] = self.source[half, self.me]

    def wait(self, half):
        span = self.target.at[half, pl.ds(0, len(self.peers))]
        pltpu.make_async_copy(span, span, self.recv_sems.at[half]).wait()

    def finish(self):
        for half in range(2):
            span = self.source.at[half, pl.ds(0, len(self.peers))]
            pltpu.make_async_copy(span, span, self.send_sems.at[half]).wait()


def norm_of(resid):
    return lax.rsqrt(jnp.mean(resid * resid, axis=-1, keepdims=True) + EPS)


def cell_start(half, at):
    if half == 0:
        return COLS + at * 64
    return jnp.where(at < 2, at * 64, HALF + at * 64)


def head_masks():
    low = lax.broadcasted_iota(jnp.int32, (1, 128), 1) < 64
    return low, [jnp.where(low, 0.125, 0.0).astype(BF16), jnp.where(low, 0.0, 0.125).astype(BF16)]


def attend(q_s, k_s, v_s, bias, probs_s, mixed_s):
    low, masks = head_masks()

    def tile(at, masks):
        start = at * 128
        span = pl.ds(start if isinstance(at, int) else pl.multiple_of(start, 128), 128)
        queries, keys, values = q_s[:, span], k_s[:, span], v_s[:, span]
        found = []
        for head, mask in enumerate(masks):
            scores = dot_nt(queries * mask, keys) + bias[...]
            expo = jnp.exp(scores)
            probs = expo * (1.0 / jnp.sum(expo, axis=-1, keepdims=True))
            probs_s[2 * at + head] = probs
            found.append(dot(probs.astype(BF16), values))
        total = found[0] if len(found) == 1 else jnp.where(low, *found)
        mixed_s[:, span] = total.astype(BF16)

    def pair(at, carry):
        tile(at, masks)
        return carry

    lax.fori_loop(0, 2, pair, 0)
    tile(2, masks[:1])


def attend_back(q_s, k_s, v_s, d_s, probs_s, qp_s, kp_s, vp_s):
    low, masks = head_masks()

    def tile(at, masks):
        start = at * 128
        span = pl.ds(start if isinstance(at, int) else pl.multiple_of(start, 128), 128)
        queries, keys, values, grads = q_s[:, span], k_s[:, span], v_s[:, span], d_s[:, span]
        found = []
        for head, mask in enumerate(masks):
            probs = probs_s[2 * at + head]
            prob_grad = dot_nt(grads * mask, values)
            inner = jnp.sum(probs * prob_grad, axis=-1, keepdims=True)
            score_b = (probs * (prob_grad - inner)).astype(BF16)
            found.append(
                (
                    dot(score_b, keys),
                    dot_tn(score_b, queries),
                    dot_tn(probs.astype(BF16), grads),
                )
            )
        for place, target in enumerate((qp_s, kp_s, vp_s)):
            parts = [part[place] for part in found]
            total = parts[0] if len(parts) == 1 else jnp.where(low, *parts)
            target[:, span] = total.astype(BF16)

    def pair(at, carry):
        tile(at, masks)
        return carry

    lax.fori_loop(0, 2, pair, 0)
    tile(2, masks[:1])


def block_kernel(sizes, latents, conv_w, query_w, key_w, value_w, out_w, gain, out_grad, *refs):
    (block_hbm, back_hbm, conv_hbm, small_hbm), refs = refs[:4], refs[4:]
    (
        lat_in, grad_in, lat, grad, weights, wq, wk, wv, wo, gain_v, in_sems,
        padded, wide, halo, halo_send, halo_recv, acc, resid, act_c, act_in, act_t,
        normed_out, normed_in, og_out, og_in, ng_out, ng_in, mix_out, mix_in,
        swap_send, swap_recv,
        og_n, normed_n, mixed_n, back_n,
        q_s, k_s, v_s, d_s, bias, probs_s, out_acc, mixed_s, qp_s, kp_s, vp_s, parts, flip,
        resid_grad, rg_in, conv_acc, pair_send, pair_recv, grad_pad, gain_acc, conv_terms, small_terms,
        block_out, latents_grad, conv_total, small_total, out_sems,
    ), refs = refs[:62], refs[62:]
    frames = lax.axis_size("frame")
    rows_n = lax.axis_size("row")
    chunk = HALF // frames
    me, row = lax.axis_index("frame"), lax.axis_index("row")
    place = my_place()
    peers = []
    for step in range(1, frames):
        frame = lax.rem(me + step, frames)
        peers.append((frame, (frame, row)))
    above = (me, lax.rem(row + rows_n - 1, rows_n))
    below = (me, lax.rem(row + 1, rows_n))

    barrier = pltpu.get_barrier_semaphore()
    partners = [device for _, device in peers] + [above, below]
    for axis in "cxy":
        partners += [along(place, axis, step, sizes) for step in range(1, sizes[axis])]
    for device in partners:
        pl.semaphore_signal(barrier, inc=1, device_id=device, device_id_type=MESH)

    loads = []
    pairs = (
        (latents, lat_in), (out_grad, grad_in), (conv_w, weights), (gain, gain_v),
        (out_w, wo), (query_w, wq), (key_w, wk), (value_w, wv),
    )
    for at, (source, target) in enumerate(pairs):
        loads.append(pltpu.make_async_copy(source, target, in_sems.at[at]))
        loads[-1].start()

    loads[0].wait()

    def activate(at, carry):
        span = pl.ds(at * COLS, COLS)
        cells = lat_in[at].astype(F32).T
        lat[span] = cells.astype(BF16)
        act = (cells * jax.nn.sigmoid(cells)).astype(BF16).astype(F32)
        span = pl.ds((at + 1) * COLS, COLS)
        for shift, copy in enumerate(shifts(act)):
            wide[span, shift * CHAN : shift * CHAN + CHAN] = copy.astype(BF16)
        padded[span] = act.astype(BF16)
        return carry

    lax.fori_loop(0, ROWS, activate, 0)
    loads[1].wait()

    def flip_grad(at, carry):
        cells = grad_in[at].astype(F32).T.astype(BF16)
        grad[pl.ds(at * COLS, COLS)] = cells
        half = jnp.where((at == 0) | (at == ROWS - 1), 1, 0)
        span = pl.ds(jnp.where(at >= 2, frames // 2, 0), frames // 2)
        og_out[half, span] = cells[:, :256].reshape(frames // 2, chunk, 256)
        normed_out[half, span, :, CHAN:] = cells[:, 256:].reshape(frames // 2, chunk, 64)
        return carry

    lax.fori_loop(0, ROWS, flip_grad, 0)
    pl.semaphore_wait(barrier, len(partners))

    def halo_start(source, kind):
        return [
            remote(source.at[pl.ds(COLS, COLS)], halo.at[kind, 1],
                   halo_send.at[kind, 0], halo_recv.at[kind, 0], above),
            remote(source.at[pl.ds(ROWS * COLS, COLS)], halo.at[kind, 0],
                   halo_send.at[kind, 1], halo_recv.at[kind, 1], below),
        ]

    def halo_end(copies, kind, store):
        for copy in copies:
            copy.wait_recv()
        ends = (row > 0, row < rows_n - 1)
        for side, inside in enumerate(ends):
            keep = jnp.where(inside, 1.0, 0.0).astype(F32)
            cells = halo[kind, side].astype(F32) * keep
            store(pl.ds(side * (ROWS + 1) * COLS, COLS), cells)

    def store_act(span, cells):
        for shift, copy in enumerate(shifts(cells)):
            wide[span, shift * CHAN : shift * CHAN + CHAN] = copy.astype(BF16)
        padded[span] = cells.astype(BF16)

    def store_grad(span, cells):
        for shift, copy in enumerate(shifts(cells)):
            grad_pad[shift, span] = copy.astype(BF16)

    act_halo = halo_start(padded, 0)

    swaps = []
    buffers = ((og_out, og_in), (normed_out, normed_in), (ng_out, ng_in), (mix_out, mix_in))
    for at, (source, target) in enumerate(buffers):
        swaps.append(Swap(source, target, swap_send.at[at], swap_recv.at[at], peers, me))
    og_swap, normed_swap, ng_swap, mix_swap = swaps

    loads[2].wait()
    loads[3].wait()

    def conv_half(half):
        total = None
        for a in range(3):
            if half == 0:
                cells = wide[(a + 1) * COLS : (a + 1) * COLS + HALF]
            else:
                cells = jnp.concatenate(
                    [wide[a * COLS : (a + 1) * COLS], wide[(a + 3) * COLS : (a + 4) * COLS]]
                )
            term = dot(cells, weights[3 * a : 3 * a + 3].reshape(3 * CHAN, CHAN))
            total = term if total is None else total + term
        acc[pl.ds(0, HALF)] = total
        count = 64 // chunk

        def finish(at, carry):
            cells = lat[pl.ds(pl.multiple_of(cell_start(half, at), 64), 64)].astype(F32)
            held = (cells + acc[pl.ds(at * 64, 64)]).astype(BF16)
            resid[half, pl.ds(at * 64, 64)] = held
            held = held.astype(F32)
            normed = (held * norm_of(held) * gain_v[...].reshape(1, CHAN)).astype(BF16)
            normed_out[half, pl.ds(at * count, count), :, :CHAN] = normed.reshape(count, chunk, CHAN)
            return carry

        lax.fori_loop(0, 4, finish, 0)

    og_swap.start(0)
    conv_half(0)
    normed_swap.start(0)
    halo_end(act_halo, 0, store_act)
    conv_half(1)
    normed_swap.start(1)
    og_swap.start(1)

    position = lax.broadcasted_iota(jnp.int32, (HALF, HALF), 0)
    other = lax.broadcasted_iota(jnp.int32, (HALF, HALF), 1)
    same = lax.rem(position, chunk) == lax.rem(other, chunk)
    bias[...] = jnp.where(same, 0.0, -1e30)
    for field in (q_s, k_s, v_s, d_s):
        field[:, 256:] = jnp.zeros((HALF, 128), BF16)
    act_c[...] = padded[...].astype(F32).T.astype(BF16)
    core = place["c"]
    partner = along(place, "c", 1, sizes)
    mine = pl.ds(pl.multiple_of(core * HALF_CHAN, HALF_CHAN), HALF_CHAN)
    theirs = pl.ds(pl.multiple_of((1 - core) * HALF_CHAN, HALF_CHAN), HALF_CHAN)
    pair = [remote(act_c.at[theirs], act_in, pair_send.at[0], pair_recv.at[0], partner)]

    def shift_lanes(at, carry, source, side):
        span = pl.ds(pl.multiple_of(at * COLS, COLS), COLS)
        cells = source[:, span].astype(F32)
        column = lax.broadcasted_iota(jnp.int32, cells.shape, 1)
        left = jnp.where(column == 0, 0.0, pltpu.roll(cells, 1, 1))
        right = jnp.where(column == COLS - 1, 0.0, pltpu.roll(cells, COLS - 1, 1))
        for shift, copy in enumerate((left, cells, right)):
            act_t[side, shift * HALF_CHAN : (shift + 1) * HALF_CHAN, span] = copy.astype(BF16)
        return carry

    own_rows = functools.partial(shift_lanes, source=act_c.at[mine], side=0)
    lax.fori_loop(0, ROWS + 2, own_rows, 0)
    for load in loads[4:]:
        load.wait()

    for half in range(2):
        normed_swap.wait(half)
        arrived = normed_in[half].reshape(HALF, WIDE)
        normed_n[half] = arrived[:, :CHAN]
        og_n[half, :, 256:] = arrived[:, CHAN:]
        q_s[:, :CHAN] = dot(normed_n[half], wq[...]).astype(BF16)
        k_s[:, :CHAN] = dot(normed_n[half], wk[...]).astype(BF16)
        v_s[:, :CHAN] = dot(normed_n[half], wv[...]).astype(BF16)
        attend(q_s, k_s, v_s, bias, probs_s, mixed_s)
        mixed_n[half] = mixed_s[:, :CHAN]
        mix_out[half] = mixed_s[:, :256].reshape(frames, chunk, 256)
        ng_out[half, :, :, CHAN:] = mixed_s[:, 256:CHAN].reshape(frames, chunk, 64)
        og_swap.wait(half)
        og_n[half, :, :256] = og_in[half].reshape(HALF, 256)
        d_s[:, :CHAN] = dot_nt(og_n[half], wo[...]).astype(BF16)
        attend_back(q_s, k_s, v_s, d_s, probs_s, qp_s, kp_s, vp_s)
        back = dot_nt(qp_s[:, :CHAN], wq[...])
        back = back + dot_nt(kp_s[:, :CHAN], wk[...])
        back = back + dot_nt(vp_s[:, :CHAN], wv[...])
        ng_out[half, :, :, :CHAN] = back.astype(BF16).reshape(frames, chunk, CHAN)
        ng_swap.start(half)
        for at, field in enumerate((qp_s, kp_s, vp_s)):
            parts[at, pl.ds(half * HALF, HALF)] = field[:, :CHAN]

    flip[0] = normed_n[...].reshape(2 * HALF, CHAN).astype(F32).T.astype(BF16)
    flip[1] = mixed_n[...].reshape(2 * HALF, CHAN).astype(F32).T.astype(BF16)
    for at in range(3):
        pack(dot(flip[0], parts[at]), small_terms, at * MATRIX_TILES)
    pack(dot(flip[1], og_n[...].reshape(2 * HALF, CHAN)), small_terms, 3 * MATRIX_TILES)
    spare = SMALL_TILES - 4 * MATRIX_TILES
    small_terms[pl.ds(4 * MATRIX_TILES, spare)] = jnp.zeros((spare, 16, 128), BF16)

    conv = ConvSummer(place, sizes, conv_terms, conv_total, refs[9:])
    small = Summer("yxz", place, sizes, small_terms, small_total, 0, refs[:9])
    small.core_start()

    gain_acc[...] = jnp.zeros((8, CHAN), F32)
    for half in range(2):
        ng_swap.wait(half)

        def undo_norm(at, carry, half=half):
            count = 64 // chunk
            begin = pl.multiple_of(cell_start(half, at), 64)
            held = resid[half, pl.ds(at * 64, 64)].astype(F32)
            back = ng_in[half, pl.ds(at * count, count), :, :CHAN].reshape(64, CHAN).astype(F32)
            inv = norm_of(held)
            product = back * held
            total = jnp.sum((product * inv).reshape(8, 8, CHAN), axis=0)
            gain_acc[...] += total
            tangent = back * gain_v[...].reshape(1, CHAN)
            mean = jnp.mean(product * gain_v[...].reshape(1, CHAN), axis=-1, keepdims=True)
            value = grad[pl.ds(begin, 64)].astype(F32) + (
                inv * tangent - held * (inv * inv * inv) * mean
            )
            resid_grad[half, pl.ds(at * 64, 64)] = value.astype(BF16)
            return carry

        lax.fori_loop(0, 4, undo_norm, 0)
        pair.append(
            remote(
                resid_grad.at[half],
                rg_in.at[half],
                pair_send.at[1 + half],
                pair_recv.at[1 + half],
                partner,
            )
        )
        if half == 0:
            pair[0].wait_recv()
            other_rows = functools.partial(shift_lanes, source=act_in, side=1)
            lax.fori_loop(0, ROWS + 2, other_rows, 0)

            def inner_taps(at, carry, side, cells):
                span = pl.ds(pl.multiple_of((at + 1) * COLS, COLS), HALF)
                total = dot(act_t[side, :, span], cells[0])
                if side == 0:
                    conv_acc[at] = total
                else:
                    conv_acc[at] += total
                return carry

            lax.fori_loop(
                0, 3, functools.partial(inner_taps, side=0, cells=resid_grad), 0
            )
            small.core_end()
            small.scatter_start(0)
            pair[1].wait_recv()
            lax.fori_loop(0, 3, functools.partial(inner_taps, side=1, cells=rg_in), 0)
        else:
            mix_swap.start(0)
            mix_swap.start(1)


    def pad_grad(at, carry):
        half = jnp.where((at == 0) | (at == ROWS - 1), 1, 0)
        side = jnp.where(at >= 2, 1, 0)
        cells = resid_grad[half, pl.ds(side * COLS, COLS)].astype(F32)
        for shift, copy in enumerate(shifts(cells)):
            grad_pad[shift, pl.ds((at + 1) * COLS, COLS)] = copy.astype(BF16)
        return carry

    def edge_cells(side, at):
        spans = [pl.ds(pl.multiple_of((at + gap) * COLS, COLS), COLS) for gap in (0, ROWS - 1)]
        return jnp.concatenate([act_t[side, :, span] for span in spans], axis=1)

    def second_taps(at, carry):
        conv_acc[at] += dot(edge_cells(0, at), resid_grad[1])
        return carry

    lax.fori_loop(0, 3, second_taps, 0)
    lax.fori_loop(0, ROWS, pad_grad, 0)
    grad_halo = halo_start(grad_pad.at[1], 1)

    spare = PART - 9 * HALF_TILES
    conv_terms[pl.ds(9 * HALF_TILES, spare)] = jnp.zeros((spare, 16, 128), BF16)
    gains = jnp.sum(gain_acc[...], axis=0, keepdims=True)
    line = lax.broadcasted_iota(jnp.int32, (16, 128), 0)
    gain_tile = jnp.where(line == 0, gains[:, :128], jnp.where(line == 1, gains[:, 128:256], 0.0))
    conv_terms[GAIN_TILE] = gain_tile.astype(BF16)
    tail = jnp.where(line[:, :64] == 0, gains[:, 256:], 0.0)
    conv_terms[GAIN_TILE + 1, :, :64] = tail.astype(BF16)
    pair[2].wait_recv()

    def last_taps(at, carry):
        total = conv_acc[at] + dot(edge_cells(1, at), rg_in[1])
        for b in range(3):
            part = total[b * HALF_CHAN : (b + 1) * HALF_CHAN]
            pack_half(part, conv_terms, (at * 3 + b) * HALF_TILES)
        return carry

    lax.fori_loop(0, 2, last_taps, 0)
    conv.scatter_first(0)
    lax.fori_loop(2, 3, last_taps, 0)
    conv.scatter_first(1)
    small.scatter_end(0)
    small.scatter_start(1)

    def project_out(half):
        mix_swap.wait(half)
        back_n[:, :256] = mix_in[half].reshape(HALF, 256)
        back_n[:, 256:] = ng_in[half, :, :, CHAN:].reshape(HALF, 64)
        out_acc[...] = dot(back_n[...], wo[...])

        def write_out(at, carry):
            held = resid[half, pl.ds(at * COLS, COLS)].astype(F32)
            total = held + out_acc[pl.ds(at * COLS, COLS)]
            block_out[at + 1 if half == 0 else at * 3] = total.T.astype(BF16)
            return carry

        lax.fori_loop(0, 2, write_out, 0)

    halo_end(grad_halo, 1, store_grad)
    acc[...] = jnp.zeros((2 * HALF, CHAN), F32)

    def back_tap(at, carry):
        a, b = at // 3, lax.rem(at, 3)
        cells = grad_pad[2 - b, pl.ds((2 - a) * COLS, ROWS * COLS)]
        acc[...] += dot_nt(cells, weights[at])
        return carry

    lax.fori_loop(0, 3, back_tap, 0)
    small.scatter_end(1)
    small.scatter_start(2)
    lax.fori_loop(3, 5, back_tap, 0)
    conv.scatter_second()
    small.scatter_end(2)
    small.gather_start(2)
    stores = []

    def store(source, target):
        stores.append(pltpu.make_async_copy(source, target, out_sems.at[len(stores)]))
        stores[-1].start()

    project_out(0)
    project_out(1)
    store(block_out, block_hbm)
    conv.scatter_third()
    small.arrive()
    small.gather_start(1)
    lax.fori_loop(5, 9, back_tap, 0)
    conv.gather_third()
    small.arrive()
    small.gather_start(0)
    def write_back(at, carry):
        cells = lat[pl.ds(at * COLS, COLS)].astype(F32)
        sigma = jax.nn.sigmoid(cells)
        slope = sigma * (1.0 + cells * (1.0 - sigma))
        half = jnp.where((at == 0) | (at == ROWS - 1), 1, 0)
        side = jnp.where(at >= 2, 1, 0)
        value = resid_grad[half, pl.ds(side * COLS, COLS)].astype(F32) + acc[pl.ds(at * COLS, COLS)] * slope
        latents_grad[at] = value.T.astype(BF16)
        return carry

    lax.fori_loop(0, ROWS, write_back, 0)
    store(latents_grad, back_hbm)
    def return_small():
        small.arrive()
        small.core_back()

    conv.gather_rest(return_small)
    own_half = pl.ds(place["c"] * PART, PART)
    store(conv_total.at[own_half], conv_hbm.at[own_half])
    small.arrive()
    store(small_total, small_hbm)
    conv.back_wait()
    other_half = pl.ds((1 - place["c"]) * PART, PART)
    store(conv_total.at[other_half], conv_hbm.at[other_half])
    small.finish()
    conv.finish()
    for swap in swaps:
        swap.finish()
    for copy in act_halo + grad_halo + pair:
        copy.wait_send()
    for copy in stores:
        copy.wait()


def block_scratch(sizes, frames):
    narrow, wide = (2, frames, HALF // frames, 256), (2, frames, HALF // frames, WIDE)
    vmem = pltpu.VMEM
    dma = pltpu.SemaphoreType.DMA
    weight = vmem((CHAN, CHAN), BF16)
    shapes = [
        vmem((ROWS, CHAN, COLS), BF16), vmem((ROWS, CHAN, COLS), BF16),
        vmem((ROWS * COLS, CHAN), BF16), vmem((ROWS * COLS, CHAN), BF16),
        vmem((9, CHAN, CHAN), BF16), weight, weight, weight, weight, vmem((CHAN,), F32), dma((8,)),
        vmem(((ROWS + 2) * COLS, CHAN), BF16), vmem(((ROWS + 2) * COLS, 3 * CHAN), BF16),
        vmem((2, 2, COLS, CHAN), BF16),
        dma((2, 2)), dma((2, 2)), vmem((2 * HALF, CHAN), F32), vmem((2, HALF, CHAN), BF16),
        vmem((CHAN, (ROWS + 2) * COLS), BF16), vmem((HALF_CHAN, (ROWS + 2) * COLS), BF16),
        vmem((2, 3 * HALF_CHAN, (ROWS + 2) * COLS), BF16),
    ]
    shapes += [vmem(shape, BF16) for shape in (wide, wide, narrow, narrow, wide, wide, narrow, narrow)]
    shapes += [dma((4, 2)), dma((4, 2))]
    shapes += [vmem((2, HALF, CHAN), BF16)] * 3 + [vmem((HALF, CHAN), BF16)]
    shapes += [vmem((HALF, WIDE), BF16)] * 4 + [vmem((HALF, HALF), F32)]
    shapes += [vmem((5, HALF, HALF), F32), vmem((HALF, CHAN), F32)]
    shapes += [vmem((HALF, WIDE), BF16)] * 4
    shapes += [vmem((3, 2 * HALF, CHAN), BF16), vmem((2, CHAN, 2 * HALF), BF16)]
    shapes += [vmem((2, HALF, CHAN), BF16), vmem((2, HALF, CHAN), BF16)]
    shapes += [vmem((3, 3 * HALF_CHAN, CHAN), F32), dma((3,)), dma((3,))]
    shapes += [vmem((3, (ROWS + 2) * COLS, CHAN), BF16)]
    shapes += [vmem((8, CHAN), F32)]
    shapes += [vmem((PART, 16, 128), BF16), vmem((SMALL_TILES, 16, 128), BF16)]
    shapes += [vmem((ROWS, CHAN, COLS), BF16)] * 2
    shapes += [vmem((CONV_TILES, 16, 128), BF16), vmem((SMALL_TILES, 16, 128), BF16), dma((5,))]
    return shapes + summer_scratch("yxz", sizes) + conv_summer_scratch(sizes)


def on_device(
    latents, conv_weight, query_weight, key_weight, value_weight, out_weight, norm_gain, out_grad
):
    sizes = chip_sizes()
    frames = lax.axis_size("frame")
    anywhere = pl.BlockSpec(memory_space=pl.ANY)
    inside = pl.BlockSpec(memory_space=pltpu.VMEM)
    field = jax.ShapeDtypeStruct((ROWS, CHAN, COLS), BF16)
    block_out, latents_grad, conv_sum, small_sum = pl.pallas_call(
        functools.partial(block_kernel, sizes),
        out_shape=[
            field,
            field,
            jax.ShapeDtypeStruct((CONV_TILES, 16, 128), BF16),
            jax.ShapeDtypeStruct((SMALL_TILES, 16, 128), BF16),
        ],
        in_specs=[anywhere] * 8,
        out_specs=[anywhere] * 4,
        scratch_shapes=block_scratch(sizes, frames),
        compiler_params=pltpu.CompilerParams(
            collective_id=0, has_side_effects=True, vmem_limit_bytes=56 << 20
        ),
    )(
        jnp.swapaxes(latents[0], 1, 2),
        conv_weight.reshape(9, CHAN, CHAN),
        query_weight,
        key_weight,
        value_weight,
        out_weight,
        norm_gain,
        jnp.swapaxes(out_grad[0], 1, 2),
    )
    factor = (ROWS * COLS * frames * lax.axis_size("row")) ** (-0.5)
    weight = jax.ShapeDtypeStruct((CHAN, CHAN), F32)
    outs = pl.pallas_call(
        functools.partial(finish_kernel, factor),
        out_shape=[
            field,
            field,
            jax.ShapeDtypeStruct((9, CHAN, CHAN), F32),
            weight,
            weight,
            weight,
            weight,
            jax.ShapeDtypeStruct((CHAN,), F32),
        ],
        in_specs=[anywhere] * 4,
        out_specs=[anywhere] * 7 + [inside],
        scratch_shapes=[
            pltpu.VMEM((CONV_TILES, 16, 128), BF16),
            pltpu.VMEM((SMALL_TILES, 16, 128), BF16),
            pltpu.VMEM((13, CHAN, CHAN), F32),
            pltpu.VMEM((2, ROWS, CHAN, COLS), BF16),
            pltpu.SemaphoreType.DMA((4,)),
            pltpu.SemaphoreType.DMA((13,)),
            pltpu.SemaphoreType.DMA((10, 2)),
            pltpu.SemaphoreType.DMA((13,)),
        ],
        compiler_params=pltpu.CompilerParams(vmem_limit_bytes=56 << 20),
    )(block_out, latents_grad, conv_sum, small_sum)
    return (
        jnp.swapaxes(outs[0], 1, 2)[None],
        jnp.swapaxes(outs[1], 1, 2)[None],
        outs[2].reshape(3, 3, CHAN, CHAN),
        *outs[3:7],
        outs[7],
    )


def solution(mesh):
    split = P("frame", "row", None, None)
    return jax.shard_map(
        on_device,
        mesh=mesh,
        in_specs=(split, P(), P(), P(), P(), P(), P(), split),
        out_specs=(split, split, P(), P(), P(), P(), P(), P()),
        check_vma=False,
    )
```

```python
import functools

import jax
import jax.numpy as jnp
from jax import lax
from jax.experimental import pallas as pl
from jax.experimental.pallas import tpu as pltpu
from jax.sharding import PartitionSpec as P

EPS = 1e-06
MESH = pl.DeviceIdType.MESH
CHAN = 320
WIDE = 384
COLS = 128
ROWS = 4
HALF = 256
CONV_TILES = 512
SMALL_TILES = 256
PART = 256
MATRIX_TILES = 50
GAIN_TILE = 230
HALF_CHAN = 160
HALF_TILES = 25
BLOCK = 16
F32 = jnp.float32
BF16 = jnp.bfloat16


def chip_sizes():
    return {"c": 2, "x": 4, "y": lax.axis_size("row") // 4, "z": lax.axis_size("frame") // 2}


def my_place():
    frame, row = lax.axis_index("frame"), lax.axis_index("row")
    return {
        "z": frame // 2,
        "x": lax.rem(row // 2, 2) * 2 + lax.rem(frame, 2),
        "y": row // 4,
        "c": lax.rem(row, 2),
    }


def device_of(place):
    return (
        place["z"] * 2 + lax.rem(place["x"], 2),
        (place["y"] * 2 + place["x"] // 2) * 2 + place["c"],
    )


def along(place, axis, step, sizes):
    moved = dict(place)
    moved[axis] = lax.rem(place[axis] + step, sizes[axis])
    return device_of(moved)


def aslant(place, axis, step, depth, sizes):
    moved = dict(place)
    moved["z"] = lax.rem(place["z"] + depth, sizes["z"])
    return along(moved, axis, step, sizes)


def remote(source, target, send_sem, recv_sem, device):
    copy = pltpu.make_async_remote_copy(
        src_ref=source,
        dst_ref=target,
        send_sem=send_sem,
        recv_sem=recv_sem,
        device_id=device,
        device_id_type=MESH,
    )
    copy.start()
    return copy


def dot(left, right):
    return jnp.dot(left, right, preferred_element_type=F32)


def dot_nt(left, right):
    return lax.dot_general(left, right, (((1,), (1,)), ((), ())), preferred_element_type=F32)


def dot_tn(left, right):
    return lax.dot_general(left, right, (((0,), (0,)), ((), ())), preferred_element_type=F32)


def add_up(target, start, own, own_start, received):
    count = received[0].shape[0]
    step = min(count, BLOCK)

    def body(at, carry):
        at = at * step
        total = own[pl.ds(own_start + at, step)].astype(F32)
        for part in received:
            total = total + part[pl.ds(at, step)].astype(F32)
        target[pl.ds(start + at, step)] = total.astype(BF16)
        return carry

    lax.fori_loop(0, count // step, body, 0)


def wait_bytes(span, sem):
    pltpu.make_async_copy(span, span, sem).wait()


class ConvSummer:
    ORDERS = ("xy", "yx")

    def __init__(self, place, sizes, terms, total, scratch):
        self.place, self.sizes, self.terms, self.total = place, sizes, terms, total
        (
            self.inbox0, self.held1, self.inbox2,
            self.scatter0, self.scatter2,
            self.gather2, self.gather1, self.gather0, self.back, self.sends,
        ) = scratch
        self.unit = PART // (2 * sizes["x"] * sizes["y"] * sizes["z"])
        self.group = self.unit * sizes["z"]
        self.n1 = [sizes[order[0]] for order in self.ORDERS]
        self.n2 = [sizes[order[1]] for order in self.ORDERS]

    def at(self, part, axis):
        return self.place[self.ORDERS[part][axis]]

    def peer(self, part, axis, step):
        return lax.rem(self.at(part, axis) + step, self.sizes[self.ORDERS[part][axis]])

    def device(self, axis, step):
        return along(self.place, axis, step, self.sizes)

    def local(self, part, chunk, group, unit=0):
        span = self.n2[part] * self.group
        return part * (PART // 2) + chunk * span + group * self.group + unit * self.unit

    def tile(self, part, chunk, group, unit=0):
        return self.place["c"] * PART + self.local(part, chunk, group, unit)

    def scatter_first(self, part):
        for step2 in range(self.n2[0]):
            step2 = (step2 + 1) % self.n2[0]
            for step in range(1, self.n1[0]):
                chunk, group = self.peer(part, 0, step), self.peer(part, 1, step2)
                remote(
                    self.terms.at[pl.ds(self.local(part, chunk, group), self.group)],
                    self.inbox0.at[part, group, pl.ds((step - 1) * self.group, self.group)],
                    self.sends.at[part],
                    self.scatter0.at[part, step2],
                    self.device(self.ORDERS[part][0], step),
                )

    def scatter_second(self):
        for step2 in range(self.n2[0]):
            step2 = (step2 + 1) % self.n2[0]
            for part in range(2):
                chunk, group = self.at(part, 0), self.peer(part, 1, step2)
                wait_bytes(self.inbox0.at[part, group], self.scatter0.at[part, step2])
                total = self.terms[pl.ds(self.local(part, chunk, group), self.group)].astype(F32)
                for step in range(self.n1[part] - 1):
                    span = pl.ds(step * self.group, self.group)
                    total = total + self.inbox0[part, group, span].astype(F32)
                held = self.held1.at[part, group]
                held[...] = total.astype(BF16)
                nz = self.sizes["z"]
                for depth in range(nz):
                    if step2 + depth == 0:
                        continue
                    peer = lax.rem(self.place["z"] + depth, nz)
                    slot = step2 * nz + depth - 1
                    remote(
                        held.at[pl.ds(peer * self.unit, self.unit)],
                        self.inbox2.at[part, pl.ds(slot * self.unit, self.unit)],
                        self.sends.at[2],
                        self.scatter2.at[part],
                        aslant(self.place, self.ORDERS[part][1], step2, depth, self.sizes),
                    )

    def gather_third(self):
        for part in range(2):
            wait_bytes(self.inbox2.at[part], self.scatter2.at[part])
            z = self.place["z"]
            own = self.held1[part, self.at(part, 1), pl.ds(z * self.unit, self.unit)].astype(F32)
            others = self.inbox2[part].astype(F32).reshape(-1, self.unit, 16, 128)
            total = own + jnp.sum(others, axis=0)
            mine = self.tile(part, self.at(part, 0), self.at(part, 1), z)
            self.total[pl.ds(mine, self.unit)] = total.astype(BF16)
            span = self.total.at[pl.ds(mine, self.unit)]
            for step in range(1, self.sizes["z"]):
                remote(
                    span, span, self.sends.at[4], self.gather2.at[part], self.device("z", step)
                )

    def spread(self, part, chunk, group, axis, steps, send, sem):
        span = self.total.at[pl.ds(self.tile(part, chunk, group), self.group)]
        for step in steps:
            remote(span, span, self.sends.at[send], sem, self.device(axis, step))

    def gather_rest(self, between):
        n1, n2 = self.n1[0], self.n2[0]
        for part in range(2):
            wait_bytes(
                self.total.at[pl.ds(0, (self.sizes["z"] - 1) * self.unit)], self.gather2.at[part]
            )
            first, second = self.ORDERS[part]
            chunk, group = self.at(part, 0), self.at(part, 1)
            for step in range(1, n2):
                sem = self.gather1.at[part, step]
                self.spread(part, chunk, group, second, [step], 5, sem)
            self.spread(part, chunk, group, first, range(1, n1), 6, self.gather0.at[part, 0])
            self.spread(part, chunk, group, "c", [1], 7, self.back.at[0])
        for step2 in range(1, n2):
            for part in range(2):
                first = self.ORDERS[part][0]
                chunk = self.at(part, 0)
                group = self.peer(part, 1, n2 - step2)
                wait_bytes(self.total.at[pl.ds(0, self.group)], self.gather1.at[part, step2])
                self.spread(
                    part, chunk, group, first, range(1, n1), 6, self.gather0.at[part, step2]
                )
                self.spread(part, chunk, group, "c", [1], 7, self.back.at[0])
        between()
        for step2 in range(n2):
            for part in range(2):
                wait_bytes(
                    self.total.at[pl.ds(0, (n1 - 1) * self.group)], self.gather0.at[part, step2]
                )
                group = self.peer(part, 1, n2 - step2)
                for step in range(1, n1):
                    chunk = self.peer(part, 0, n1 - step)
                    self.spread(part, chunk, group, "c", [1], 7, self.back.at[0])

    def back_wait(self):
        wait_bytes(self.total.at[pl.ds(0, PART)], self.back.at[0])

    def finish(self):
        n1, n2, nz = self.n1[0], self.n2[0], self.sizes["z"]
        counts = (
            n2 * (n1 - 1) * self.group, n2 * (n1 - 1) * self.group, 2 * (n2 * nz - 1) * self.unit,
            0, 2 * (nz - 1) * self.unit, 2 * (n2 - 1) * self.group,
            2 * n2 * (n1 - 1) * self.group, PART,
        )
        for at, count in enumerate(counts):
            if count:
                wait_bytes(self.total.at[pl.ds(0, count)], self.sends.at[at])


def conv_summer_scratch(sizes):
    unit = PART // (2 * sizes["x"] * sizes["y"] * sizes["z"])
    group = unit * sizes["z"]
    n1, n2 = sizes["x"], sizes["y"]
    tiles = [
        (2, n2, (n1 - 1) * group), (2, n2, group),
        (2, (n2 * sizes["z"] - 1) * unit),
    ]
    sems = [(2, n2), (2,), (2,), (2, n2), (2, n2), (1,), (8,)]
    return [pltpu.VMEM(shape + (16, 128), BF16) for shape in tiles] + [
        pltpu.SemaphoreType.DMA(shape) for shape in sems
    ]


class Summer:
    def __init__(self, order, place, sizes, term, total, base, scratch):
        self.order, self.place, self.sizes = order, place, sizes
        self.term, self.total, self.base = term, total, base
        self.core_in, self.held, self.inbox = scratch[0], scratch[1:4], scratch[4:7]
        self.send_sems, self.recv_sems = scratch[7], scratch[8]
        self.spans = [PART // 2]
        for axis in order:
            self.spans.append(self.spans[-1] // sizes[axis])
        self.slot = 0
        self.sent = []
        self.wait = []

    def push(self, source, target, axis, step):
        device = along(self.place, axis, step, self.sizes)
        copy = remote(
            source, target, self.send_sems.at[self.slot], self.recv_sems.at[self.slot], device
        )
        self.slot += 1
        self.sent.append(copy)
        self.wait.append(copy)

    def arrive(self):
        for copy in self.wait:
            copy.wait_recv()
        self.wait = []

    def core_start(self):
        other = self.base + (1 - self.place["c"]) * self.spans[0]
        self.push(self.term.at[pl.ds(other, self.spans[0])], self.core_in, "c", 1)

    def core_end(self):
        self.arrive()
        mine = self.base + self.place["c"] * self.spans[0]
        add_up(self.held[0], 0, self.term, mine, [self.core_in])

    def scatter_start(self, level):
        axis, span = self.order[level], self.spans[level + 1]
        for step in range(1, self.sizes[axis]):
            peer = lax.rem(self.place[axis] + step, self.sizes[axis])
            self.push(
                self.held[level].at[pl.ds(peer * span, span)],
                self.inbox[level].at[step - 1],
                axis,
                step,
            )

    def scatter_end(self, level):
        self.arrive()
        axis, span = self.order[level], self.spans[level + 1]
        received = [self.inbox[level].at[step] for step in range(self.sizes[axis] - 1)]
        mine = self.place[axis] * span
        if level < 2:
            add_up(self.held[level + 1], 0, self.held[level], mine, received)
        else:
            add_up(self.total, self.start_of(3), self.held[level], mine, received)

    def start_of(self, levels):
        start = self.base + self.place["c"] * self.spans[0]
        for level in range(levels):
            start = start + self.place[self.order[level]] * self.spans[level + 1]
        return start

    def gather_start(self, level):
        axis = self.order[level]
        mine = self.total.at[pl.ds(self.start_of(level + 1), self.spans[level + 1])]
        for step in range(1, self.sizes[axis]):
            self.push(mine, mine, axis, step)

    def core_back(self):
        mine = self.total.at[pl.ds(self.start_of(0), self.spans[0])]
        self.push(mine, mine, "c", 1)

    def finish(self):
        for copy in self.sent:
            copy.wait_send()


def summer_scratch(order, sizes):
    spans = [PART // 2]
    for axis in order:
        spans.append(spans[-1] // sizes[axis])
    shapes = [(spans[0], 16, 128)]
    shapes += [(span, 16, 128) for span in spans[:3]]
    shapes += [(sizes[axis] - 1, span, 16, 128) for axis, span in zip(order, spans[1:])]
    copies = 2 * (1 + sum(sizes[axis] - 1 for axis in order))
    return [pltpu.VMEM(shape, BF16) for shape in shapes] + [
        pltpu.SemaphoreType.DMA((copies,)),
        pltpu.SemaphoreType.DMA((copies,)),
    ]


def pack(matrix, tiles, base):
    held = matrix.astype(BF16)
    for block in range(2):
        cut = held[:, block * 128 : block * 128 + 128]
        tiles[pl.ds(base + 20 * block, 20)] = cut.reshape(20, 16, 128)
    low, high = held[:160, 256:], held[160:, 256:]
    tail = jnp.concatenate([low, high], axis=1)
    tiles[pl.ds(base + 40, 10)] = tail.reshape(10, 16, 128)


def pack_half(matrix, tiles, base):
    held = matrix.astype(BF16)
    for block in range(2):
        cut = held[:, block * 128 : block * 128 + 128]
        tiles[pl.ds(base + 10 * block, 10)] = cut.reshape(10, 16, 128)
    tail = jnp.concatenate([held[:80, 256:], held[80:, 256:]], axis=1)
    tiles[pl.ds(base + 20, 5)] = tail.reshape(5, 16, 128)


def unpack_half(tiles, base, target, at, row, factor):
    span = pl.ds(row, HALF_CHAN)
    for block in range(2):
        cut = tiles[pl.ds(base + 10 * block, 10)].reshape(HALF_CHAN, 128)
        target[at, span, block * 128 : block * 128 + 128] = cut.astype(F32) * factor
    tail = tiles[pl.ds(base + 20, 5)].reshape(80, 128).astype(F32) * factor
    target[at, pl.ds(row, 80), 256:] = tail[:, :64]
    target[at, pl.ds(row + 80, 80), 256:] = tail[:, 64:]


def unpack(tiles, base, target, at, factor):
    for block in range(2):
        cut = tiles[pl.ds(base + 20 * block, 20)].reshape(CHAN, 128)
        target[at, :, block * 128 : block * 128 + 128] = cut.astype(F32) * factor
    tail = tiles[pl.ds(base + 40, 10)].reshape(160, 128).astype(F32) * factor
    target[at, :160, 256:] = tail[:, :64]
    target[at, 160:, 256:] = tail[:, 64:]


def finish_kernel(factor, block_in, back_in, conv_in, small_in, *refs):
    (block_out, back_out, conv_out), small_outs, gain_out = refs[:3], refs[3:7], refs[7]
    conv, small, wide, fields, through, load_sems, half_sems, store_sems = refs[8:]
    moves = []
    for at, (source, target) in enumerate(((block_in, block_out), (back_in, back_out))):
        moves.append(
            (
                pltpu.make_async_copy(source, fields.at[at], through.at[at]),
                pltpu.make_async_copy(fields.at[at], target, through.at[at + 2]),
            )
        )
        moves[-1][0].start()

    def load(at, source, target):
        span = pl.ds(at * MATRIX_TILES, MATRIX_TILES)
        return source.at[span], target.at[span]

    for at in range(4):
        pltpu.make_async_copy(*load(at, small_in, small), load_sems.at[9 + at]).start()
    def load_half(at, core):
        span = pl.ds(core * PART + at * HALF_TILES, HALF_TILES)
        return pltpu.make_async_copy(conv_in.at[span], conv.at[span], half_sems.at[at, core])

    for at in range(9):
        for core in range(2):
            load_half(at, core).start()
    gain_loads = []
    for core in range(2):
        span = pl.ds(core * PART + GAIN_TILE, 2)
        gain_loads.append(
            pltpu.make_async_copy(conv_in.at[span], conv.at[span], half_sems.at[9, core])
        )
        gain_loads[-1].start()
    for at in range(4):
        pltpu.make_async_copy(*load(at, small_in, small), load_sems.at[9 + at]).wait()
        unpack(small, at * MATRIX_TILES, wide, 9 + at, factor)
        pltpu.make_async_copy(wide.at[9 + at], small_outs[at], store_sems.at[9 + at]).start()

    def conv_tap(at, carry):
        for core in range(2):
            load_half(at, core).wait()
            start = core * PART + at * HALF_TILES
            unpack_half(conv, start, wide, at, core * HALF_CHAN, factor)
        pltpu.make_async_copy(wide.at[at], conv_out.at[at], store_sems.at[at]).start()
        return carry

    for move in moves:
        move[0].wait()
        move[1].start()
    lax.fori_loop(0, 9, conv_tap, 0)
    for copy in gain_loads:
        copy.wait()
    pieces = []
    for at in range(2):
        tiles = [conv[core * PART + GAIN_TILE + at].astype(F32) for core in range(2)]
        pieces.append((tiles[0] + tiles[1]) * factor)
    gain_out[0:128] = pieces[0][0]
    gain_out[128:256] = pieces[0][1]
    gain_out[256:] = pieces[1][0, :64]
    for move in moves:
        move[1].wait()
    for at in range(9):
        pltpu.make_async_copy(wide.at[at], conv_out.at[at], store_sems.at[at]).wait()
    for at in range(4):
        pltpu.make_async_copy(wide.at[9 + at], small_outs[at], store_sems.at[9 + at]).wait()


def shifts(cells):
    column = lax.broadcasted_iota(jnp.int32, cells.shape, 0)
    left = jnp.where(column == 0, 0.0, pltpu.roll(cells, 1, 0))
    right = jnp.where(column == COLS - 1, 0.0, pltpu.roll(cells, COLS - 1, 0))
    return [left, cells, right]


class Swap:
    def __init__(self, source, target, send_sems, recv_sems, peers, me):
        self.source, self.target, self.peers, self.me = source, target, peers, me
        self.send_sems, self.recv_sems = send_sems, recv_sems

    def start(self, half):
        for frame, device in self.peers:
            remote(
                self.source.at[half, frame],
                self.target.at[half, self.me],
                self.send_sems.at[half],
                self.recv_sems.at[half],
                device,
            )
        self.target[half, self.me] = self.source[half, self.me]

    def wait(self, half):
        span = self.target.at[half, pl.ds(0, len(self.peers))]
        pltpu.make_async_copy(span, span, self.recv_sems.at[half]).wait()

    def finish(self):
        for half in range(2):
            span = self.source.at[half, pl.ds(0, len(self.peers))]
            pltpu.make_async_copy(span, span, self.send_sems.at[half]).wait()


def norm_of(resid):
    return lax.rsqrt(jnp.mean(resid * resid, axis=-1, keepdims=True) + EPS)


def cell_start(half, at):
    if half == 0:
        return COLS + at * 64
    return jnp.where(at < 2, at * 64, HALF + at * 64)


def head_masks():
    low = lax.broadcasted_iota(jnp.int32, (1, 128), 1) < 64
    return low, [jnp.where(low, 0.125, 0.0).astype(BF16), jnp.where(low, 0.0, 0.125).astype(BF16)]


def attend(q_s, k_s, v_s, bias, probs_s, mixed_s):
    low, masks = head_masks()

    def tile(at, masks):
        start = at * 128
        span = pl.ds(start if isinstance(at, int) else pl.multiple_of(start, 128), 128)
        queries, keys, values = q_s[:, span], k_s[:, span], v_s[:, span]
        found = []
        for head, mask in enumerate(masks):
            scores = dot_nt(keys, queries * mask) + bias[...]
            expo = jnp.exp(scores)
            probs = expo * (1.0 / jnp.sum(expo, axis=0, keepdims=True))
            probs_s[2 * at + head] = probs
            found.append(dot_tn(probs.astype(BF16), values))
        total = found[0] if len(found) == 1 else jnp.where(low, *found)
        mixed_s[:, span] = total.astype(BF16)

    def pair(at, carry):
        tile(at, masks)
        return carry

    lax.fori_loop(0, 2, pair, 0)
    tile(2, masks[:1])


def attend_back(q_s, k_s, v_s, d_s, probs_s, qp_s, kp_s, vp_s):
    low, masks = head_masks()

    def tile(at, masks):
        start = at * 128
        span = pl.ds(start if isinstance(at, int) else pl.multiple_of(start, 128), 128)
        queries, keys, values, grads = q_s[:, span], k_s[:, span], v_s[:, span], d_s[:, span]
        found = []
        for head, mask in enumerate(masks):
            probs = probs_s[2 * at + head]
            prob_grad = dot_nt(values, grads * mask)
            inner = jnp.sum(probs * prob_grad, axis=0, keepdims=True)
            score_b = (probs * (prob_grad - inner)).astype(BF16)
            found.append(
                (
                    dot_tn(score_b, keys),
                    dot(score_b, queries),
                    dot(probs.astype(BF16), grads),
                )
            )
        for place, target in enumerate((qp_s, kp_s, vp_s)):
            parts = [part[place] for part in found]
            total = parts[0] if len(parts) == 1 else jnp.where(low, *parts)
            target[:, span] = total.astype(BF16)

    def pair(at, carry):
        tile(at, masks)
        return carry

    lax.fori_loop(0, 2, pair, 0)
    tile(2, masks[:1])


def block_kernel(sizes, latents, conv_w, query_w, key_w, value_w, out_w, gain, out_grad, *refs):
    (block_hbm, back_hbm, conv_hbm, small_hbm), refs = refs[:4], refs[4:]
    (
        lat_in, grad_in, lat, grad, weights, wq, wk, wv, wo, gain_v, in_sems,
        padded, wide, halo, halo_send, halo_recv, acc, resid, act_c, act_in, act_t,
        normed_out, normed_in, og_out, og_in, ng_out, ng_in, mix_out, mix_in,
        swap_send, swap_recv,
        og_n, normed_n, mixed_n, back_n,
        q_s, k_s, v_s, d_s, bias, probs_s, out_acc, mixed_s, qp_s, kp_s, vp_s, parts, flip,
        resid_grad, rg_in, conv_acc, pair_send, pair_recv, grad_pad, gain_acc, conv_terms, small_terms,
        block_out, latents_grad, conv_total, small_total, out_sems,
    ), refs = refs[:62], refs[62:]
    frames = lax.axis_size("frame")
    rows_n = lax.axis_size("row")
    chunk = HALF // frames
    me, row = lax.axis_index("frame"), lax.axis_index("row")
    place = my_place()
    peers = []
    for step in range(1, frames):
        frame = lax.rem(me + step, frames)
        peers.append((frame, (frame, row)))
    above = (me, lax.rem(row + rows_n - 1, rows_n))
    below = (me, lax.rem(row + 1, rows_n))

    barrier = pltpu.get_barrier_semaphore()
    partners = [device for _, device in peers] + [above, below]
    for axis in "cxy":
        partners += [along(place, axis, step, sizes) for step in range(1, sizes[axis])]
    for axis in "xy":
        for step in range(1, sizes[axis]):
            partners += [
                aslant(place, axis, step, depth, sizes) for depth in range(1, sizes["z"])
            ]
    for device in partners:
        pl.semaphore_signal(barrier, inc=1, device_id=device, device_id_type=MESH)

    loads = []
    pairs = (
        (latents, lat_in), (out_grad, grad_in), (conv_w, weights), (gain, gain_v),
        (out_w, wo), (query_w, wq), (key_w, wk), (value_w, wv),
    )
    for at, (source, target) in enumerate(pairs):
        loads.append(pltpu.make_async_copy(source, target, in_sems.at[at]))
        loads[-1].start()

    loads[0].wait()

    def activate(at, carry):
        span = pl.ds(at * COLS, COLS)
        cells = lat_in[at].astype(F32).T
        lat[span] = cells.astype(BF16)
        act = (cells * jax.nn.sigmoid(cells)).astype(BF16).astype(F32)
        span = pl.ds((at + 1) * COLS, COLS)
        for shift, copy in enumerate(shifts(act)):
            wide[span, shift * CHAN : shift * CHAN + CHAN] = copy.astype(BF16)
        padded[span] = act.astype(BF16)
        return carry

    lax.fori_loop(0, ROWS, activate, 0)
    loads[1].wait()

    def flip_grad(at, carry):
        cells = grad_in[at].astype(F32).T.astype(BF16)
        grad[pl.ds(at * COLS, COLS)] = cells
        half = jnp.where((at == 0) | (at == ROWS - 1), 1, 0)
        span = pl.ds(jnp.where(at >= 2, frames // 2, 0), frames // 2)
        og_out[half, span] = cells[:, :256].reshape(frames // 2, chunk, 256)
        normed_out[half, span, :, CHAN:] = cells[:, 256:].reshape(frames // 2, chunk, 64)
        return carry

    lax.fori_loop(0, ROWS, flip_grad, 0)
    pl.semaphore_wait(barrier, len(partners))

    def halo_start(source, kind):
        return [
            remote(source.at[pl.ds(COLS, COLS)], halo.at[kind, 1],
                   halo_send.at[kind, 0], halo_recv.at[kind, 0], above),
            remote(source.at[pl.ds(ROWS * COLS, COLS)], halo.at[kind, 0],
                   halo_send.at[kind, 1], halo_recv.at[kind, 1], below),
        ]

    def halo_end(copies, kind, store):
        for copy in copies:
            copy.wait_recv()
        ends = (row > 0, row < rows_n - 1)
        for side, inside in enumerate(ends):
            keep = jnp.where(inside, 1.0, 0.0).astype(F32)
            cells = halo[kind, side].astype(F32) * keep
            store(pl.ds(side * (ROWS + 1) * COLS, COLS), cells)

    def store_act(span, cells):
        for shift, copy in enumerate(shifts(cells)):
            wide[span, shift * CHAN : shift * CHAN + CHAN] = copy.astype(BF16)
        padded[span] = cells.astype(BF16)

    def store_grad(span, cells):
        for shift, copy in enumerate(shifts(cells)):
            grad_pad[shift, span] = copy.astype(BF16)

    act_halo = halo_start(padded, 0)

    swaps = []
    buffers = ((og_out, og_in), (normed_out, normed_in), (ng_out, ng_in), (mix_out, mix_in))
    for at, (source, target) in enumerate(buffers):
        swaps.append(Swap(source, target, swap_send.at[at], swap_recv.at[at], peers, me))
    og_swap, normed_swap, ng_swap, mix_swap = swaps

    loads[2].wait()
    loads[3].wait()

    def conv_half(half):
        total = None
        for a in range(3):
            if half == 0:
                cells = wide[(a + 1) * COLS : (a + 1) * COLS + HALF]
            else:
                cells = jnp.concatenate(
                    [wide[a * COLS : (a + 1) * COLS], wide[(a + 3) * COLS : (a + 4) * COLS]]
                )
            term = dot(cells, weights[3 * a : 3 * a + 3].reshape(3 * CHAN, CHAN))
            total = term if total is None else total + term
        acc[pl.ds(0, HALF)] = total
        count = 64 // chunk

        def finish(at, carry):
            cells = lat[pl.ds(pl.multiple_of(cell_start(half, at), 64), 64)].astype(F32)
            held = (cells + acc[pl.ds(at * 64, 64)]).astype(BF16)
            resid[half, pl.ds(at * 64, 64)] = held
            held = held.astype(F32)
            normed = (held * norm_of(held) * gain_v[...].reshape(1, CHAN)).astype(BF16)
            normed_out[half, pl.ds(at * count, count), :, :CHAN] = normed.reshape(count, chunk, CHAN)
            return carry

        lax.fori_loop(0, 4, finish, 0)

    og_swap.start(0)
    conv_half(0)
    normed_swap.start(0)
    halo_end(act_halo, 0, store_act)
    conv_half(1)
    normed_swap.start(1)
    og_swap.start(1)

    position = lax.broadcasted_iota(jnp.int32, (HALF, HALF), 0)
    other = lax.broadcasted_iota(jnp.int32, (HALF, HALF), 1)
    same = lax.rem(position, chunk) == lax.rem(other, chunk)
    bias[...] = jnp.where(same, 0.0, -1e30)
    for field in (q_s, k_s, v_s, d_s):
        field[:, 256:] = jnp.zeros((HALF, 128), BF16)
    act_c[...] = padded[...].astype(F32).T.astype(BF16)
    core = place["c"]
    partner = along(place, "c", 1, sizes)
    mine = pl.ds(pl.multiple_of(core * HALF_CHAN, HALF_CHAN), HALF_CHAN)
    theirs = pl.ds(pl.multiple_of((1 - core) * HALF_CHAN, HALF_CHAN), HALF_CHAN)
    pair = [remote(act_c.at[theirs], act_in, pair_send.at[0], pair_recv.at[0], partner)]

    def shift_lanes(at, carry, source, side):
        span = pl.ds(pl.multiple_of(at * COLS, COLS), COLS)
        cells = source[:, span].astype(F32)
        column = lax.broadcasted_iota(jnp.int32, cells.shape, 1)
        left = jnp.where(column == 0, 0.0, pltpu.roll(cells, 1, 1))
        right = jnp.where(column == COLS - 1, 0.0, pltpu.roll(cells, COLS - 1, 1))
        for shift, copy in enumerate((left, cells, right)):
            act_t[side, shift * HALF_CHAN : (shift + 1) * HALF_CHAN, span] = copy.astype(BF16)
        return carry

    own_rows = functools.partial(shift_lanes, source=act_c.at[mine], side=0)
    lax.fori_loop(0, ROWS + 2, own_rows, 0)
    for load in loads[4:]:
        load.wait()

    for half in range(2):
        normed_swap.wait(half)
        arrived = normed_in[half].reshape(HALF, WIDE)
        normed_n[half] = arrived[:, :CHAN]
        og_n[half, :, 256:] = arrived[:, CHAN:]
        q_s[:, :CHAN] = dot(normed_n[half], wq[...]).astype(BF16)
        k_s[:, :CHAN] = dot(normed_n[half], wk[...]).astype(BF16)
        v_s[:, :CHAN] = dot(normed_n[half], wv[...]).astype(BF16)
        attend(q_s, k_s, v_s, bias, probs_s, mixed_s)
        mixed_n[half] = mixed_s[:, :CHAN]
        mix_out[half] = mixed_s[:, :256].reshape(frames, chunk, 256)
        ng_out[half, :, :, CHAN:] = mixed_s[:, 256:CHAN].reshape(frames, chunk, 64)
        og_swap.wait(half)
        og_n[half, :, :256] = og_in[half].reshape(HALF, 256)
        d_s[:, :CHAN] = dot_nt(og_n[half], wo[...]).astype(BF16)
        attend_back(q_s, k_s, v_s, d_s, probs_s, qp_s, kp_s, vp_s)
        back = dot_nt(qp_s[:, :CHAN], wq[...])
        back = back + dot_nt(kp_s[:, :CHAN], wk[...])
        back = back + dot_nt(vp_s[:, :CHAN], wv[...])
        ng_out[half, :, :, :CHAN] = back.astype(BF16).reshape(frames, chunk, CHAN)
        ng_swap.start(half)
        for at, field in enumerate((qp_s, kp_s, vp_s)):
            parts[at, pl.ds(half * HALF, HALF)] = field[:, :CHAN]

    flip[0] = normed_n[...].reshape(2 * HALF, CHAN).astype(F32).T.astype(BF16)
    flip[1] = mixed_n[...].reshape(2 * HALF, CHAN).astype(F32).T.astype(BF16)
    for at in range(3):
        pack(dot(flip[0], parts[at]), small_terms, at * MATRIX_TILES)
    pack(dot(flip[1], og_n[...].reshape(2 * HALF, CHAN)), small_terms, 3 * MATRIX_TILES)
    spare = SMALL_TILES - 4 * MATRIX_TILES
    small_terms[pl.ds(4 * MATRIX_TILES, spare)] = jnp.zeros((spare, 16, 128), BF16)

    conv = ConvSummer(place, sizes, conv_terms, conv_total, refs[9:])
    small = Summer("yxz", place, sizes, small_terms, small_total, 0, refs[:9])
    small.core_start()

    gain_acc[...] = jnp.zeros((8, CHAN), F32)
    for half in range(2):
        ng_swap.wait(half)

        def undo_norm(at, carry, half=half):
            count = 64 // chunk
            begin = pl.multiple_of(cell_start(half, at), 64)
            held = resid[half, pl.ds(at * 64, 64)].astype(F32)
            back = ng_in[half, pl.ds(at * count, count), :, :CHAN].reshape(64, CHAN).astype(F32)
            inv = norm_of(held)
            product = back * held
            total = jnp.sum((product * inv).reshape(8, 8, CHAN), axis=0)
            gain_acc[...] += total
            tangent = back * gain_v[...].reshape(1, CHAN)
            mean = jnp.mean(product * gain_v[...].reshape(1, CHAN), axis=-1, keepdims=True)
            value = grad[pl.ds(begin, 64)].astype(F32) + (
                inv * tangent - held * (inv * inv * inv) * mean
            )
            resid_grad[half, pl.ds(at * 64, 64)] = value.astype(BF16)
            return carry

        lax.fori_loop(0, 4, undo_norm, 0)
        pair.append(
            remote(
                resid_grad.at[half],
                rg_in.at[half],
                pair_send.at[1 + half],
                pair_recv.at[1 + half],
                partner,
            )
        )
        if half == 0:
            pair[0].wait_recv()
            other_rows = functools.partial(shift_lanes, source=act_in, side=1)
            lax.fori_loop(0, ROWS + 2, other_rows, 0)

            def inner_taps(at, carry, side, cells):
                span = pl.ds(pl.multiple_of((at + 1) * COLS, COLS), HALF)
                total = dot(act_t[side, :, span], cells[0])
                if side == 0:
                    conv_acc[at] = total
                else:
                    conv_acc[at] += total
                return carry

            lax.fori_loop(
                0, 3, functools.partial(inner_taps, side=0, cells=resid_grad), 0
            )
            small.core_end()
            small.scatter_start(0)
            pair[1].wait_recv()
            lax.fori_loop(0, 3, functools.partial(inner_taps, side=1, cells=rg_in), 0)
        else:
            mix_swap.start(0)
            mix_swap.start(1)


    def pad_grad(at, carry):
        half = jnp.where((at == 0) | (at == ROWS - 1), 1, 0)
        side = jnp.where(at >= 2, 1, 0)
        cells = resid_grad[half, pl.ds(side * COLS, COLS)].astype(F32)
        for shift, copy in enumerate(shifts(cells)):
            grad_pad[shift, pl.ds((at + 1) * COLS, COLS)] = copy.astype(BF16)
        return carry

    def edge_cells(side, at):
        spans = [pl.ds(pl.multiple_of((at + gap) * COLS, COLS), COLS) for gap in (0, ROWS - 1)]
        return jnp.concatenate([act_t[side, :, span] for span in spans], axis=1)

    def second_taps(at, carry):
        conv_acc[at] += dot(edge_cells(0, at), resid_grad[1])
        return carry

    lax.fori_loop(0, 3, second_taps, 0)
    lax.fori_loop(0, ROWS, pad_grad, 0)
    grad_halo = halo_start(grad_pad.at[1], 1)

    spare = PART - 9 * HALF_TILES
    conv_terms[pl.ds(9 * HALF_TILES, spare)] = jnp.zeros((spare, 16, 128), BF16)
    gains = jnp.sum(gain_acc[...], axis=0, keepdims=True)
    line = lax.broadcasted_iota(jnp.int32, (16, 128), 0)
    gain_tile = jnp.where(line == 0, gains[:, :128], jnp.where(line == 1, gains[:, 128:256], 0.0))
    conv_terms[GAIN_TILE] = gain_tile.astype(BF16)
    tail = jnp.where(line[:, :64] == 0, gains[:, 256:], 0.0)
    conv_terms[GAIN_TILE + 1, :, :64] = tail.astype(BF16)
    pair[2].wait_recv()

    def last_taps(at, carry):
        total = conv_acc[at] + dot(edge_cells(1, at), rg_in[1])
        for b in range(3):
            part = total[b * HALF_CHAN : (b + 1) * HALF_CHAN]
            pack_half(part, conv_terms, (at * 3 + b) * HALF_TILES)
        return carry

    lax.fori_loop(0, 2, last_taps, 0)
    conv.scatter_first(0)
    lax.fori_loop(2, 3, last_taps, 0)
    conv.scatter_first(1)
    small.scatter_end(0)
    small.scatter_start(1)

    def project_out(half):
        mix_swap.wait(half)
        back_n[:, :256] = mix_in[half].reshape(HALF, 256)
        back_n[:, 256:] = ng_in[half, :, :, CHAN:].reshape(HALF, 64)
        out_acc[...] = dot(back_n[...], wo[...])

        def write_out(at, carry):
            held = resid[half, pl.ds(at * COLS, COLS)].astype(F32)
            total = held + out_acc[pl.ds(at * COLS, COLS)]
            block_out[at + 1 if half == 0 else at * 3] = total.T.astype(BF16)
            return carry

        lax.fori_loop(0, 2, write_out, 0)

    halo_end(grad_halo, 1, store_grad)
    acc[...] = jnp.zeros((2 * HALF, CHAN), F32)

    def back_tap(at, carry):
        a, b = at // 3, lax.rem(at, 3)
        cells = grad_pad[2 - b, pl.ds((2 - a) * COLS, ROWS * COLS)]
        acc[...] += dot_nt(cells, weights[at])
        return carry

    lax.fori_loop(0, 3, back_tap, 0)
    small.scatter_end(1)
    small.scatter_start(2)
    lax.fori_loop(3, 5, back_tap, 0)
    conv.scatter_second()
    small.scatter_end(2)
    small.gather_start(2)
    stores = []

    def store(source, target):
        stores.append(pltpu.make_async_copy(source, target, out_sems.at[len(stores)]))
        stores[-1].start()

    project_out(0)
    project_out(1)
    store(block_out, block_hbm)
    small.arrive()
    small.gather_start(1)
    lax.fori_loop(5, 9, back_tap, 0)
    conv.gather_third()
    small.arrive()
    small.gather_start(0)
    def write_back(at, carry):
        cells = lat[pl.ds(at * COLS, COLS)].astype(F32)
        sigma = jax.nn.sigmoid(cells)
        slope = sigma * (1.0 + cells * (1.0 - sigma))
        half = jnp.where((at == 0) | (at == ROWS - 1), 1, 0)
        side = jnp.where(at >= 2, 1, 0)
        value = resid_grad[half, pl.ds(side * COLS, COLS)].astype(F32) + acc[pl.ds(at * COLS, COLS)] * slope
        latents_grad[at] = value.T.astype(BF16)
        return carry

    lax.fori_loop(0, ROWS, write_back, 0)
    store(latents_grad, back_hbm)
    def return_small():
        small.arrive()
        small.core_back()

    conv.gather_rest(return_small)
    own_half = pl.ds(place["c"] * PART, PART)
    store(conv_total.at[own_half], conv_hbm.at[own_half])
    small.arrive()
    store(small_total, small_hbm)
    conv.back_wait()
    other_half = pl.ds((1 - place["c"]) * PART, PART)
    store(conv_total.at[other_half], conv_hbm.at[other_half])
    small.finish()
    conv.finish()
    for swap in swaps:
        swap.finish()
    for copy in act_halo + grad_halo + pair:
        copy.wait_send()
    for copy in stores:
        copy.wait()


def block_scratch(sizes, frames):
    narrow, wide = (2, frames, HALF // frames, 256), (2, frames, HALF // frames, WIDE)
    vmem = pltpu.VMEM
    dma = pltpu.SemaphoreType.DMA
    weight = vmem((CHAN, CHAN), BF16)
    shapes = [
        vmem((ROWS, CHAN, COLS), BF16), vmem((ROWS, CHAN, COLS), BF16),
        vmem((ROWS * COLS, CHAN), BF16), vmem((ROWS * COLS, CHAN), BF16),
        vmem((9, CHAN, CHAN), BF16), weight, weight, weight, weight, vmem((CHAN,), F32), dma((8,)),
        vmem(((ROWS + 2) * COLS, CHAN), BF16), vmem(((ROWS + 2) * COLS, 3 * CHAN), BF16),
        vmem((2, 2, COLS, CHAN), BF16),
        dma((2, 2)), dma((2, 2)), vmem((2 * HALF, CHAN), F32), vmem((2, HALF, CHAN), BF16),
        vmem((CHAN, (ROWS + 2) * COLS), BF16), vmem((HALF_CHAN, (ROWS + 2) * COLS), BF16),
        vmem((2, 3 * HALF_CHAN, (ROWS + 2) * COLS), BF16),
    ]
    shapes += [vmem(shape, BF16) for shape in (wide, wide, narrow, narrow, wide, wide, narrow, narrow)]
    shapes += [dma((4, 2)), dma((4, 2))]
    shapes += [vmem((2, HALF, CHAN), BF16)] * 3 + [vmem((HALF, CHAN), BF16)]
    shapes += [vmem((HALF, WIDE), BF16)] * 4 + [vmem((HALF, HALF), F32)]
    shapes += [vmem((5, HALF, HALF), F32), vmem((HALF, CHAN), F32)]
    shapes += [vmem((HALF, WIDE), BF16)] * 4
    shapes += [vmem((3, 2 * HALF, CHAN), BF16), vmem((2, CHAN, 2 * HALF), BF16)]
    shapes += [vmem((2, HALF, CHAN), BF16), vmem((2, HALF, CHAN), BF16)]
    shapes += [vmem((3, 3 * HALF_CHAN, CHAN), F32), dma((3,)), dma((3,))]
    shapes += [vmem((3, (ROWS + 2) * COLS, CHAN), BF16)]
    shapes += [vmem((8, CHAN), F32)]
    shapes += [vmem((PART, 16, 128), BF16), vmem((SMALL_TILES, 16, 128), BF16)]
    shapes += [vmem((ROWS, CHAN, COLS), BF16)] * 2
    shapes += [vmem((CONV_TILES, 16, 128), BF16), vmem((SMALL_TILES, 16, 128), BF16), dma((5,))]
    return shapes + summer_scratch("yxz", sizes) + conv_summer_scratch(sizes)


def on_device(
    latents, conv_weight, query_weight, key_weight, value_weight, out_weight, norm_gain, out_grad
):
    sizes = chip_sizes()
    frames = lax.axis_size("frame")
    anywhere = pl.BlockSpec(memory_space=pl.ANY)
    inside = pl.BlockSpec(memory_space=pltpu.VMEM)
    field = jax.ShapeDtypeStruct((ROWS, CHAN, COLS), BF16)
    block_out, latents_grad, conv_sum, small_sum = pl.pallas_call(
        functools.partial(block_kernel, sizes),
        out_shape=[
            field,
            field,
            jax.ShapeDtypeStruct((CONV_TILES, 16, 128), BF16),
            jax.ShapeDtypeStruct((SMALL_TILES, 16, 128), BF16),
        ],
        in_specs=[anywhere] * 8,
        out_specs=[anywhere] * 4,
        scratch_shapes=block_scratch(sizes, frames),
        compiler_params=pltpu.CompilerParams(
            collective_id=0, has_side_effects=True, vmem_limit_bytes=56 << 20
        ),
    )(
        jnp.swapaxes(latents[0], 1, 2),
        conv_weight.reshape(9, CHAN, CHAN),
        query_weight,
        key_weight,
        value_weight,
        out_weight,
        norm_gain,
        jnp.swapaxes(out_grad[0], 1, 2),
    )
    factor = (ROWS * COLS * frames * lax.axis_size("row")) ** (-0.5)
    weight = jax.ShapeDtypeStruct((CHAN, CHAN), F32)
    outs = pl.pallas_call(
        functools.partial(finish_kernel, factor),
        out_shape=[
            field,
            field,
            jax.ShapeDtypeStruct((9, CHAN, CHAN), F32),
            weight,
            weight,
            weight,
            weight,
            jax.ShapeDtypeStruct((CHAN,), F32),
        ],
        in_specs=[anywhere] * 4,
        out_specs=[anywhere] * 7 + [inside],
        scratch_shapes=[
            pltpu.VMEM((CONV_TILES, 16, 128), BF16),
            pltpu.VMEM((SMALL_TILES, 16, 128), BF16),
            pltpu.VMEM((13, CHAN, CHAN), F32),
            pltpu.VMEM((2, ROWS, CHAN, COLS), BF16),
            pltpu.SemaphoreType.DMA((4,)),
            pltpu.SemaphoreType.DMA((13,)),
            pltpu.SemaphoreType.DMA((10, 2)),
            pltpu.SemaphoreType.DMA((13,)),
        ],
        compiler_params=pltpu.CompilerParams(vmem_limit_bytes=56 << 20),
    )(block_out, latents_grad, conv_sum, small_sum)
    return (
        jnp.swapaxes(outs[0], 1, 2)[None],
        jnp.swapaxes(outs[1], 1, 2)[None],
        outs[2].reshape(3, 3, CHAN, CHAN),
        *outs[3:7],
        outs[7],
    )


def solution(mesh):
    split = P("frame", "row", None, None)
    return jax.shard_map(
        on_device,
        mesh=mesh,
        in_specs=(split, P(), P(), P(), P(), P(), P(), split),
        out_specs=(split, split, P(), P(), P(), P(), P(), P()),
        check_vma=False,
    )
```

```python
import functools

import jax
import jax.numpy as jnp
from jax import lax
from jax.experimental import pallas as pl
from jax.experimental.pallas import tpu as pltpu
from jax.sharding import PartitionSpec as P

EPS = 1e-06
MESH = pl.DeviceIdType.MESH
CHAN = 320
WIDE = 384
COLS = 128
ROWS = 4
HALF = 256
CONV_TILES = 512
SMALL_TILES = 256
PART = 256
MATRIX_TILES = 50
GAIN_TILE = 230
HALF_CHAN = 160
HALF_TILES = 25
BLOCK = 16
F32 = jnp.float32
BF16 = jnp.bfloat16


def chip_sizes():
    return {"c": 2, "x": 4, "y": lax.axis_size("row") // 4, "z": lax.axis_size("frame") // 2}


def my_place():
    frame, row = lax.axis_index("frame"), lax.axis_index("row")
    return {
        "z": frame // 2,
        "x": lax.rem(row // 2, 2) * 2 + lax.rem(frame, 2),
        "y": row // 4,
        "c": lax.rem(row, 2),
    }


def device_of(place):
    return (
        place["z"] * 2 + lax.rem(place["x"], 2),
        (place["y"] * 2 + place["x"] // 2) * 2 + place["c"],
    )


def along(place, axis, step, sizes):
    moved = dict(place)
    moved[axis] = lax.rem(place[axis] + step, sizes[axis])
    return device_of(moved)


def remote(source, target, send_sem, recv_sem, device):
    copy = pltpu.make_async_remote_copy(
        src_ref=source,
        dst_ref=target,
        send_sem=send_sem,
        recv_sem=recv_sem,
        device_id=device,
        device_id_type=MESH,
    )
    copy.start()
    return copy


def dot(left, right):
    return jnp.dot(left, right, preferred_element_type=F32)


def dot_nt(left, right):
    return lax.dot_general(left, right, (((1,), (1,)), ((), ())), preferred_element_type=F32)


def dot_tn(left, right):
    return lax.dot_general(left, right, (((0,), (0,)), ((), ())), preferred_element_type=F32)


def add_up(target, start, own, own_start, received):
    count = received[0].shape[0]
    step = min(count, BLOCK)

    def body(at, carry):
        at = at * step
        total = own[pl.ds(own_start + at, step)].astype(F32)
        for part in received:
            total = total + part[pl.ds(at, step)].astype(F32)
        target[pl.ds(start + at, step)] = total.astype(BF16)
        return carry

    lax.fori_loop(0, count // step, body, 0)


def wait_bytes(span, sem):
    pltpu.make_async_copy(span, span, sem).wait()


class ConvSummer:
    ORDERS = ("xy", "yx")

    def __init__(self, place, sizes, terms, total, scratch):
        self.place, self.sizes, self.terms, self.total = place, sizes, terms, total
        (
            self.inbox0, self.held1, self.inbox1, self.held2, self.inbox2,
            self.scatter0, self.scatter1, self.scatter2,
            self.gather2, self.gather1, self.gather0, self.back, self.sends,
        ) = scratch
        self.unit = PART // (2 * sizes["x"] * sizes["y"] * sizes["z"])
        self.group = self.unit * sizes["z"]
        self.n1 = [sizes[order[0]] for order in self.ORDERS]
        self.n2 = [sizes[order[1]] for order in self.ORDERS]

    def at(self, part, axis):
        return self.place[self.ORDERS[part][axis]]

    def peer(self, part, axis, step):
        return lax.rem(self.at(part, axis) + step, self.sizes[self.ORDERS[part][axis]])

    def device(self, axis, step):
        return along(self.place, axis, step, self.sizes)

    def local(self, part, chunk, group, unit=0):
        span = self.n2[part] * self.group
        return part * (PART // 2) + chunk * span + group * self.group + unit * self.unit

    def tile(self, part, chunk, group, unit=0):
        return self.place["c"] * PART + self.local(part, chunk, group, unit)

    def scatter_first(self, part):
        for step2 in range(self.n2[0]):
            step2 = (step2 + 1) % self.n2[0]
            for step in range(1, self.n1[0]):
                chunk, group = self.peer(part, 0, step), self.peer(part, 1, step2)
                remote(
                    self.terms.at[pl.ds(self.local(part, chunk, group), self.group)],
                    self.inbox0.at[part, group, pl.ds((step - 1) * self.group, self.group)],
                    self.sends.at[part],
                    self.scatter0.at[part, step2],
                    self.device(self.ORDERS[part][0], step),
                )

    def scatter_second(self):
        for step2 in range(self.n2[0]):
            step2 = (step2 + 1) % self.n2[0]
            for part in range(2):
                chunk, group = self.at(part, 0), self.peer(part, 1, step2)
                wait_bytes(self.inbox0.at[part, group], self.scatter0.at[part, step2])
                total = self.terms[pl.ds(self.local(part, chunk, group), self.group)].astype(F32)
                for step in range(self.n1[part] - 1):
                    span = pl.ds(step * self.group, self.group)
                    total = total + self.inbox0[part, group, span].astype(F32)
                held = self.held1.at[part, group]
                held[...] = total.astype(BF16)
                if step2 > 0:
                    remote(
                        held,
                        self.inbox1.at[part, pl.ds((step2 - 1) * self.group, self.group)],
                        self.sends.at[2],
                        self.scatter1.at[part],
                        self.device(self.ORDERS[part][1], step2),
                    )

    def scatter_third(self):
        for part in range(2):
            wait_bytes(self.inbox1.at[part], self.scatter1.at[part])
            total = self.held1[part, self.at(part, 1)].astype(F32)
            for step in range(self.n2[part] - 1):
                total = total + self.inbox1[part, pl.ds(step * self.group, self.group)].astype(F32)
            self.held2[part] = total.astype(BF16)
            for step in range(1, self.sizes["z"]):
                peer = lax.rem(self.place["z"] + step, self.sizes["z"])
                remote(
                    self.held2.at[part, pl.ds(peer * self.unit, self.unit)],
                    self.inbox2.at[part, pl.ds((step - 1) * self.unit, self.unit)],
                    self.sends.at[3],
                    self.scatter2.at[part],
                    self.device("z", step),
                )

    def gather_third(self):
        for part in range(2):
            wait_bytes(self.inbox2.at[part], self.scatter2.at[part])
            z = self.place["z"]
            total = self.held2[part, pl.ds(z * self.unit, self.unit)].astype(F32)
            for step in range(self.sizes["z"] - 1):
                total = total + self.inbox2[part, pl.ds(step * self.unit, self.unit)].astype(F32)
            mine = self.tile(part, self.at(part, 0), self.at(part, 1), z)
            self.total[pl.ds(mine, self.unit)] = total.astype(BF16)
            span = self.total.at[pl.ds(mine, self.unit)]
            for step in range(1, self.sizes["z"]):
                remote(
                    span, span, self.sends.at[4], self.gather2.at[part], self.device("z", step)
                )

    def spread(self, part, chunk, group, axis, steps, send, sem):
        span = self.total.at[pl.ds(self.tile(part, chunk, group), self.group)]
        for step in steps:
            remote(span, span, self.sends.at[send], sem, self.device(axis, step))

    def gather_rest(self, between):
        n1, n2 = self.n1[0], self.n2[0]
        for part in range(2):
            wait_bytes(
                self.total.at[pl.ds(0, (self.sizes["z"] - 1) * self.unit)], self.gather2.at[part]
            )
            first, second = self.ORDERS[part]
            chunk, group = self.at(part, 0), self.at(part, 1)
            for step in range(1, n2):
                sem = self.gather1.at[part, step]
                self.spread(part, chunk, group, second, [step], 5, sem)
            self.spread(part, chunk, group, first, range(1, n1), 6, self.gather0.at[part, 0])
            self.spread(part, chunk, group, "c", [1], 7, self.back.at[0])
        for step2 in range(1, n2):
            for part in range(2):
                first = self.ORDERS[part][0]
                chunk = self.at(part, 0)
                group = self.peer(part, 1, n2 - step2)
                wait_bytes(self.total.at[pl.ds(0, self.group)], self.gather1.at[part, step2])
                self.spread(
                    part, chunk, group, first, range(1, n1), 6, self.gather0.at[part, step2]
                )
                self.spread(part, chunk, group, "c", [1], 7, self.back.at[0])
        between()
        for step2 in range(n2):
            for part in range(2):
                wait_bytes(
                    self.total.at[pl.ds(0, (n1 - 1) * self.group)], self.gather0.at[part, step2]
                )
                group = self.peer(part, 1, n2 - step2)
                for step in range(1, n1):
                    chunk = self.peer(part, 0, n1 - step)
                    self.spread(part, chunk, group, "c", [1], 7, self.back.at[0])

    def back_wait(self):
        wait_bytes(self.total.at[pl.ds(0, PART)], self.back.at[0])

    def finish(self):
        n1, n2, nz = self.n1[0], self.n2[0], self.sizes["z"]
        counts = (
            n2 * (n1 - 1) * self.group, n2 * (n1 - 1) * self.group, 2 * (n2 - 1) * self.group,
            2 * (nz - 1) * self.unit, 2 * (nz - 1) * self.unit, 2 * (n2 - 1) * self.group,
            2 * n2 * (n1 - 1) * self.group, PART,
        )
        for at, count in enumerate(counts):
            wait_bytes(self.total.at[pl.ds(0, count)], self.sends.at[at])


def conv_summer_scratch(sizes):
    unit = PART // (2 * sizes["x"] * sizes["y"] * sizes["z"])
    group = unit * sizes["z"]
    n1, n2 = sizes["x"], sizes["y"]
    tiles = [
        (2, n2, (n1 - 1) * group), (2, n2, group), (2, (n2 - 1) * group),
        (2, group), (2, (sizes["z"] - 1) * unit),
    ]
    sems = [(2, n2), (2,), (2,), (2,), (2, n2), (2, n2), (1,), (8,)]
    return [pltpu.VMEM(shape + (16, 128), BF16) for shape in tiles] + [
        pltpu.SemaphoreType.DMA(shape) for shape in sems
    ]


class Summer:
    def __init__(self, order, place, sizes, term, total, base, scratch):
        self.order, self.place, self.sizes = order, place, sizes
        self.term, self.total, self.base = term, total, base
        self.core_in, self.held, self.inbox = scratch[0], scratch[1:4], scratch[4:7]
        self.send_sems, self.recv_sems = scratch[7], scratch[8]
        self.spans = [PART // 2]
        for axis in order:
            self.spans.append(self.spans[-1] // sizes[axis])
        self.slot = 0
        self.sent = []
        self.wait = []

    def push(self, source, target, axis, step):
        device = along(self.place, axis, step, self.sizes)
        copy = remote(
            source, target, self.send_sems.at[self.slot], self.recv_sems.at[self.slot], device
        )
        self.slot += 1
        self.sent.append(copy)
        self.wait.append(copy)

    def arrive(self):
        for copy in self.wait:
            copy.wait_recv()
        self.wait = []

    def core_start(self):
        other = self.base + (1 - self.place["c"]) * self.spans[0]
        self.push(self.term.at[pl.ds(other, self.spans[0])], self.core_in, "c", 1)

    def core_end(self):
        self.arrive()
        mine = self.base + self.place["c"] * self.spans[0]
        add_up(self.held[0], 0, self.term, mine, [self.core_in])

    def scatter_start(self, level):
        axis, span = self.order[level], self.spans[level + 1]
        for step in range(1, self.sizes[axis]):
            peer = lax.rem(self.place[axis] + step, self.sizes[axis])
            self.push(
                self.held[level].at[pl.ds(peer * span, span)],
                self.inbox[level].at[step - 1],
                axis,
                step,
            )

    def scatter_end(self, level):
        self.arrive()
        axis, span = self.order[level], self.spans[level + 1]
        received = [self.inbox[level].at[step] for step in range(self.sizes[axis] - 1)]
        mine = self.place[axis] * span
        if level < 2:
            add_up(self.held[level + 1], 0, self.held[level], mine, received)
        else:
            add_up(self.total, self.start_of(3), self.held[level], mine, received)

    def start_of(self, levels):
        start = self.base + self.place["c"] * self.spans[0]
        for level in range(levels):
            start = start + self.place[self.order[level]] * self.spans[level + 1]
        return start

    def gather_start(self, level):
        axis = self.order[level]
        mine = self.total.at[pl.ds(self.start_of(level + 1), self.spans[level + 1])]
        for step in range(1, self.sizes[axis]):
            self.push(mine, mine, axis, step)

    def core_back(self):
        mine = self.total.at[pl.ds(self.start_of(0), self.spans[0])]
        self.push(mine, mine, "c", 1)

    def finish(self):
        for copy in self.sent:
            copy.wait_send()


def summer_scratch(order, sizes):
    spans = [PART // 2]
    for axis in order:
        spans.append(spans[-1] // sizes[axis])
    shapes = [(spans[0], 16, 128)]
    shapes += [(span, 16, 128) for span in spans[:3]]
    shapes += [(sizes[axis] - 1, span, 16, 128) for axis, span in zip(order, spans[1:])]
    copies = 2 * (1 + sum(sizes[axis] - 1 for axis in order))
    return [pltpu.VMEM(shape, BF16) for shape in shapes] + [
        pltpu.SemaphoreType.DMA((copies,)),
        pltpu.SemaphoreType.DMA((copies,)),
    ]


def pack(matrix, tiles, base):
    held = matrix.astype(BF16)
    for block in range(2):
        cut = held[:, block * 128 : block * 128 + 128]
        tiles[pl.ds(base + 20 * block, 20)] = cut.reshape(20, 16, 128)
    low, high = held[:160, 256:], held[160:, 256:]
    tail = jnp.concatenate([low, high], axis=1)
    tiles[pl.ds(base + 40, 10)] = tail.reshape(10, 16, 128)


def pack_half(matrix, tiles, base):
    held = matrix.astype(BF16)
    for block in range(2):
        cut = held[:, block * 128 : block * 128 + 128]
        tiles[pl.ds(base + 10 * block, 10)] = cut.reshape(10, 16, 128)
    tail = jnp.concatenate([held[:80, 256:], held[80:, 256:]], axis=1)
    tiles[pl.ds(base + 20, 5)] = tail.reshape(5, 16, 128)


def unpack_half(tiles, base, target, at, row, factor):
    span = pl.ds(row, HALF_CHAN)
    for block in range(2):
        cut = tiles[pl.ds(base + 10 * block, 10)].reshape(HALF_CHAN, 128)
        target[at, span, block * 128 : block * 128 + 128] = cut.astype(F32) * factor
    tail = tiles[pl.ds(base + 20, 5)].reshape(80, 128).astype(F32) * factor
    target[at, pl.ds(row, 80), 256:] = tail[:, :64]
    target[at, pl.ds(row + 80, 80), 256:] = tail[:, 64:]


def unpack(tiles, base, target, at, factor):
    for block in range(2):
        cut = tiles[pl.ds(base + 20 * block, 20)].reshape(CHAN, 128)
        target[at, :, block * 128 : block * 128 + 128] = cut.astype(F32) * factor
    tail = tiles[pl.ds(base + 40, 10)].reshape(160, 128).astype(F32) * factor
    target[at, :160, 256:] = tail[:, :64]
    target[at, 160:, 256:] = tail[:, 64:]


def finish_kernel(factor, block_in, back_in, conv_in, small_in, *refs):
    (block_out, back_out, conv_out), small_outs, gain_out = refs[:3], refs[3:7], refs[7]
    conv, small, wide, fields, through, load_sems, half_sems, store_sems = refs[8:]
    moves = []
    for at, (source, target) in enumerate(((block_in, block_out), (back_in, back_out))):
        moves.append(
            (
                pltpu.make_async_copy(source, fields.at[at], through.at[at]),
                pltpu.make_async_copy(fields.at[at], target, through.at[at + 2]),
            )
        )
        moves[-1][0].start()

    def load(at, source, target):
        span = pl.ds(at * MATRIX_TILES, MATRIX_TILES)
        return source.at[span], target.at[span]

    for at in range(4):
        pltpu.make_async_copy(*load(at, small_in, small), load_sems.at[9 + at]).start()
    def load_half(at, core):
        span = pl.ds(core * PART + at * HALF_TILES, HALF_TILES)
        return pltpu.make_async_copy(conv_in.at[span], conv.at[span], half_sems.at[at, core])

    for at in range(9):
        for core in range(2):
            load_half(at, core).start()
    gain_loads = []
    for core in range(2):
        span = pl.ds(core * PART + GAIN_TILE, 2)
        gain_loads.append(
            pltpu.make_async_copy(conv_in.at[span], conv.at[span], half_sems.at[9, core])
        )
        gain_loads[-1].start()
    for at in range(4):
        pltpu.make_async_copy(*load(at, small_in, small), load_sems.at[9 + at]).wait()
        unpack(small, at * MATRIX_TILES, wide, 9 + at, factor)
        pltpu.make_async_copy(wide.at[9 + at], small_outs[at], store_sems.at[9 + at]).start()

    def conv_tap(at, carry):
        for core in range(2):
            load_half(at, core).wait()
            start = core * PART + at * HALF_TILES
            unpack_half(conv, start, wide, at, core * HALF_CHAN, factor)
        pltpu.make_async_copy(wide.at[at], conv_out.at[at], store_sems.at[at]).start()
        return carry

    for move in moves:
        move[0].wait()
        move[1].start()
    lax.fori_loop(0, 9, conv_tap, 0)
    for copy in gain_loads:
        copy.wait()
    pieces = []
    for at in range(2):
        tiles = [conv[core * PART + GAIN_TILE + at].astype(F32) for core in range(2)]
        pieces.append((tiles[0] + tiles[1]) * factor)
    gain_out[0:128] = pieces[0][0]
    gain_out[128:256] = pieces[0][1]
    gain_out[256:] = pieces[1][0, :64]
    for move in moves:
        move[1].wait()
    for at in range(9):
        pltpu.make_async_copy(wide.at[at], conv_out.at[at], store_sems.at[at]).wait()
    for at in range(4):
        pltpu.make_async_copy(wide.at[9 + at], small_outs[at], store_sems.at[9 + at]).wait()


def shifts(cells):
    column = lax.broadcasted_iota(jnp.int32, cells.shape, 0)
    left = jnp.where(column == 0, 0.0, pltpu.roll(cells, 1, 0))
    right = jnp.where(column == COLS - 1, 0.0, pltpu.roll(cells, COLS - 1, 0))
    return [left, cells, right]


class Swap:
    def __init__(self, source, target, send_sems, recv_sems, peers, me):
        self.source, self.target, self.peers, self.me = source, target, peers, me
        self.send_sems, self.recv_sems = send_sems, recv_sems

    def start(self, half):
        for frame, device in self.peers:
            remote(
                self.source.at[half, frame],
                self.target.at[half, self.me],
                self.send_sems.at[half],
                self.recv_sems.at[half],
                device,
            )
        self.target[half, self.me] = self.source[half, self.me]

    def wait(self, half):
        span = self.target.at[half, pl.ds(0, len(self.peers))]
        pltpu.make_async_copy(span, span, self.recv_sems.at[half]).wait()

    def finish(self):
        for half in range(2):
            span = self.source.at[half, pl.ds(0, len(self.peers))]
            pltpu.make_async_copy(span, span, self.send_sems.at[half]).wait()


def norm_of(resid):
    return lax.rsqrt(jnp.mean(resid * resid, axis=-1, keepdims=True) + EPS)


def cell_start(half, at):
    if half == 0:
        return COLS + at * 64
    return jnp.where(at < 2, at * 64, HALF + at * 64)


def head_masks():
    low = lax.broadcasted_iota(jnp.int32, (1, 128), 1) < 64
    return low, [jnp.where(low, 0.125, 0.0).astype(BF16), jnp.where(low, 0.0, 0.125).astype(BF16)]


def attend(q_s, k_s, v_s, bias, probs_s, mixed_s):
    low, masks = head_masks()

    def tile(at, masks):
        start = at * 128
        span = pl.ds(start if isinstance(at, int) else pl.multiple_of(start, 128), 128)
        queries, keys, values = q_s[:, span], k_s[:, span], v_s[:, span]
        found = []
        for head, mask in enumerate(masks):
            scores = dot_nt(keys, queries * mask) + bias[...]
            expo = jnp.exp(scores)
            probs = expo * (1.0 / jnp.sum(expo, axis=0, keepdims=True))
            probs_s[2 * at + head] = probs
            found.append(dot_tn(probs.astype(BF16), values))
        total = found[0] if len(found) == 1 else jnp.where(low, *found)
        mixed_s[:, span] = total.astype(BF16)

    def pair(at, carry):
        tile(at, masks)
        return carry

    lax.fori_loop(0, 2, pair, 0)
    tile(2, masks[:1])


def attend_back(q_s, k_s, v_s, d_s, probs_s, qp_s, kp_s, vp_s):
    low, masks = head_masks()

    def tile(at, masks):
        start = at * 128
        span = pl.ds(start if isinstance(at, int) else pl.multiple_of(start, 128), 128)
        queries, keys, values, grads = q_s[:, span], k_s[:, span], v_s[:, span], d_s[:, span]
        found = []
        for head, mask in enumerate(masks):
            probs = probs_s[2 * at + head]
            prob_grad = dot_nt(values, grads * mask)
            inner = jnp.sum(probs * prob_grad, axis=0, keepdims=True)
            score_b = (probs * (prob_grad - inner)).astype(BF16)
            found.append(
                (
                    dot_tn(score_b, keys),
                    dot(score_b, queries),
                    dot(probs.astype(BF16), grads),
                )
            )
        for place, target in enumerate((qp_s, kp_s, vp_s)):
            parts = [part[place] for part in found]
            total = parts[0] if len(parts) == 1 else jnp.where(low, *parts)
            target[:, span] = total.astype(BF16)

    def pair(at, carry):
        tile(at, masks)
        return carry

    lax.fori_loop(0, 2, pair, 0)
    tile(2, masks[:1])


def block_kernel(sizes, latents, conv_w, query_w, key_w, value_w, out_w, gain, out_grad, *refs):
    (block_hbm, back_hbm, conv_hbm, small_hbm), refs = refs[:4], refs[4:]
    (
        lat_in, grad_in, lat, grad, weights, wq, wk, wv, wo, gain_v, in_sems,
        padded, wide, halo, halo_send, halo_recv, acc, resid, act_c, act_in, act_t,
        normed_out, normed_in, og_out, og_in, ng_out, ng_in, mix_out, mix_in,
        swap_send, swap_recv,
        og_n, normed_n, mixed_n, back_n,
        q_s, k_s, v_s, d_s, bias, probs_s, out_acc, mixed_s, qp_s, kp_s, vp_s, parts, flip,
        resid_grad, rg_in, conv_acc, pair_send, pair_recv, grad_pad, gain_acc, conv_terms, small_terms,
        block_out, latents_grad, conv_total, small_total, out_sems,
    ), refs = refs[:62], refs[62:]
    frames = lax.axis_size("frame")
    rows_n = lax.axis_size("row")
    chunk = HALF // frames
    me, row = lax.axis_index("frame"), lax.axis_index("row")
    place = my_place()
    peers = []
    for step in range(1, frames):
        frame = lax.rem(me + step, frames)
        peers.append((frame, (frame, row)))
    above = (me, lax.rem(row + rows_n - 1, rows_n))
    below = (me, lax.rem(row + 1, rows_n))

    barrier = pltpu.get_barrier_semaphore()
    partners = [device for _, device in peers] + [above, below]
    for axis in "cxy":
        partners += [along(place, axis, step, sizes) for step in range(1, sizes[axis])]
    for device in partners:
        pl.semaphore_signal(barrier, inc=1, device_id=device, device_id_type=MESH)

    loads = []
    pairs = (
        (latents, lat_in), (out_grad, grad_in), (conv_w, weights), (gain, gain_v),
        (out_w, wo), (query_w, wq), (key_w, wk), (value_w, wv),
    )
    for at, (source, target) in enumerate(pairs):
        loads.append(pltpu.make_async_copy(source, target, in_sems.at[at]))
        loads[-1].start()

    loads[0].wait()

    def activate(at, carry):
        span = pl.ds(at * COLS, COLS)
        cells = lat_in[at].astype(F32).T
        lat[span] = cells.astype(BF16)
        act = (cells * jax.nn.sigmoid(cells)).astype(BF16).astype(F32)
        span = pl.ds((at + 1) * COLS, COLS)
        for shift, copy in enumerate(shifts(act)):
            wide[span, shift * CHAN : shift * CHAN + CHAN] = copy.astype(BF16)
        padded[span] = act.astype(BF16)
        return carry

    lax.fori_loop(0, ROWS, activate, 0)
    loads[1].wait()

    def flip_grad(at, carry):
        cells = grad_in[at].astype(F32).T.astype(BF16)
        grad[pl.ds(at * COLS, COLS)] = cells
        half = jnp.where((at == 0) | (at == ROWS - 1), 1, 0)
        span = pl.ds(jnp.where(at >= 2, frames // 2, 0), frames // 2)
        og_out[half, span] = cells[:, :256].reshape(frames // 2, chunk, 256)
        normed_out[half, span, :, CHAN:] = cells[:, 256:].reshape(frames // 2, chunk, 64)
        return carry

    lax.fori_loop(0, ROWS, flip_grad, 0)
    pl.semaphore_wait(barrier, len(partners))

    def halo_start(source, kind):
        return [
            remote(source.at[pl.ds(COLS, COLS)], halo.at[kind, 1],
                   halo_send.at[kind, 0], halo_recv.at[kind, 0], above),
            remote(source.at[pl.ds(ROWS * COLS, COLS)], halo.at[kind, 0],
                   halo_send.at[kind, 1], halo_recv.at[kind, 1], below),
        ]

    def halo_end(copies, kind, store):
        for copy in copies:
            copy.wait_recv()
        ends = (row > 0, row < rows_n - 1)
        for side, inside in enumerate(ends):
            keep = jnp.where(inside, 1.0, 0.0).astype(F32)
            cells = halo[kind, side].astype(F32) * keep
            store(pl.ds(side * (ROWS + 1) * COLS, COLS), cells)

    def store_act(span, cells):
        for shift, copy in enumerate(shifts(cells)):
            wide[span, shift * CHAN : shift * CHAN + CHAN] = copy.astype(BF16)
        padded[span] = cells.astype(BF16)

    def store_grad(span, cells):
        for shift, copy in enumerate(shifts(cells)):
            grad_pad[shift, span] = copy.astype(BF16)

    act_halo = halo_start(padded, 0)

    swaps = []
    buffers = ((og_out, og_in), (normed_out, normed_in), (ng_out, ng_in), (mix_out, mix_in))
    for at, (source, target) in enumerate(buffers):
        swaps.append(Swap(source, target, swap_send.at[at], swap_recv.at[at], peers, me))
    og_swap, normed_swap, ng_swap, mix_swap = swaps

    loads[2].wait()
    loads[3].wait()

    def conv_half(half):
        total = None
        for a in range(3):
            if half == 0:
                cells = wide[(a + 1) * COLS : (a + 1) * COLS + HALF]
            else:
                cells = jnp.concatenate(
                    [wide[a * COLS : (a + 1) * COLS], wide[(a + 3) * COLS : (a + 4) * COLS]]
                )
            term = dot(cells, weights[3 * a : 3 * a + 3].reshape(3 * CHAN, CHAN))
            total = term if total is None else total + term
        acc[pl.ds(0, HALF)] = total
        count = 64 // chunk

        def finish(at, carry):
            cells = lat[pl.ds(pl.multiple_of(cell_start(half, at), 64), 64)].astype(F32)
            held = (cells + acc[pl.ds(at * 64, 64)]).astype(BF16)
            resid[half, pl.ds(at * 64, 64)] = held
            held = held.astype(F32)
            normed = (held * norm_of(held) * gain_v[...].reshape(1, CHAN)).astype(BF16)
            normed_out[half, pl.ds(at * count, count), :, :CHAN] = normed.reshape(count, chunk, CHAN)
            return carry

        lax.fori_loop(0, 4, finish, 0)

    og_swap.start(0)
    conv_half(0)
    normed_swap.start(0)
    halo_end(act_halo, 0, store_act)
    conv_half(1)
    normed_swap.start(1)
    og_swap.start(1)

    position = lax.broadcasted_iota(jnp.int32, (HALF, HALF), 0)
    other = lax.broadcasted_iota(jnp.int32, (HALF, HALF), 1)
    same = lax.rem(position, chunk) == lax.rem(other, chunk)
    bias[...] = jnp.where(same, 0.0, -1e30)
    for field in (q_s, k_s, v_s, d_s):
        field[:, 256:] = jnp.zeros((HALF, 128), BF16)
    act_c[...] = padded[...].astype(F32).T.astype(BF16)
    core = place["c"]
    partner = along(place, "c", 1, sizes)
    mine = pl.ds(pl.multiple_of(core * HALF_CHAN, HALF_CHAN), HALF_CHAN)
    theirs = pl.ds(pl.multiple_of((1 - core) * HALF_CHAN, HALF_CHAN), HALF_CHAN)
    pair = [remote(act_c.at[theirs], act_in, pair_send.at[0], pair_recv.at[0], partner)]

    def shift_lanes(at, carry, source, side):
        span = pl.ds(pl.multiple_of(at * COLS, COLS), COLS)
        cells = source[:, span].astype(F32)
        column = lax.broadcasted_iota(jnp.int32, cells.shape, 1)
        left = jnp.where(column == 0, 0.0, pltpu.roll(cells, 1, 1))
        right = jnp.where(column == COLS - 1, 0.0, pltpu.roll(cells, COLS - 1, 1))
        for shift, copy in enumerate((left, cells, right)):
            act_t[side, shift * HALF_CHAN : (shift + 1) * HALF_CHAN, span] = copy.astype(BF16)
        return carry

    own_rows = functools.partial(shift_lanes, source=act_c.at[mine], side=0)
    lax.fori_loop(0, ROWS + 2, own_rows, 0)
    for load in loads[4:]:
        load.wait()

    for half in range(2):
        normed_swap.wait(half)
        arrived = normed_in[half].reshape(HALF, WIDE)
        normed_n[half] = arrived[:, :CHAN]
        og_n[half, :, 256:] = arrived[:, CHAN:]
        q_s[:, :CHAN] = dot(normed_n[half], wq[...]).astype(BF16)
        k_s[:, :CHAN] = dot(normed_n[half], wk[...]).astype(BF16)
        v_s[:, :CHAN] = dot(normed_n[half], wv[...]).astype(BF16)
        attend(q_s, k_s, v_s, bias, probs_s, mixed_s)
        mixed_n[half] = mixed_s[:, :CHAN]
        mix_out[half] = mixed_s[:, :256].reshape(frames, chunk, 256)
        ng_out[half, :, :, CHAN:] = mixed_s[:, 256:CHAN].reshape(frames, chunk, 64)
        og_swap.wait(half)
        og_n[half, :, :256] = og_in[half].reshape(HALF, 256)
        d_s[:, :CHAN] = dot_nt(og_n[half], wo[...]).astype(BF16)
        attend_back(q_s, k_s, v_s, d_s, probs_s, qp_s, kp_s, vp_s)
        back = dot_nt(qp_s[:, :CHAN], wq[...])
        back = back + dot_nt(kp_s[:, :CHAN], wk[...])
        back = back + dot_nt(vp_s[:, :CHAN], wv[...])
        ng_out[half, :, :, :CHAN] = back.astype(BF16).reshape(frames, chunk, CHAN)
        ng_swap.start(half)
        for at, field in enumerate((qp_s, kp_s, vp_s)):
            parts[at, pl.ds(half * HALF, HALF)] = field[:, :CHAN]

    flip[0] = normed_n[...].reshape(2 * HALF, CHAN).astype(F32).T.astype(BF16)
    flip[1] = mixed_n[...].reshape(2 * HALF, CHAN).astype(F32).T.astype(BF16)
    for at in range(3):
        pack(dot(flip[0], parts[at]), small_terms, at * MATRIX_TILES)
    pack(dot(flip[1], og_n[...].reshape(2 * HALF, CHAN)), small_terms, 3 * MATRIX_TILES)
    spare = SMALL_TILES - 4 * MATRIX_TILES
    small_terms[pl.ds(4 * MATRIX_TILES, spare)] = jnp.zeros((spare, 16, 128), BF16)

    conv = ConvSummer(place, sizes, conv_terms, conv_total, refs[9:])
    small = Summer("yxz", place, sizes, small_terms, small_total, 0, refs[:9])
    small.core_start()

    gain_acc[...] = jnp.zeros((8, CHAN), F32)
    for half in range(2):
        ng_swap.wait(half)

        def undo_norm(at, carry, half=half):
            count = 64 // chunk
            begin = pl.multiple_of(cell_start(half, at), 64)
            held = resid[half, pl.ds(at * 64, 64)].astype(F32)
            back = ng_in[half, pl.ds(at * count, count), :, :CHAN].reshape(64, CHAN).astype(F32)
            inv = norm_of(held)
            product = back * held
            total = jnp.sum((product * inv).reshape(8, 8, CHAN), axis=0)
            gain_acc[...] += total
            tangent = back * gain_v[...].reshape(1, CHAN)
            mean = jnp.mean(product * gain_v[...].reshape(1, CHAN), axis=-1, keepdims=True)
            value = grad[pl.ds(begin, 64)].astype(F32) + (
                inv * tangent - held * (inv * inv * inv) * mean
            )
            resid_grad[half, pl.ds(at * 64, 64)] = value.astype(BF16)
            return carry

        lax.fori_loop(0, 4, undo_norm, 0)
        pair.append(
            remote(
                resid_grad.at[half],
                rg_in.at[half],
                pair_send.at[1 + half],
                pair_recv.at[1 + half],
                partner,
            )
        )
        if half == 0:
            pair[0].wait_recv()
            other_rows = functools.partial(shift_lanes, source=act_in, side=1)
            lax.fori_loop(0, ROWS + 2, other_rows, 0)

            def inner_taps(at, carry, side, cells):
                span = pl.ds(pl.multiple_of((at + 1) * COLS, COLS), HALF)
                total = dot(act_t[side, :, span], cells[0])
                if side == 0:
                    conv_acc[at] = total
                else:
                    conv_acc[at] += total
                return carry

            lax.fori_loop(
                0, 3, functools.partial(inner_taps, side=0, cells=resid_grad), 0
            )
            small.core_end()
            small.scatter_start(0)
            pair[1].wait_recv()
            lax.fori_loop(0, 3, functools.partial(inner_taps, side=1, cells=rg_in), 0)


    def pad_grad(at, carry):
        half = jnp.where((at == 0) | (at == ROWS - 1), 1, 0)
        side = jnp.where(at >= 2, 1, 0)
        cells = resid_grad[half, pl.ds(side * COLS, COLS)].astype(F32)
        for shift, copy in enumerate(shifts(cells)):
            grad_pad[shift, pl.ds((at + 1) * COLS, COLS)] = copy.astype(BF16)
        return carry

    def edge_cells(side, at):
        spans = [pl.ds(pl.multiple_of((at + gap) * COLS, COLS), COLS) for gap in (0, ROWS - 1)]
        return jnp.concatenate([act_t[side, :, span] for span in spans], axis=1)

    def second_taps(at, carry):
        conv_acc[at] += dot(edge_cells(0, at), resid_grad[1])
        return carry

    lax.fori_loop(0, 3, second_taps, 0)
    lax.fori_loop(0, ROWS, pad_grad, 0)
    grad_halo = halo_start(grad_pad.at[1], 1)

    spare = PART - 9 * HALF_TILES
    conv_terms[pl.ds(9 * HALF_TILES, spare)] = jnp.zeros((spare, 16, 128), BF16)
    gains = jnp.sum(gain_acc[...], axis=0, keepdims=True)
    line = lax.broadcasted_iota(jnp.int32, (16, 128), 0)
    gain_tile = jnp.where(line == 0, gains[:, :128], jnp.where(line == 1, gains[:, 128:256], 0.0))
    conv_terms[GAIN_TILE] = gain_tile.astype(BF16)
    tail = jnp.where(line[:, :64] == 0, gains[:, 256:], 0.0)
    conv_terms[GAIN_TILE + 1, :, :64] = tail.astype(BF16)
    pair[2].wait_recv()

    def last_taps(at, carry):
        total = conv_acc[at] + dot(edge_cells(1, at), rg_in[1])
        for b in range(3):
            part = total[b * HALF_CHAN : (b + 1) * HALF_CHAN]
            pack_half(part, conv_terms, (at * 3 + b) * HALF_TILES)
        return carry

    lax.fori_loop(0, 2, last_taps, 0)
    conv.scatter_first(0)
    lax.fori_loop(2, 3, last_taps, 0)
    conv.scatter_first(1)
    mix_swap.start(0)
    mix_swap.start(1)
    small.scatter_end(0)
    small.scatter_start(1)

    def project_out(half):
        mix_swap.wait(half)
        back_n[:, :256] = mix_in[half].reshape(HALF, 256)
        back_n[:, 256:] = ng_in[half, :, :, CHAN:].reshape(HALF, 64)
        out_acc[...] = dot(back_n[...], wo[...])

        def write_out(at, carry):
            held = resid[half, pl.ds(at * COLS, COLS)].astype(F32)
            total = held + out_acc[pl.ds(at * COLS, COLS)]
            block_out[at + 1 if half == 0 else at * 3] = total.T.astype(BF16)
            return carry

        lax.fori_loop(0, 2, write_out, 0)

    halo_end(grad_halo, 1, store_grad)
    acc[...] = jnp.zeros((2 * HALF, CHAN), F32)

    def back_tap(at, carry):
        a, b = at // 3, lax.rem(at, 3)
        cells = grad_pad[2 - b, pl.ds((2 - a) * COLS, ROWS * COLS)]
        acc[...] += dot_nt(cells, weights[at])
        return carry

    lax.fori_loop(0, 3, back_tap, 0)
    small.scatter_end(1)
    small.scatter_start(2)
    lax.fori_loop(3, 5, back_tap, 0)
    conv.scatter_second()
    small.scatter_end(2)
    small.gather_start(2)
    stores = []

    def store(source, target):
        stores.append(pltpu.make_async_copy(source, target, out_sems.at[len(stores)]))
        stores[-1].start()

    lax.fori_loop(5, 9, back_tap, 0)
    conv.scatter_third()
    small.arrive()
    small.gather_start(1)
    project_out(0)
    project_out(1)
    store(block_out, block_hbm)
    conv.gather_third()
    small.arrive()
    small.gather_start(0)
    def write_back(at, carry):
        cells = lat[pl.ds(at * COLS, COLS)].astype(F32)
        sigma = jax.nn.sigmoid(cells)
        slope = sigma * (1.0 + cells * (1.0 - sigma))
        half = jnp.where((at == 0) | (at == ROWS - 1), 1, 0)
        side = jnp.where(at >= 2, 1, 0)
        value = resid_grad[half, pl.ds(side * COLS, COLS)].astype(F32) + acc[pl.ds(at * COLS, COLS)] * slope
        latents_grad[at] = value.T.astype(BF16)
        return carry

    lax.fori_loop(0, ROWS, write_back, 0)
    store(latents_grad, back_hbm)
    def return_small():
        small.arrive()
        small.core_back()

    conv.gather_rest(return_small)
    own_half = pl.ds(place["c"] * PART, PART)
    store(conv_total.at[own_half], conv_hbm.at[own_half])
    small.arrive()
    store(small_total, small_hbm)
    conv.back_wait()
    other_half = pl.ds((1 - place["c"]) * PART, PART)
    store(conv_total.at[other_half], conv_hbm.at[other_half])
    small.finish()
    conv.finish()
    for swap in swaps:
        swap.finish()
    for copy in act_halo + grad_halo + pair:
        copy.wait_send()
    for copy in stores:
        copy.wait()


def block_scratch(sizes, frames):
    narrow, wide = (2, frames, HALF // frames, 256), (2, frames, HALF // frames, WIDE)
    vmem = pltpu.VMEM
    dma = pltpu.SemaphoreType.DMA
    weight = vmem((CHAN, CHAN), BF16)
    shapes = [
        vmem((ROWS, CHAN, COLS), BF16), vmem((ROWS, CHAN, COLS), BF16),
        vmem((ROWS * COLS, CHAN), BF16), vmem((ROWS * COLS, CHAN), BF16),
        vmem((9, CHAN, CHAN), BF16), weight, weight, weight, weight, vmem((CHAN,), F32), dma((8,)),
        vmem(((ROWS + 2) * COLS, CHAN), BF16), vmem(((ROWS + 2) * COLS, 3 * CHAN), BF16),
        vmem((2, 2, COLS, CHAN), BF16),
        dma((2, 2)), dma((2, 2)), vmem((2 * HALF, CHAN), F32), vmem((2, HALF, CHAN), BF16),
        vmem((CHAN, (ROWS + 2) * COLS), BF16), vmem((HALF_CHAN, (ROWS + 2) * COLS), BF16),
        vmem((2, 3 * HALF_CHAN, (ROWS + 2) * COLS), BF16),
    ]
    shapes += [vmem(shape, BF16) for shape in (wide, wide, narrow, narrow, wide, wide, narrow, narrow)]
    shapes += [dma((4, 2)), dma((4, 2))]
    shapes += [vmem((2, HALF, CHAN), BF16)] * 3 + [vmem((HALF, CHAN), BF16)]
    shapes += [vmem((HALF, WIDE), BF16)] * 4 + [vmem((HALF, HALF), F32)]
    shapes += [vmem((5, HALF, HALF), F32), vmem((HALF, CHAN), F32)]
    shapes += [vmem((HALF, WIDE), BF16)] * 4
    shapes += [vmem((3, 2 * HALF, CHAN), BF16), vmem((2, CHAN, 2 * HALF), BF16)]
    shapes += [vmem((2, HALF, CHAN), BF16), vmem((2, HALF, CHAN), BF16)]
    shapes += [vmem((3, 3 * HALF_CHAN, CHAN), F32), dma((3,)), dma((3,))]
    shapes += [vmem((3, (ROWS + 2) * COLS, CHAN), BF16)]
    shapes += [vmem((8, CHAN), F32)]
    shapes += [vmem((PART, 16, 128), BF16), vmem((SMALL_TILES, 16, 128), BF16)]
    shapes += [vmem((ROWS, CHAN, COLS), BF16)] * 2
    shapes += [vmem((CONV_TILES, 16, 128), BF16), vmem((SMALL_TILES, 16, 128), BF16), dma((5,))]
    return shapes + summer_scratch("yxz", sizes) + conv_summer_scratch(sizes)


def on_device(
    latents, conv_weight, query_weight, key_weight, value_weight, out_weight, norm_gain, out_grad
):
    sizes = chip_sizes()
    frames = lax.axis_size("frame")
    anywhere = pl.BlockSpec(memory_space=pl.ANY)
    inside = pl.BlockSpec(memory_space=pltpu.VMEM)
    field = jax.ShapeDtypeStruct((ROWS, CHAN, COLS), BF16)
    block_out, latents_grad, conv_sum, small_sum = pl.pallas_call(
        functools.partial(block_kernel, sizes),
        out_shape=[
            field,
            field,
            jax.ShapeDtypeStruct((CONV_TILES, 16, 128), BF16),
            jax.ShapeDtypeStruct((SMALL_TILES, 16, 128), BF16),
        ],
        in_specs=[anywhere] * 8,
        out_specs=[anywhere] * 4,
        scratch_shapes=block_scratch(sizes, frames),
        compiler_params=pltpu.CompilerParams(
            collective_id=0, has_side_effects=True, vmem_limit_bytes=56 << 20
        ),
    )(
        jnp.swapaxes(latents[0], 1, 2),
        conv_weight.reshape(9, CHAN, CHAN),
        query_weight,
        key_weight,
        value_weight,
        out_weight,
        norm_gain,
        jnp.swapaxes(out_grad[0], 1, 2),
    )
    factor = (ROWS * COLS * frames * lax.axis_size("row")) ** (-0.5)
    weight = jax.ShapeDtypeStruct((CHAN, CHAN), F32)
    outs = pl.pallas_call(
        functools.partial(finish_kernel, factor),
        out_shape=[
            field,
            field,
            jax.ShapeDtypeStruct((9, CHAN, CHAN), F32),
            weight,
            weight,
            weight,
            weight,
            jax.ShapeDtypeStruct((CHAN,), F32),
        ],
        in_specs=[anywhere] * 4,
        out_specs=[anywhere] * 7 + [inside],
        scratch_shapes=[
            pltpu.VMEM((CONV_TILES, 16, 128), BF16),
            pltpu.VMEM((SMALL_TILES, 16, 128), BF16),
            pltpu.VMEM((13, CHAN, CHAN), F32),
            pltpu.VMEM((2, ROWS, CHAN, COLS), BF16),
            pltpu.SemaphoreType.DMA((4,)),
            pltpu.SemaphoreType.DMA((13,)),
            pltpu.SemaphoreType.DMA((10, 2)),
            pltpu.SemaphoreType.DMA((13,)),
        ],
        compiler_params=pltpu.CompilerParams(vmem_limit_bytes=56 << 20),
    )(block_out, latents_grad, conv_sum, small_sum)
    return (
        jnp.swapaxes(outs[0], 1, 2)[None],
        jnp.swapaxes(outs[1], 1, 2)[None],
        outs[2].reshape(3, 3, CHAN, CHAN),
        *outs[3:7],
        outs[7],
    )


def solution(mesh):
    split = P("frame", "row", None, None)
    return jax.shard_map(
        on_device,
        mesh=mesh,
        in_specs=(split, P(), P(), P(), P(), P(), P(), split),
        out_specs=(split, split, P(), P(), P(), P(), P(), P()),
        check_vma=False,
    )
```

```python
import functools

import jax
import jax.numpy as jnp
from jax import lax
from jax.experimental import pallas as pl
from jax.experimental.pallas import tpu as pltpu
from jax.sharding import PartitionSpec as P

EPS = 1e-06
MESH = pl.DeviceIdType.MESH
CHAN = 320
WIDE = 384
COLS = 128
ROWS = 4
HALF = 256
CONV_TILES = 512
SMALL_TILES = 256
PART = 256
MATRIX_TILES = 50
GAIN_TILE = 230
HALF_CHAN = 160
HALF_TILES = 25
BLOCK = 16
F32 = jnp.float32
BF16 = jnp.bfloat16


def chip_sizes():
    return {"c": 2, "x": 4, "y": lax.axis_size("row") // 4, "z": lax.axis_size("frame") // 2}


def my_place():
    frame, row = lax.axis_index("frame"), lax.axis_index("row")
    return {
        "z": frame // 2,
        "x": lax.rem(row // 2, 2) * 2 + lax.rem(frame, 2),
        "y": row // 4,
        "c": lax.rem(row, 2),
    }


def device_of(place):
    return (
        place["z"] * 2 + lax.rem(place["x"], 2),
        (place["y"] * 2 + place["x"] // 2) * 2 + place["c"],
    )


def along(place, axis, step, sizes):
    moved = dict(place)
    moved[axis] = lax.rem(place[axis] + step, sizes[axis])
    return device_of(moved)


def remote(source, target, send_sem, recv_sem, device):
    copy = pltpu.make_async_remote_copy(
        src_ref=source,
        dst_ref=target,
        send_sem=send_sem,
        recv_sem=recv_sem,
        device_id=device,
        device_id_type=MESH,
    )
    copy.start()
    return copy


def dot(left, right):
    return jnp.dot(left, right, preferred_element_type=F32)


def dot_nt(left, right):
    return lax.dot_general(left, right, (((1,), (1,)), ((), ())), preferred_element_type=F32)


def dot_tn(left, right):
    return lax.dot_general(left, right, (((0,), (0,)), ((), ())), preferred_element_type=F32)


def add_up(target, start, own, own_start, received):
    count = received[0].shape[0]
    step = min(count, BLOCK)

    def body(at, carry):
        at = at * step
        total = own[pl.ds(own_start + at, step)].astype(F32)
        for part in received:
            total = total + part[pl.ds(at, step)].astype(F32)
        target[pl.ds(start + at, step)] = total.astype(BF16)
        return carry

    lax.fori_loop(0, count // step, body, 0)


def wait_bytes(span, sem):
    pltpu.make_async_copy(span, span, sem).wait()


class ConvSummer:
    ORDERS = ("xy", "yx")

    def __init__(self, place, sizes, terms, total, scratch):
        self.place, self.sizes, self.terms, self.total = place, sizes, terms, total
        (
            self.inbox0, self.held1, self.inbox1, self.held2, self.inbox2,
            self.scatter0, self.scatter1, self.scatter2,
            self.gather2, self.gather1, self.gather0, self.back, self.sends,
        ) = scratch
        self.unit = PART // (2 * sizes["x"] * sizes["y"] * sizes["z"])
        self.group = self.unit * sizes["z"]
        self.n1 = [sizes[order[0]] for order in self.ORDERS]
        self.n2 = [sizes[order[1]] for order in self.ORDERS]

    def at(self, part, axis):
        return self.place[self.ORDERS[part][axis]]

    def peer(self, part, axis, step):
        return lax.rem(self.at(part, axis) + step, self.sizes[self.ORDERS[part][axis]])

    def device(self, axis, step):
        return along(self.place, axis, step, self.sizes)

    def local(self, part, chunk, group, unit=0):
        span = self.n2[part] * self.group
        return part * (PART // 2) + chunk * span + group * self.group + unit * self.unit

    def tile(self, part, chunk, group, unit=0):
        return self.place["c"] * PART + self.local(part, chunk, group, unit)

    def scatter_first(self, part):
        for step2 in range(self.n2[0]):
            step2 = (step2 + 1) % self.n2[0]
            for step in range(1, self.n1[0]):
                chunk, group = self.peer(part, 0, step), self.peer(part, 1, step2)
                remote(
                    self.terms.at[pl.ds(self.local(part, chunk, group), self.group)],
                    self.inbox0.at[part, group, pl.ds((step - 1) * self.group, self.group)],
                    self.sends.at[part],
                    self.scatter0.at[part, step2],
                    self.device(self.ORDERS[part][0], step),
                )

    def scatter_second(self):
        for step2 in range(self.n2[0]):
            step2 = (step2 + 1) % self.n2[0]
            for part in range(2):
                chunk, group = self.at(part, 0), self.peer(part, 1, step2)
                wait_bytes(self.inbox0.at[part, group], self.scatter0.at[part, step2])
                total = self.terms[pl.ds(self.local(part, chunk, group), self.group)].astype(F32)
                for step in range(self.n1[part] - 1):
                    span = pl.ds(step * self.group, self.group)
                    total = total + self.inbox0[part, group, span].astype(F32)
                held = self.held1.at[part, group]
                held[...] = total.astype(BF16)
                if step2 > 0:
                    remote(
                        held,
                        self.inbox1.at[part, pl.ds((step2 - 1) * self.group, self.group)],
                        self.sends.at[2],
                        self.scatter1.at[part],
                        self.device(self.ORDERS[part][1], step2),
                    )

    def scatter_third(self):
        for part in range(2):
            wait_bytes(self.inbox1.at[part], self.scatter1.at[part])
            total = self.held1[part, self.at(part, 1)].astype(F32)
            for step in range(self.n2[part] - 1):
                total = total + self.inbox1[part, pl.ds(step * self.group, self.group)].astype(F32)
            self.held2[part] = total.astype(BF16)
            for step in range(1, self.sizes["z"]):
                peer = lax.rem(self.place["z"] + step, self.sizes["z"])
                remote(
                    self.held2.at[part, pl.ds(peer * self.unit, self.unit)],
                    self.inbox2.at[part, pl.ds((step - 1) * self.unit, self.unit)],
                    self.sends.at[3],
                    self.scatter2.at[part],
                    self.device("z", step),
                )

    def gather_third(self):
        for part in range(2):
            wait_bytes(self.inbox2.at[part], self.scatter2.at[part])
            z = self.place["z"]
            total = self.held2[part, pl.ds(z * self.unit, self.unit)].astype(F32)
            for step in range(self.sizes["z"] - 1):
                total = total + self.inbox2[part, pl.ds(step * self.unit, self.unit)].astype(F32)
            mine = self.tile(part, self.at(part, 0), self.at(part, 1), z)
            self.total[pl.ds(mine, self.unit)] = total.astype(BF16)
            span = self.total.at[pl.ds(mine, self.unit)]
            for step in range(1, self.sizes["z"]):
                remote(
                    span, span, self.sends.at[4], self.gather2.at[part], self.device("z", step)
                )

    def spread(self, part, chunk, group, axis, steps, send, sem):
        span = self.total.at[pl.ds(self.tile(part, chunk, group), self.group)]
        for step in steps:
            remote(span, span, self.sends.at[send], sem, self.device(axis, step))

    def gather_rest(self, between):
        n1, n2 = self.n1[0], self.n2[0]
        for part in range(2):
            wait_bytes(
                self.total.at[pl.ds(0, (self.sizes["z"] - 1) * self.unit)], self.gather2.at[part]
            )
            first, second = self.ORDERS[part]
            chunk, group = self.at(part, 0), self.at(part, 1)
            for step in range(1, n2):
                sem = self.gather1.at[part, step]
                self.spread(part, chunk, group, second, [step], 5, sem)
            self.spread(part, chunk, group, first, range(1, n1), 6, self.gather0.at[part, 0])
            self.spread(part, chunk, group, "c", [1], 7, self.back.at[0])
        for step2 in range(1, n2):
            for part in range(2):
                first = self.ORDERS[part][0]
                chunk = self.at(part, 0)
                group = self.peer(part, 1, n2 - step2)
                wait_bytes(self.total.at[pl.ds(0, self.group)], self.gather1.at[part, step2])
                self.spread(
                    part, chunk, group, first, range(1, n1), 6, self.gather0.at[part, step2]
                )
                self.spread(part, chunk, group, "c", [1], 7, self.back.at[0])
        between()
        for step2 in range(n2):
            for part in range(2):
                wait_bytes(
                    self.total.at[pl.ds(0, (n1 - 1) * self.group)], self.gather0.at[part, step2]
                )
                group = self.peer(part, 1, n2 - step2)
                for step in range(1, n1):
                    chunk = self.peer(part, 0, n1 - step)
                    self.spread(part, chunk, group, "c", [1], 7, self.back.at[0])

    def back_wait(self):
        wait_bytes(self.total.at[pl.ds(0, PART)], self.back.at[0])

    def finish(self):
        n1, n2, nz = self.n1[0], self.n2[0], self.sizes["z"]
        counts = (
            n2 * (n1 - 1) * self.group, n2 * (n1 - 1) * self.group, 2 * (n2 - 1) * self.group,
            2 * (nz - 1) * self.unit, 2 * (nz - 1) * self.unit, 2 * (n2 - 1) * self.group,
            2 * n2 * (n1 - 1) * self.group, PART,
        )
        for at, count in enumerate(counts):
            wait_bytes(self.total.at[pl.ds(0, count)], self.sends.at[at])


def conv_summer_scratch(sizes):
    unit = PART // (2 * sizes["x"] * sizes["y"] * sizes["z"])
    group = unit * sizes["z"]
    n1, n2 = sizes["x"], sizes["y"]
    tiles = [
        (2, n2, (n1 - 1) * group), (2, n2, group), (2, (n2 - 1) * group),
        (2, group), (2, (sizes["z"] - 1) * unit),
    ]
    sems = [(2, n2), (2,), (2,), (2,), (2, n2), (2, n2), (1,), (8,)]
    return [pltpu.VMEM(shape + (16, 128), BF16) for shape in tiles] + [
        pltpu.SemaphoreType.DMA(shape) for shape in sems
    ]


class Summer:
    def __init__(self, order, place, sizes, term, total, base, scratch):
        self.order, self.place, self.sizes = order, place, sizes
        self.term, self.total, self.base = term, total, base
        self.core_in, self.held, self.inbox = scratch[0], scratch[1:4], scratch[4:7]
        self.send_sems, self.recv_sems = scratch[7], scratch[8]
        self.spans = [PART // 2]
        for axis in order:
            self.spans.append(self.spans[-1] // sizes[axis])
        self.slot = 0
        self.sent = []
        self.wait = []

    def push(self, source, target, axis, step):
        device = along(self.place, axis, step, self.sizes)
        copy = remote(
            source, target, self.send_sems.at[self.slot], self.recv_sems.at[self.slot], device
        )
        self.slot += 1
        self.sent.append(copy)
        self.wait.append(copy)

    def arrive(self):
        for copy in self.wait:
            copy.wait_recv()
        self.wait = []

    def core_start(self):
        other = self.base + (1 - self.place["c"]) * self.spans[0]
        self.push(self.term.at[pl.ds(other, self.spans[0])], self.core_in, "c", 1)

    def core_end(self):
        self.arrive()
        mine = self.base + self.place["c"] * self.spans[0]
        add_up(self.held[0], 0, self.term, mine, [self.core_in])

    def scatter_start(self, level):
        axis, span = self.order[level], self.spans[level + 1]
        for step in range(1, self.sizes[axis]):
            peer = lax.rem(self.place[axis] + step, self.sizes[axis])
            self.push(
                self.held[level].at[pl.ds(peer * span, span)],
                self.inbox[level].at[step - 1],
                axis,
                step,
            )

    def scatter_end(self, level):
        self.arrive()
        axis, span = self.order[level], self.spans[level + 1]
        received = [self.inbox[level].at[step] for step in range(self.sizes[axis] - 1)]
        mine = self.place[axis] * span
        if level < 2:
            add_up(self.held[level + 1], 0, self.held[level], mine, received)
        else:
            add_up(self.total, self.start_of(3), self.held[level], mine, received)

    def start_of(self, levels):
        start = self.base + self.place["c"] * self.spans[0]
        for level in range(levels):
            start = start + self.place[self.order[level]] * self.spans[level + 1]
        return start

    def gather_start(self, level):
        axis = self.order[level]
        mine = self.total.at[pl.ds(self.start_of(level + 1), self.spans[level + 1])]
        for step in range(1, self.sizes[axis]):
            self.push(mine, mine, axis, step)

    def core_back(self):
        mine = self.total.at[pl.ds(self.start_of(0), self.spans[0])]
        self.push(mine, mine, "c", 1)

    def finish(self):
        for copy in self.sent:
            copy.wait_send()


def summer_scratch(order, sizes):
    spans = [PART // 2]
    for axis in order:
        spans.append(spans[-1] // sizes[axis])
    shapes = [(spans[0], 16, 128)]
    shapes += [(span, 16, 128) for span in spans[:3]]
    shapes += [(sizes[axis] - 1, span, 16, 128) for axis, span in zip(order, spans[1:])]
    copies = 2 * (1 + sum(sizes[axis] - 1 for axis in order))
    return [pltpu.VMEM(shape, BF16) for shape in shapes] + [
        pltpu.SemaphoreType.DMA((copies,)),
        pltpu.SemaphoreType.DMA((copies,)),
    ]


def pack(matrix, tiles, base):
    held = matrix.astype(BF16)
    for block in range(2):
        cut = held[:, block * 128 : block * 128 + 128]
        tiles[pl.ds(base + 20 * block, 20)] = cut.reshape(20, 16, 128)
    low, high = held[:160, 256:], held[160:, 256:]
    tail = jnp.concatenate([low, high], axis=1)
    tiles[pl.ds(base + 40, 10)] = tail.reshape(10, 16, 128)


def pack_half(matrix, tiles, base):
    held = matrix.astype(BF16)
    for block in range(2):
        cut = held[:, block * 128 : block * 128 + 128]
        tiles[pl.ds(base + 10 * block, 10)] = cut.reshape(10, 16, 128)
    tail = jnp.concatenate([held[:80, 256:], held[80:, 256:]], axis=1)
    tiles[pl.ds(base + 20, 5)] = tail.reshape(5, 16, 128)


def unpack_half(tiles, base, target, at, row, factor):
    span = pl.ds(row, HALF_CHAN)
    for block in range(2):
        cut = tiles[pl.ds(base + 10 * block, 10)].reshape(HALF_CHAN, 128)
        target[at, span, block * 128 : block * 128 + 128] = cut.astype(F32) * factor
    tail = tiles[pl.ds(base + 20, 5)].reshape(80, 128).astype(F32) * factor
    target[at, pl.ds(row, 80), 256:] = tail[:, :64]
    target[at, pl.ds(row + 80, 80), 256:] = tail[:, 64:]


def unpack(tiles, base, target, at, factor):
    for block in range(2):
        cut = tiles[pl.ds(base + 20 * block, 20)].reshape(CHAN, 128)
        target[at, :, block * 128 : block * 128 + 128] = cut.astype(F32) * factor
    tail = tiles[pl.ds(base + 40, 10)].reshape(160, 128).astype(F32) * factor
    target[at, :160, 256:] = tail[:, :64]
    target[at, 160:, 256:] = tail[:, 64:]


def finish_kernel(factor, block_in, back_in, conv_in, small_in, *refs):
    (block_out, back_out, conv_out), small_outs, gain_out = refs[:3], refs[3:7], refs[7]
    conv, small, wide, fields, through, load_sems, half_sems, store_sems = refs[8:]
    moves = []
    for at, (source, target) in enumerate(((block_in, block_out), (back_in, back_out))):
        moves.append(
            (
                pltpu.make_async_copy(source, fields.at[at], through.at[at]),
                pltpu.make_async_copy(fields.at[at], target, through.at[at + 2]),
            )
        )
        moves[-1][0].start()

    def load(at, source, target):
        span = pl.ds(at * MATRIX_TILES, MATRIX_TILES)
        return source.at[span], target.at[span]

    for at in range(4):
        pltpu.make_async_copy(*load(at, small_in, small), load_sems.at[9 + at]).start()
    def load_half(at, core):
        span = pl.ds(core * PART + at * HALF_TILES, HALF_TILES)
        return pltpu.make_async_copy(conv_in.at[span], conv.at[span], half_sems.at[at, core])

    for at in range(9):
        for core in range(2):
            load_half(at, core).start()
    gain_loads = []
    for core in range(2):
        span = pl.ds(core * PART + GAIN_TILE, 2)
        gain_loads.append(
            pltpu.make_async_copy(conv_in.at[span], conv.at[span], half_sems.at[9, core])
        )
        gain_loads[-1].start()
    for at in range(4):
        pltpu.make_async_copy(*load(at, small_in, small), load_sems.at[9 + at]).wait()
        unpack(small, at * MATRIX_TILES, wide, 9 + at, factor)
        pltpu.make_async_copy(wide.at[9 + at], small_outs[at], store_sems.at[9 + at]).start()

    def conv_tap(at, carry):
        for core in range(2):
            load_half(at, core).wait()
            start = core * PART + at * HALF_TILES
            unpack_half(conv, start, wide, at, core * HALF_CHAN, factor)
        pltpu.make_async_copy(wide.at[at], conv_out.at[at], store_sems.at[at]).start()
        return carry

    for move in moves:
        move[0].wait()
        move[1].start()
    lax.fori_loop(0, 9, conv_tap, 0)
    for copy in gain_loads:
        copy.wait()
    pieces = []
    for at in range(2):
        tiles = [conv[core * PART + GAIN_TILE + at].astype(F32) for core in range(2)]
        pieces.append((tiles[0] + tiles[1]) * factor)
    gain_out[0:128] = pieces[0][0]
    gain_out[128:256] = pieces[0][1]
    gain_out[256:] = pieces[1][0, :64]
    for move in moves:
        move[1].wait()
    for at in range(9):
        pltpu.make_async_copy(wide.at[at], conv_out.at[at], store_sems.at[at]).wait()
    for at in range(4):
        pltpu.make_async_copy(wide.at[9 + at], small_outs[at], store_sems.at[9 + at]).wait()


def shifts(cells):
    column = lax.broadcasted_iota(jnp.int32, cells.shape, 0)
    left = jnp.where(column == 0, 0.0, pltpu.roll(cells, 1, 0))
    right = jnp.where(column == COLS - 1, 0.0, pltpu.roll(cells, COLS - 1, 0))
    return [left, cells, right]


class Swap:
    def __init__(self, source, target, send_sems, recv_sems, peers, me):
        self.source, self.target, self.peers, self.me = source, target, peers, me
        self.send_sems, self.recv_sems = send_sems, recv_sems

    def start(self, half):
        for frame, device in self.peers:
            remote(
                self.source.at[half, frame],
                self.target.at[half, self.me],
                self.send_sems.at[half],
                self.recv_sems.at[half],
                device,
            )
        self.target[half, self.me] = self.source[half, self.me]

    def wait(self, half):
        span = self.target.at[half, pl.ds(0, len(self.peers))]
        pltpu.make_async_copy(span, span, self.recv_sems.at[half]).wait()

    def finish(self):
        for half in range(2):
            span = self.source.at[half, pl.ds(0, len(self.peers))]
            pltpu.make_async_copy(span, span, self.send_sems.at[half]).wait()


def norm_of(resid):
    return lax.rsqrt(jnp.mean(resid * resid, axis=-1, keepdims=True) + EPS)


def cell_start(half, at):
    if half == 0:
        return COLS + at * 64
    return jnp.where(at < 2, at * 64, HALF + at * 64)


def head_masks():
    low = lax.broadcasted_iota(jnp.int32, (1, 128), 1) < 64
    return low, [jnp.where(low, 0.125, 0.0).astype(BF16), jnp.where(low, 0.0, 0.125).astype(BF16)]


def attend(q_s, k_s, v_s, bias, probs_s, mixed_s):
    low, masks = head_masks()

    def tile(at, masks):
        start = at * 128
        span = pl.ds(start if isinstance(at, int) else pl.multiple_of(start, 128), 128)
        queries, keys, values = q_s[:, span], k_s[:, span], v_s[:, span]
        found = []
        for head, mask in enumerate(masks):
            scores = dot_nt(keys, queries * mask) + bias[...]
            expo = jnp.exp(scores)
            probs = expo * (1.0 / jnp.sum(expo, axis=0, keepdims=True))
            probs_s[2 * at + head] = probs
            found.append(dot_tn(probs.astype(BF16), values))
        total = found[0] if len(found) == 1 else jnp.where(low, *found)
        mixed_s[:, span] = total.astype(BF16)

    def pair(at, carry):
        tile(at, masks)
        return carry

    lax.fori_loop(0, 2, pair, 0)
    tile(2, masks[:1])


def attend_back(q_s, k_s, v_s, d_s, probs_s, qp_s, kp_s, vp_s):
    low, masks = head_masks()

    def tile(at, masks):
        start = at * 128
        span = pl.ds(start if isinstance(at, int) else pl.multiple_of(start, 128), 128)
        queries, keys, values, grads = q_s[:, span], k_s[:, span], v_s[:, span], d_s[:, span]
        found = []
        for head, mask in enumerate(masks):
            probs = probs_s[2 * at + head]
            prob_grad = dot_nt(values, grads * mask)
            inner = jnp.sum(probs * prob_grad, axis=0, keepdims=True)
            score_b = (probs * (prob_grad - inner)).astype(BF16)
            found.append(
                (
                    dot_tn(score_b, keys),
                    dot(score_b, queries),
                    dot(probs.astype(BF16), grads),
                )
            )
        for place, target in enumerate((qp_s, kp_s, vp_s)):
            parts = [part[place] for part in found]
            total = parts[0] if len(parts) == 1 else jnp.where(low, *parts)
            target[:, span] = total.astype(BF16)

    def pair(at, carry):
        tile(at, masks)
        return carry

    lax.fori_loop(0, 2, pair, 0)
    tile(2, masks[:1])


def block_kernel(sizes, latents, conv_w, query_w, key_w, value_w, out_w, gain, out_grad, *refs):
    (block_hbm, back_hbm, conv_hbm, small_hbm), refs = refs[:4], refs[4:]
    (
        lat_in, grad_in, lat, grad, weights, wq, wk, wv, wo, gain_v, in_sems,
        padded, wide, halo, halo_send, halo_recv, acc, resid, act_c, act_in, act_t,
        normed_out, normed_in, og_out, og_in, ng_out, ng_in, mix_out, mix_in,
        swap_send, swap_recv,
        og_n, normed_n, mixed_n, back_n,
        q_s, k_s, v_s, d_s, bias, probs_s, out_acc, mixed_s, qp_s, kp_s, vp_s, parts, flip,
        resid_grad, rg_in, conv_acc, pair_send, pair_recv, grad_pad, gain_acc, conv_terms, small_terms,
        block_out, latents_grad, conv_total, small_total, out_sems,
    ), refs = refs[:62], refs[62:]
    frames = lax.axis_size("frame")
    rows_n = lax.axis_size("row")
    chunk = HALF // frames
    me, row = lax.axis_index("frame"), lax.axis_index("row")
    place = my_place()
    peers = []
    for step in range(1, frames):
        frame = lax.rem(me + step, frames)
        peers.append((frame, (frame, row)))
    above = (me, lax.rem(row + rows_n - 1, rows_n))
    below = (me, lax.rem(row + 1, rows_n))

    barrier = pltpu.get_barrier_semaphore()
    partners = [device for _, device in peers] + [above, below]
    for axis in "cxy":
        partners += [along(place, axis, step, sizes) for step in range(1, sizes[axis])]
    for device in partners:
        pl.semaphore_signal(barrier, inc=1, device_id=device, device_id_type=MESH)

    loads = []
    pairs = (
        (latents, lat_in), (out_grad, grad_in), (conv_w, weights), (gain, gain_v),
        (out_w, wo), (query_w, wq), (key_w, wk), (value_w, wv),
    )
    for at, (source, target) in enumerate(pairs):
        loads.append(pltpu.make_async_copy(source, target, in_sems.at[at]))
        loads[-1].start()

    loads[0].wait()

    def activate(at, carry):
        span = pl.ds(at * COLS, COLS)
        cells = lat_in[at].astype(F32).T
        lat[span] = cells.astype(BF16)
        act = (cells * jax.nn.sigmoid(cells)).astype(BF16).astype(F32)
        span = pl.ds((at + 1) * COLS, COLS)
        for shift, copy in enumerate(shifts(act)):
            wide[span, shift * CHAN : shift * CHAN + CHAN] = copy.astype(BF16)
        padded[span] = act.astype(BF16)
        return carry

    lax.fori_loop(0, ROWS, activate, 0)
    loads[1].wait()

    def flip_grad(at, carry):
        cells = grad_in[at].astype(F32).T.astype(BF16)
        grad[pl.ds(at * COLS, COLS)] = cells
        half = jnp.where((at == 0) | (at == ROWS - 1), 1, 0)
        span = pl.ds(jnp.where(at >= 2, frames // 2, 0), frames // 2)
        og_out[half, span] = cells[:, :256].reshape(frames // 2, chunk, 256)
        normed_out[half, span, :, CHAN:] = cells[:, 256:].reshape(frames // 2, chunk, 64)
        return carry

    lax.fori_loop(0, ROWS, flip_grad, 0)
    pl.semaphore_wait(barrier, len(partners))

    def halo_start(source, kind):
        return [
            remote(source.at[pl.ds(COLS, COLS)], halo.at[kind, 1],
                   halo_send.at[kind, 0], halo_recv.at[kind, 0], above),
            remote(source.at[pl.ds(ROWS * COLS, COLS)], halo.at[kind, 0],
                   halo_send.at[kind, 1], halo_recv.at[kind, 1], below),
        ]

    def halo_end(copies, kind, store):
        for copy in copies:
            copy.wait_recv()
        ends = (row > 0, row < rows_n - 1)
        for side, inside in enumerate(ends):
            keep = jnp.where(inside, 1.0, 0.0).astype(F32)
            cells = halo[kind, side].astype(F32) * keep
            store(pl.ds(side * (ROWS + 1) * COLS, COLS), cells)

    def store_act(span, cells):
        for shift, copy in enumerate(shifts(cells)):
            wide[span, shift * CHAN : shift * CHAN + CHAN] = copy.astype(BF16)
        padded[span] = cells.astype(BF16)

    def store_grad(span, cells):
        for shift, copy in enumerate(shifts(cells)):
            grad_pad[shift, span] = copy.astype(BF16)

    act_halo = halo_start(padded, 0)

    swaps = []
    buffers = ((og_out, og_in), (normed_out, normed_in), (ng_out, ng_in), (mix_out, mix_in))
    for at, (source, target) in enumerate(buffers):
        swaps.append(Swap(source, target, swap_send.at[at], swap_recv.at[at], peers, me))
    og_swap, normed_swap, ng_swap, mix_swap = swaps

    loads[2].wait()
    loads[3].wait()

    def conv_half(half):
        total = None
        for a in range(3):
            if half == 0:
                cells = wide[(a + 1) * COLS : (a + 1) * COLS + HALF]
            else:
                cells = jnp.concatenate(
                    [wide[a * COLS : (a + 1) * COLS], wide[(a + 3) * COLS : (a + 4) * COLS]]
                )
            term = dot(cells, weights[3 * a : 3 * a + 3].reshape(3 * CHAN, CHAN))
            total = term if total is None else total + term
        acc[pl.ds(0, HALF)] = total
        count = 64 // chunk

        def finish(at, carry):
            cells = lat[pl.ds(pl.multiple_of(cell_start(half, at), 64), 64)].astype(F32)
            held = (cells + acc[pl.ds(at * 64, 64)]).astype(BF16)
            resid[half, pl.ds(at * 64, 64)] = held
            held = held.astype(F32)
            normed = (held * norm_of(held) * gain_v[...].reshape(1, CHAN)).astype(BF16)
            normed_out[half, pl.ds(at * count, count), :, :CHAN] = normed.reshape(count, chunk, CHAN)
            return carry

        lax.fori_loop(0, 4, finish, 0)

    og_swap.start(0)
    conv_half(0)
    normed_swap.start(0)
    halo_end(act_halo, 0, store_act)
    conv_half(1)
    normed_swap.start(1)
    og_swap.start(1)

    position = lax.broadcasted_iota(jnp.int32, (HALF, HALF), 0)
    other = lax.broadcasted_iota(jnp.int32, (HALF, HALF), 1)
    same = lax.rem(position, chunk) == lax.rem(other, chunk)
    bias[...] = jnp.where(same, 0.0, -1e30)
    for field in (q_s, k_s, v_s, d_s):
        field[:, 256:] = jnp.zeros((HALF, 128), BF16)
    act_c[...] = padded[...].astype(F32).T.astype(BF16)
    core = place["c"]
    partner = along(place, "c", 1, sizes)
    mine = pl.ds(pl.multiple_of(core * HALF_CHAN, HALF_CHAN), HALF_CHAN)
    theirs = pl.ds(pl.multiple_of((1 - core) * HALF_CHAN, HALF_CHAN), HALF_CHAN)
    pair = [remote(act_c.at[theirs], act_in, pair_send.at[0], pair_recv.at[0], partner)]

    def shift_lanes(at, carry, source, side):
        span = pl.ds(pl.multiple_of(at * COLS, COLS), COLS)
        cells = source[:, span].astype(F32)
        column = lax.broadcasted_iota(jnp.int32, cells.shape, 1)
        left = jnp.where(column == 0, 0.0, pltpu.roll(cells, 1, 1))
        right = jnp.where(column == COLS - 1, 0.0, pltpu.roll(cells, COLS - 1, 1))
        for shift, copy in enumerate((left, cells, right)):
            act_t[side, shift * HALF_CHAN : (shift + 1) * HALF_CHAN, span] = copy.astype(BF16)
        return carry

    own_rows = functools.partial(shift_lanes, source=act_c.at[mine], side=0)
    lax.fori_loop(0, ROWS + 2, own_rows, 0)
    for load in loads[4:]:
        load.wait()

    for half in range(2):
        normed_swap.wait(half)
        arrived = normed_in[half].reshape(HALF, WIDE)
        normed_n[half] = arrived[:, :CHAN]
        og_n[half, :, 256:] = arrived[:, CHAN:]
        q_s[:, :CHAN] = dot(normed_n[half], wq[...]).astype(BF16)
        k_s[:, :CHAN] = dot(normed_n[half], wk[...]).astype(BF16)
        v_s[:, :CHAN] = dot(normed_n[half], wv[...]).astype(BF16)
        attend(q_s, k_s, v_s, bias, probs_s, mixed_s)
        mixed_n[half] = mixed_s[:, :CHAN]
        mix_out[half] = mixed_s[:, :256].reshape(frames, chunk, 256)
        ng_out[half, :, :, CHAN:] = mixed_s[:, 256:CHAN].reshape(frames, chunk, 64)
        og_swap.wait(half)
        og_n[half, :, :256] = og_in[half].reshape(HALF, 256)
        d_s[:, :CHAN] = dot_nt(og_n[half], wo[...]).astype(BF16)
        attend_back(q_s, k_s, v_s, d_s, probs_s, qp_s, kp_s, vp_s)
        back = dot_nt(qp_s[:, :CHAN], wq[...])
        back = back + dot_nt(kp_s[:, :CHAN], wk[...])
        back = back + dot_nt(vp_s[:, :CHAN], wv[...])
        ng_out[half, :, :, :CHAN] = back.astype(BF16).reshape(frames, chunk, CHAN)
        ng_swap.start(half)
        for at, field in enumerate((qp_s, kp_s, vp_s)):
            parts[at, pl.ds(half * HALF, HALF)] = field[:, :CHAN]

    flip[0] = normed_n[...].reshape(2 * HALF, CHAN).astype(F32).T.astype(BF16)
    flip[1] = mixed_n[...].reshape(2 * HALF, CHAN).astype(F32).T.astype(BF16)
    for at in range(3):
        pack(dot(flip[0], parts[at]), small_terms, at * MATRIX_TILES)
    pack(dot(flip[1], og_n[...].reshape(2 * HALF, CHAN)), small_terms, 3 * MATRIX_TILES)
    spare = SMALL_TILES - 4 * MATRIX_TILES
    small_terms[pl.ds(4 * MATRIX_TILES, spare)] = jnp.zeros((spare, 16, 128), BF16)

    conv = ConvSummer(place, sizes, conv_terms, conv_total, refs[9:])
    small = Summer("yxz", place, sizes, small_terms, small_total, 0, refs[:9])
    small.core_start()

    gain_acc[...] = jnp.zeros((8, CHAN), F32)
    for half in range(2):
        ng_swap.wait(half)

        def undo_norm(at, carry, half=half):
            count = 64 // chunk
            begin = pl.multiple_of(cell_start(half, at), 64)
            held = resid[half, pl.ds(at * 64, 64)].astype(F32)
            back = ng_in[half, pl.ds(at * count, count), :, :CHAN].reshape(64, CHAN).astype(F32)
            inv = norm_of(held)
            product = back * held
            total = jnp.sum((product * inv).reshape(8, 8, CHAN), axis=0)
            gain_acc[...] += total
            tangent = back * gain_v[...].reshape(1, CHAN)
            mean = jnp.mean(product * gain_v[...].reshape(1, CHAN), axis=-1, keepdims=True)
            value = grad[pl.ds(begin, 64)].astype(F32) + (
                inv * tangent - held * (inv * inv * inv) * mean
            )
            resid_grad[half, pl.ds(at * 64, 64)] = value.astype(BF16)
            return carry

        lax.fori_loop(0, 4, undo_norm, 0)
        pair.append(
            remote(
                resid_grad.at[half],
                rg_in.at[half],
                pair_send.at[1 + half],
                pair_recv.at[1 + half],
                partner,
            )
        )
        if half == 0:
            pair[0].wait_recv()
            other_rows = functools.partial(shift_lanes, source=act_in, side=1)
            lax.fori_loop(0, ROWS + 2, other_rows, 0)

            def inner_taps(at, carry, side, cells):
                span = pl.ds(pl.multiple_of((at + 1) * COLS, COLS), HALF)
                total = dot(act_t[side, :, span], cells[0])
                if side == 0:
                    conv_acc[at] = total
                else:
                    conv_acc[at] += total
                return carry

            lax.fori_loop(
                0, 3, functools.partial(inner_taps, side=0, cells=resid_grad), 0
            )
            small.core_end()
            small.scatter_start(0)
            pair[1].wait_recv()
            lax.fori_loop(0, 3, functools.partial(inner_taps, side=1, cells=rg_in), 0)
        else:
            mix_swap.start(0)
            mix_swap.start(1)


    def pad_grad(at, carry):
        half = jnp.where((at == 0) | (at == ROWS - 1), 1, 0)
        side = jnp.where(at >= 2, 1, 0)
        cells = resid_grad[half, pl.ds(side * COLS, COLS)].astype(F32)
        for shift, copy in enumerate(shifts(cells)):
            grad_pad[shift, pl.ds((at + 1) * COLS, COLS)] = copy.astype(BF16)
        return carry

    def edge_cells(side, at):
        spans = [pl.ds(pl.multiple_of((at + gap) * COLS, COLS), COLS) for gap in (0, ROWS - 1)]
        return jnp.concatenate([act_t[side, :, span] for span in spans], axis=1)

    def second_taps(at, carry):
        conv_acc[at] += dot(edge_cells(0, at), resid_grad[1])
        return carry

    lax.fori_loop(0, 3, second_taps, 0)
    lax.fori_loop(0, ROWS, pad_grad, 0)
    grad_halo = halo_start(grad_pad.at[1], 1)

    spare = PART - 9 * HALF_TILES
    conv_terms[pl.ds(9 * HALF_TILES, spare)] = jnp.zeros((spare, 16, 128), BF16)
    gains = jnp.sum(gain_acc[...], axis=0, keepdims=True)
    line = lax.broadcasted_iota(jnp.int32, (16, 128), 0)
    gain_tile = jnp.where(line == 0, gains[:, :128], jnp.where(line == 1, gains[:, 128:256], 0.0))
    conv_terms[GAIN_TILE] = gain_tile.astype(BF16)
    tail = jnp.where(line[:, :64] == 0, gains[:, 256:], 0.0)
    conv_terms[GAIN_TILE + 1, :, :64] = tail.astype(BF16)
    pair[2].wait_recv()

    def last_taps(at, carry):
        total = conv_acc[at] + dot(edge_cells(1, at), rg_in[1])
        for b in range(3):
            part = total[b * HALF_CHAN : (b + 1) * HALF_CHAN]
            pack_half(part, conv_terms, (at * 3 + b) * HALF_TILES)
        return carry

    lax.fori_loop(0, 2, last_taps, 0)
    conv.scatter_first(0)
    lax.fori_loop(2, 3, last_taps, 0)
    conv.scatter_first(1)
    small.scatter_end(0)
    small.scatter_start(1)

    def project_out(half):
        mix_swap.wait(half)
        back_n[:, :256] = mix_in[half].reshape(HALF, 256)
        back_n[:, 256:] = ng_in[half, :, :, CHAN:].reshape(HALF, 64)
        out_acc[...] = dot(back_n[...], wo[...])

        def write_out(at, carry):
            held = resid[half, pl.ds(at * COLS, COLS)].astype(F32)
            total = held + out_acc[pl.ds(at * COLS, COLS)]
            block_out[at + 1 if half == 0 else at * 3] = total.T.astype(BF16)
            return carry

        lax.fori_loop(0, 2, write_out, 0)

    halo_end(grad_halo, 1, store_grad)
    acc[...] = jnp.zeros((2 * HALF, CHAN), F32)

    def back_tap(at, carry):
        a, b = at // 3, lax.rem(at, 3)
        cells = grad_pad[2 - b, pl.ds((2 - a) * COLS, ROWS * COLS)]
        acc[...] += dot_nt(cells, weights[at])
        return carry

    lax.fori_loop(0, 3, back_tap, 0)
    small.scatter_end(1)
    small.scatter_start(2)
    lax.fori_loop(3, 5, back_tap, 0)
    conv.scatter_second()
    small.scatter_end(2)
    small.gather_start(2)
    stores = []

    def store(source, target):
        stores.append(pltpu.make_async_copy(source, target, out_sems.at[len(stores)]))
        stores[-1].start()

    project_out(0)
    project_out(1)
    store(block_out, block_hbm)
    conv.scatter_third()
    small.arrive()
    small.gather_start(1)
    lax.fori_loop(5, 9, back_tap, 0)
    conv.gather_third()
    small.arrive()
    small.gather_start(0)
    def write_back(at, carry):
        cells = lat[pl.ds(at * COLS, COLS)].astype(F32)
        sigma = jax.nn.sigmoid(cells)
        slope = sigma * (1.0 + cells * (1.0 - sigma))
        half = jnp.where((at == 0) | (at == ROWS - 1), 1, 0)
        side = jnp.where(at >= 2, 1, 0)
        value = resid_grad[half, pl.ds(side * COLS, COLS)].astype(F32) + acc[pl.ds(at * COLS, COLS)] * slope
        latents_grad[at] = value.T.astype(BF16)
        return carry

    lax.fori_loop(0, ROWS, write_back, 0)
    store(latents_grad, back_hbm)
    def return_small():
        small.arrive()
        small.core_back()

    conv.gather_rest(return_small)
    own_half = pl.ds(place["c"] * PART, PART)
    store(conv_total.at[own_half], conv_hbm.at[own_half])
    small.arrive()
    store(small_total, small_hbm)
    conv.back_wait()
    other_half = pl.ds((1 - place["c"]) * PART, PART)
    store(conv_total.at[other_half], conv_hbm.at[other_half])
    small.finish()
    conv.finish()
    for swap in swaps:
        swap.finish()
    for copy in act_halo + grad_halo + pair:
        copy.wait_send()
    for copy in stores:
        copy.wait()


def block_scratch(sizes, frames):
    narrow, wide = (2, frames, HALF // frames, 256), (2, frames, HALF // frames, WIDE)
    vmem = pltpu.VMEM
    dma = pltpu.SemaphoreType.DMA
    weight = vmem((CHAN, CHAN), BF16)
    shapes = [
        vmem((ROWS, CHAN, COLS), BF16), vmem((ROWS, CHAN, COLS), BF16),
        vmem((ROWS * COLS, CHAN), BF16), vmem((ROWS * COLS, CHAN), BF16),
        vmem((9, CHAN, CHAN), BF16), weight, weight, weight, weight, vmem((CHAN,), F32), dma((8,)),
        vmem(((ROWS + 2) * COLS, CHAN), BF16), vmem(((ROWS + 2) * COLS, 3 * CHAN), BF16),
        vmem((2, 2, COLS, CHAN), BF16),
        dma((2, 2)), dma((2, 2)), vmem((2 * HALF, CHAN), F32), vmem((2, HALF, CHAN), BF16),
        vmem((CHAN, (ROWS + 2) * COLS), BF16), vmem((HALF_CHAN, (ROWS + 2) * COLS), BF16),
        vmem((2, 3 * HALF_CHAN, (ROWS + 2) * COLS), BF16),
    ]
    shapes += [vmem(shape, BF16) for shape in (wide, wide, narrow, narrow, wide, wide, narrow, narrow)]
    shapes += [dma((4, 2)), dma((4, 2))]
    shapes += [vmem((2, HALF, CHAN), BF16)] * 3 + [vmem((HALF, CHAN), BF16)]
    shapes += [vmem((HALF, WIDE), BF16)] * 4 + [vmem((HALF, HALF), F32)]
    shapes += [vmem((5, HALF, HALF), F32), vmem((HALF, CHAN), F32)]
    shapes += [vmem((HALF, WIDE), BF16)] * 4
    shapes += [vmem((3, 2 * HALF, CHAN), BF16), vmem((2, CHAN, 2 * HALF), BF16)]
    shapes += [vmem((2, HALF, CHAN), BF16), vmem((2, HALF, CHAN), BF16)]
    shapes += [vmem((3, 3 * HALF_CHAN, CHAN), F32), dma((3,)), dma((3,))]
    shapes += [vmem((3, (ROWS + 2) * COLS, CHAN), BF16)]
    shapes += [vmem((8, CHAN), F32)]
    shapes += [vmem((PART, 16, 128), BF16), vmem((SMALL_TILES, 16, 128), BF16)]
    shapes += [vmem((ROWS, CHAN, COLS), BF16)] * 2
    shapes += [vmem((CONV_TILES, 16, 128), BF16), vmem((SMALL_TILES, 16, 128), BF16), dma((5,))]
    return shapes + summer_scratch("yxz", sizes) + conv_summer_scratch(sizes)


def on_device(
    latents, conv_weight, query_weight, key_weight, value_weight, out_weight, norm_gain, out_grad
):
    sizes = chip_sizes()
    frames = lax.axis_size("frame")
    anywhere = pl.BlockSpec(memory_space=pl.ANY)
    inside = pl.BlockSpec(memory_space=pltpu.VMEM)
    field = jax.ShapeDtypeStruct((ROWS, CHAN, COLS), BF16)
    block_out, latents_grad, conv_sum, small_sum = pl.pallas_call(
        functools.partial(block_kernel, sizes),
        out_shape=[
            field,
            field,
            jax.ShapeDtypeStruct((CONV_TILES, 16, 128), BF16),
            jax.ShapeDtypeStruct((SMALL_TILES, 16, 128), BF16),
        ],
        in_specs=[anywhere] * 8,
        out_specs=[anywhere] * 4,
        scratch_shapes=block_scratch(sizes, frames),
        compiler_params=pltpu.CompilerParams(
            collective_id=0, has_side_effects=True, vmem_limit_bytes=56 << 20
        ),
    )(
        jnp.swapaxes(latents[0], 1, 2),
        conv_weight.reshape(9, CHAN, CHAN),
        query_weight,
        key_weight,
        value_weight,
        out_weight,
        norm_gain,
        jnp.swapaxes(out_grad[0], 1, 2),
    )
    factor = (ROWS * COLS * frames * lax.axis_size("row")) ** (-0.5)
    weight = jax.ShapeDtypeStruct((CHAN, CHAN), F32)
    outs = pl.pallas_call(
        functools.partial(finish_kernel, factor),
        out_shape=[
            field,
            field,
            jax.ShapeDtypeStruct((9, CHAN, CHAN), F32),
            weight,
            weight,
            weight,
            weight,
            jax.ShapeDtypeStruct((CHAN,), F32),
        ],
        in_specs=[anywhere] * 4,
        out_specs=[anywhere] * 7 + [inside],
        scratch_shapes=[
            pltpu.VMEM((CONV_TILES, 16, 128), BF16),
            pltpu.VMEM((SMALL_TILES, 16, 128), BF16),
            pltpu.VMEM((13, CHAN, CHAN), F32),
            pltpu.VMEM((2, ROWS, CHAN, COLS), BF16),
            pltpu.SemaphoreType.DMA((4,)),
            pltpu.SemaphoreType.DMA((13,)),
            pltpu.SemaphoreType.DMA((10, 2)),
            pltpu.SemaphoreType.DMA((13,)),
        ],
        compiler_params=pltpu.CompilerParams(vmem_limit_bytes=56 << 20),
    )(block_out, latents_grad, conv_sum, small_sum)
    return (
        jnp.swapaxes(outs[0], 1, 2)[None],
        jnp.swapaxes(outs[1], 1, 2)[None],
        outs[2].reshape(3, 3, CHAN, CHAN),
        *outs[3:7],
        outs[7],
    )


def solution(mesh):
    split = P("frame", "row", None, None)
    return jax.shard_map(
        on_device,
        mesh=mesh,
        in_specs=(split, P(), P(), P(), P(), P(), P(), split),
        out_specs=(split, split, P(), P(), P(), P(), P(), P()),
        check_vma=False,
    )
```
